32 devices in a mesh: tm: 8 (over z, y), space: 4 (over x, core).
Axes of the slice: x: 2, y: 2, z: 4, core: 2. Of those that a mesh axis runs over, the one named last changes fastest.
Arguments:
- snapshots: bfloat16 [3, 2048, 4096], P(None, 'tm', 'space'), may hold values from -6 to 6
- tile_table: int32 [8, 10, 2], P('tm'), may hold values from -1 to 7, as said below
Outputs:
- gram_tiles: float32 [8, 10, 256, 256], P('tm', None, 'space')
The draws below stay inside these ranges and needn't reach their ends.
Inputs may be any that keep to these rules, and one draw needn't show every extreme that they name: `tile_table`: every pair a <= b of block numbers below 8 stands in exactly one slot of the table, with a as row block and b as column block. In each owner's row the filled slots come first and the empty slots, -1 in both entries, last. Some owner has all 10 slots filled; owners may have no tiles.
All inputs are finite; a program needn't handle non-finite values.
Results may differ from the reference program's by a relative error of at most 0.0003.
Values may be sent and summed in bfloat16 or wider, within the bound.
No kernel may reach another device: no remote copies, remote signals or barrier semaphores. Data moves between devices by JAX's collectives and lax.ppermute only.
A program may use at most 128 MiB of HBM per device.

```python
import math
import jax
import jax.numpy as jnp
from jax import lax

COMP = 3
SNAP_DEV = 256
MAXT = 10
SNAPS = 2048
CELLS = 4096
N_TM = 8


def draw_tile_table(key, part):
    blocks_count = N_TM
    slot_count = MAXT
    upper_rows, upper_cols = jnp.triu_indices(blocks_count)
    upper_rows = upper_rows.astype(jnp.int32)
    upper_cols = upper_cols.astype(jnp.int32)
    pair_count = blocks_count * (blocks_count + 1) // 2
    key_order = jax.random.fold_in(key, 11)
    key_owner = jax.random.fold_in(key, 12)
    key_moves = jax.random.fold_in(key, 13)
    order = jax.random.permutation(key_order, pair_count).astype(jnp.int32)
    owners = jax.random.permutation(key_owner, blocks_count).astype(jnp.int32)
    remain = pair_count - slot_count
    quota = remain // (blocks_count - 1)
    extra = remain % (blocks_count - 1)
    others_count = (jnp.arange(blocks_count - 1, dtype=jnp.int32) < extra).astype(jnp.int32) + quota
    pair_moves = (blocks_count - 1) // 2
    moves = jax.random.randint(key_moves, (pair_moves,), 0, quota + 1).astype(jnp.int32)
    others_count = others_count.at[0:2 * pair_moves:2].add(-moves)
    others_count = others_count.at[1:2 * pair_moves:2].add(moves)
    counts = jnp.zeros((blocks_count,), jnp.int32)
    counts = counts.at[owners[0]].set(slot_count)
    counts = counts.at[owners[1:]].set(others_count)
    starts = jnp.cumsum(counts) - counts
    slot_index = jnp.arange(slot_count, dtype=jnp.int32)
    position = starts[:, None] + slot_index[None, :]
    valid = slot_index[None, :] < counts[:, None]
    chosen = order[jnp.clip(position, 0, pair_count - 1)]
    row_block = jnp.where(valid, upper_rows[chosen], -1)
    col_block = jnp.where(valid, upper_cols[chosen], -1)
    return jnp.stack([row_block, col_block], axis=-1).astype(jnp.int32)


def shard_levels(own_key, shape, split, least, top_value):
    level, own = 1.0, jax.random.fold_in(own_key, 6)
    for dim, blocks in split:
        steps = jnp.exp(jax.random.uniform(jax.random.fold_in(own, dim), (blocks,), jnp.float32, least / len(split), top_value / len(split)))
        level = level * jnp.repeat(steps, shape[dim] // blocks).reshape([-1 if axis == dim else 1 for axis in range(len(shape))])
    return level


def centred(key, shape, scale, bound, split=(), held_as=jnp.bfloat16):
    drawn = jax.random.normal(key, shape, jnp.float32) * scale
    if len(split) > 0:
        drawn = shard_levels(key, shape, split, -0.22, 0.18) * drawn
    return jnp.clip(drawn, min=-bound, max=bound).astype(held_as)


def setup_inputs(seed: int = 0) -> dict:
    splits = jax.random.split(jax.random.key(seed), 3)
    snapshots = centred(splits[0], (COMP, SNAPS, CELLS), 1.0, 6.0, ((1, 8), (2, 4)))
    tile_table = draw_tile_table(jax.random.fold_in(splits[2], 71), 0)
    return dict(snapshots=snapshots, tile_table=tile_table)


def reference(snapshots, tile_table):
    scale_factor = 1.0 / math.sqrt(COMP * CELLS)
    values = snapshots.astype(jnp.float32)
    flat = jnp.transpose(values, (1, 0, 2)).reshape(SNAPS, COMP * CELLS)
    gram = jnp.dot(flat, flat.T, precision=lax.Precision.HIGHEST, preferred_element_type=jnp.float32)
    gram = gram * scale_factor
    blocked = gram.reshape(N_TM, SNAP_DEV, N_TM, SNAP_DEV)
    row_block = tile_table[:, :, 0]
    col_block = tile_table[:, :, 1]
    valid = row_block >= 0
    row_safe = jnp.maximum(row_block, 0).astype(jnp.int32)
    col_safe = jnp.maximum(col_block, 0).astype(jnp.int32)
    tiles = blocked[row_safe, :, col_safe, :]
    zeros_tile = jnp.zeros_like(tiles)
    return jnp.where(valid[:, :, None, None], tiles, zeros_tile)
```

```python
import math

import jax
import jax.numpy as jnp
import numpy as np
from jax import lax
from jax.sharding import PartitionSpec as P


def per_device(snapshots, tile_table):
    components, block_size, cells_dev = snapshots.shape
    space_count = lax.axis_size("space")
    block_count = lax.axis_size("tm")
    scale_factor = 1.0 / math.sqrt(components * cells_dev * space_count)
    rows_dev = block_size // space_count
    upper_rows, upper_cols = np.triu_indices(block_count)

    mixed = lax.all_to_all(snapshots, "tm", split_axis=2, concat_axis=1, tiled=True)
    deep = lax.all_gather(mixed, "space", axis=2, tiled=True)
    blocks = deep.reshape(components, block_count, block_size, deep.shape[2])
    mine = lax.dynamic_slice_in_dim(
        blocks, lax.axis_index("space") * rows_dev, rows_dev, 2
    )
    product = jnp.einsum(
        "kaic,kbjc->abij", mine, blocks, preferred_element_type=jnp.float32
    )
    pairs = product[upper_rows, upper_cols]
    summed = lax.psum(pairs, "tm") * scale_factor

    table = tile_table[0]
    row_block = table[:, 0]
    col_block = table[:, 1]
    valid = row_block >= 0
    first = jnp.maximum(row_block, 0)
    second = jnp.maximum(col_block, 0)
    pair = first * block_count - (first * (first - 1)) // 2 + second - first
    result = summed[pair]
    result = jnp.where(valid[:, None, None], result, jnp.zeros_like(result))
    return result[None]


def solution(mesh):
    in_specs = (P(None, "tm", "space"), P("tm", None, None))
    out_specs = P("tm", None, "space", None)
    return jax.shard_map(
        per_device, mesh=mesh, in_specs=in_specs, out_specs=out_specs, check_vma=False
    )
```

```python
import functools
import math

import jax
import jax.numpy as jnp
import numpy as np
from jax import lax
from jax.experimental import pallas as pl
from jax.experimental.pallas import tpu as pltpu
from jax.sharding import Mesh, PartitionSpec as P

GROUPS = 2


def tile_plan(block_count):
    rows, cols = np.triu_indices(block_count)
    pairs = np.stack([rows, cols], axis=1)
    part = len(pairs) // 4
    lists = pairs.reshape(2, 2, part, 2)
    sizes = [len(piece) for piece in np.array_split(np.arange(part), GROUPS)]
    return lists, sizes


def multiply_kernel(group_size, chunk_count, position, pairs, *refs):
    chunks = refs[: 2 * chunk_count]
    keep_ref, send_ref, blocks, arrived = refs[2 * chunk_count :]
    z, y, x, core = position[0], position[1], position[2], position[3]
    copies = []
    for index, chunk in enumerate(chunks):
        other, step = divmod(index, chunk_count)
        block = (z ^ step) * 2 + (y ^ other)
        copy = pltpu.make_async_copy(chunk, blocks.at[block], arrived.at[index])
        copy.start()
        copies.append(copy)
    for copy in copies:
        copy.wait()
    components = blocks.shape[1]
    rows_dev = keep_ref.shape[2]

    def one_tile(slot, carry):
        first, second = pairs[2 * slot], pairs[2 * slot + 1]
        tile = jnp.zeros((blocks.shape[2], blocks.shape[2]), jnp.float32)
        for component in range(components):
            tile += lax.dot_general(
                blocks[first, component],
                blocks[second, component],
                (((1,), (1,)), ((), ())),
                preferred_element_type=jnp.float32,
            )
        parts = [tile[row : row + rows_dev] for row in range(0, tile.shape[0], rows_dev)]
        half = len(parts) // 2
        for step in range(half):
            low, high = parts[2 * step], parts[2 * step + 1]
            target = x ^ step
            keep_ref[target, slot] = jnp.where(core == 0, low, high)
            send_ref[target, slot] = jnp.where(core == 0, high, low)
        return carry

    lax.fori_loop(0, group_size, one_tile, 0)


def per_device(z_count, y_count, x_count, core_count, snapshots, tile_table):
    components, block_size, cells_dev = snapshots.shape
    block_count = z_count * y_count
    space_count = x_count * core_count
    rows_dev = block_size // space_count
    scale_factor = 1.0 / math.sqrt(components * cells_dev * space_count)
    z, y, x, core = (lax.axis_index(name) for name in ("z", "y", "x", "core"))
    position = jnp.stack([z, y, x, core]).astype(jnp.int32)
    cells = cells_dev // z_count

    def swap(value, axis, bits):
        size = lax.axis_size(axis)
        return lax.ppermute(value, axis, [(i, i ^ bits) for i in range(size)])

    def part(step):
        return lax.dynamic_slice_in_dim(snapshots, (z ^ step) * cells, cells, 2)

    own = {step: swap(part(step), "z", step) for step in range(z_count - 1, 0, -1)}
    own[0] = part(0)
    other = {step: swap(own[step], "y", 1) for step in range(z_count)}
    chunks = [own[step] for step in range(z_count)] + [other[step] for step in range(z_count)]

    lists, sizes = tile_plan(block_count)
    lists = jnp.asarray(lists, jnp.int32)
    low_bit = z & 1
    mine = lists[y, low_bit]
    theirs = lists[y, 1 - low_bit]

    finals = []
    start = 0
    for size in sizes:
        pairs = jnp.concatenate([mine[start : start + size], theirs[start : start + size]])
        start += size
        shape = jax.ShapeDtypeStruct(
            (x_count, 2 * size, rows_dev, block_size), jnp.float32
        )
        keep, send = pl.pallas_call(
            functools.partial(multiply_kernel, 2 * size, z_count),
            out_shape=(shape, shape),
            in_specs=[pl.BlockSpec(memory_space=pltpu.SMEM)] * 2
            + [pl.BlockSpec(memory_space=pl.ANY)] * len(chunks),
            out_specs=(pl.BlockSpec(memory_space=pltpu.VMEM),) * 2,
            scratch_shapes=[
                pltpu.VMEM((block_count, components, block_size, cells), jnp.bfloat16),
                pltpu.SemaphoreType.DMA((len(chunks),)),
            ],
            compiler_params=pltpu.CompilerParams(vmem_limit_bytes=40 * 2**20),
            cost_estimate=pl.CostEstimate(
                flops=4 * size * block_size * block_size * components * cells,
                bytes_accessed=4 * 2**20,
                transcendentals=0,
            ),
            name="partial_tiles",
        )(position, pairs.reshape(-1), *chunks)
        total = keep + swap(send, "core", 1)
        mine_x = total[0]
        for step in range(1, x_count):
            mine_x = mine_x + swap(total[step], "x", step)
        held = mine_x[:size] + swap(mine_x[size:], "z", 1)
        bits = 2
        while bits < z_count:
            held = held + swap(held, "z", bits)
            bits *= 2
        held = held * scale_factor
        column = jnp.stack([held, swap(held, "z", 1)])
        finals.append(jnp.stack([column, swap(column, "y", 1)]))

    whole = jnp.concatenate(finals, axis=2)
    part_count = whole.shape[2]
    flat = whole.reshape(4 * part_count, rows_dev, block_size)
    table = tile_table[0]
    row_block = table[:, 0]
    col_block = table[:, 1]
    valid = row_block >= 0
    first = jnp.maximum(row_block, 0)
    second = jnp.maximum(col_block, 0)
    pair = first * block_count - (first * (first - 1)) // 2 + second - first
    quarter, slot = pair // part_count, pair % part_count
    quarter = ((quarter // 2) ^ y) * 2 + ((quarter % 2) ^ low_bit)
    result = flat[quarter * part_count + slot]
    result = jnp.where(valid[:, None, None], result, jnp.zeros_like(result))
    return result[None]


def solution(mesh):
    tm, space = mesh.shape["tm"], mesh.shape["space"]
    sizes = (tm // 2, 2, space // 2, 2)
    grid = Mesh(mesh.devices.reshape(sizes), ("z", "y", "x", "core"))
    in_specs = (P(None, ("z", "y"), ("x", "core")), P(("z", "y"), None, None))
    out_specs = P(("z", "y"), None, ("x", "core"), None)
    return jax.shard_map(
        functools.partial(per_device, *sizes),
        mesh=grid,
        in_specs=in_specs,
        out_specs=out_specs,
        check_vma=False,
    )
```

```python
import functools
import math

import jax
import jax.numpy as jnp
import numpy as np
from jax import lax
from jax.experimental import pallas as pl
from jax.experimental.pallas import tpu as pltpu
from jax.sharding import Mesh, PartitionSpec as P

VMEM_LIMIT = 48 * 2**20


def tile_lists(block_count):
    rows, cols = np.triu_indices(block_count)
    return np.stack([rows, cols], axis=1).reshape(2, 2, -1, 2)


def multiply_tiles(scalars, first_pair, blocks, keep_ref, send_ref, x_first):
    x, core = scalars[2], scalars[3]
    group_size = keep_ref.shape[2]
    rows_dev = keep_ref.shape[3]
    part_count = blocks.shape[1] // rows_dev

    def one_slot(slot, carry):
        for low in range(2):
            where = first_pair + 2 * (low * group_size + slot)
            tile = lax.dot_general(
                blocks[scalars[where]],
                blocks[scalars[where + 1]],
                (((1,), (1,)), ((), ())),
                preferred_element_type=jnp.float32,
            )
            parts = [tile[part * rows_dev : (part + 1) * rows_dev] for part in range(part_count)]
            for step in range(part_count // 2):
                even, odd = parts[2 * step], parts[2 * step + 1]
                target = x ^ step
                place = (target, low) if x_first else (low, target)
                keep_ref[place[0], place[1], slot] = jnp.where(core == 0, even, odd)
                send_ref[place[0], place[1], slot] = jnp.where(core == 0, odd, even)
        return carry

    lax.fori_loop(0, group_size, one_slot, 0)


def first_kernel(chunk_count, first_pair, scalars, *refs):
    chunks = refs[: 2 * chunk_count]
    blocks, keep_ref, send_ref = refs[2 * chunk_count :]
    z, y = scalars[0], scalars[1]
    components, _, cells = chunks[0].shape
    for index, chunk in enumerate(chunks):
        other, step = divmod(index, chunk_count)
        block = (z ^ step) * 2 + (y ^ other)
        for component in range(components):
            blocks[block, :, component * cells : (component + 1) * cells] = chunk[component]
    multiply_tiles(scalars, first_pair, blocks, keep_ref, send_ref, True)


def second_kernel(first_pair, scalars, blocks, keep_ref, send_ref):
    multiply_tiles(scalars, first_pair, blocks, keep_ref, send_ref, False)


def per_device(z_count, y_count, x_count, core_count, snapshots, tile_table):
    components, block_size, cells_dev = snapshots.shape
    block_count = z_count * y_count
    space_count = x_count * core_count
    rows_dev = block_size // space_count
    scale_factor = 1.0 / math.sqrt(components * cells_dev * space_count)
    z, y, x, core = (lax.axis_index(name) for name in ("z", "y", "x", "core"))
    low_bit = z & 1
    cells = cells_dev // z_count

    def swap(value, axis, bits):
        size = lax.axis_size(axis)
        return lax.ppermute(value, axis, [(i, i ^ bits) for i in range(size)])

    lists = tile_lists(block_count)
    quarter = lists.shape[2]
    sizes = (quarter - quarter // 2, quarter // 2)
    ordered = np.stack(
        [
            np.concatenate(
                [
                    lists[of_y, of_bit ^ flip, cut].reshape(-1)
                    for cut in (slice(0, sizes[0]), slice(sizes[0], quarter))
                    for flip in range(2)
                ]
            )
            for of_y in range(2)
            for of_bit in range(2)
        ]
    ).astype(np.int32)
    pairs = lax.dynamic_index_in_dim(jnp.asarray(ordered), y * 2 + low_bit, 0, keepdims=False)
    scalars = jnp.concatenate([jnp.stack([z, y, x, core]).astype(jnp.int32), pairs])

    def part(step):
        return lax.dynamic_slice_in_dim(snapshots, (z ^ step) * cells, cells, 2)

    parts = [part(step) for step in range(z_count)]
    own = [parts[0]]
    for step in range(1, z_count):
        piece = parts[step]
        if step >= 3:
            piece, own[step - 2] = lax.optimization_barrier((piece, own[step - 2]))
        own.append(swap(piece, "z", step))
    chunks = own + [swap(piece, "y", 1) for piece in own]

    def sums_shape(size, x_first):
        lead = (x_count, 2) if x_first else (2, x_count)
        return jax.ShapeDtypeStruct((*lead, size, rows_dev, block_size), jnp.float32)

    def call(kernel, size, out_shape, operands, name):
        vmem = pl.BlockSpec(memory_space=pltpu.VMEM)
        return pl.pallas_call(
            kernel,
            out_shape=out_shape,
            in_specs=[pl.BlockSpec(memory_space=pltpu.SMEM)] + [vmem] * len(operands),
            out_specs=[vmem] * len(out_shape),
            compiler_params=pltpu.CompilerParams(vmem_limit_bytes=VMEM_LIMIT),
            cost_estimate=pl.CostEstimate(
                flops=4 * size * block_size * block_size * components * cells,
                bytes_accessed=4 * 2**20,
                transcendentals=0,
            ),
            name=name,
        )(scalars, *operands)

    blocks_shape = jax.ShapeDtypeStruct(
        (block_count, block_size, components * cells), jnp.bfloat16
    )
    blocks, keep_a, send_a = call(
        functools.partial(first_kernel, z_count, 4),
        sizes[0],
        [blocks_shape] + [sums_shape(sizes[0], True)] * 2,
        chunks,
        "tiles_first",
    )
    keep_b, send_b = call(
        functools.partial(second_kernel, 4 + 4 * sizes[0]),
        sizes[1],
        [sums_shape(sizes[1], False)] * 2,
        [blocks],
        "tiles_second",
    )

    def over_x(value):
        total = value[0]
        for step in range(1, x_count):
            total = total + swap(value[step], "x", step)
        return total

    def over_low_bit(value):
        return value[0] + swap(value[1], "z", 1)

    def over_high_bits(value):
        bits = 2
        while bits < z_count:
            value = value + swap(value, "z", bits)
            bits *= 2
        return value * scale_factor

    total_a = keep_a + swap(send_a, "core", 1)
    total_b = keep_b + swap(send_b, "core", 1)
    held_a = over_high_bits(over_low_bit(over_x(total_a)))
    held_b = over_high_bits(over_x(over_low_bit(total_b)))

    column_a = jnp.stack([held_a, swap(held_a, "z", 1)])
    column_b = jnp.stack([held_b, swap(held_b, "y", 1)])
    whole_a = jnp.stack([column_a, swap(column_a, "y", 1)])
    whole_b = jnp.stack([column_b, swap(column_b, "z", 1)])
    flat = jnp.concatenate(
        [part.reshape(-1, rows_dev, block_size) for part in (whole_a, whole_b)]
    )

    table = tile_table[0]
    row_block = table[:, 0]
    col_block = table[:, 1]
    valid = row_block >= 0
    first = jnp.maximum(row_block, 0)
    second = jnp.maximum(col_block, 0)
    pair = first * block_count - (first * (first - 1)) // 2 + second - first
    of_list, slot = pair // quarter, pair % quarter
    off_y, off_bit = (of_list // 2) ^ y, (of_list % 2) ^ low_bit
    place_a = (off_y * 2 + off_bit) * sizes[0] + slot
    place_b = 4 * sizes[0] + (off_bit * 2 + off_y) * sizes[1] + slot - sizes[0]
    result = flat[jnp.where(slot < sizes[0], place_a, place_b)]
    result = jnp.where(valid[:, None, None], result, jnp.zeros_like(result))
    return result[None]


def solution(mesh):
    tm, space = mesh.shape["tm"], mesh.shape["space"]
    sizes = (tm // 2, 2, space // 2, 2)
    grid = Mesh(mesh.devices.reshape(sizes), ("z", "y", "x", "core"))
    in_specs = (P(None, ("z", "y"), ("x", "core")), P(("z", "y"), None, None))
    out_specs = P(("z", "y"), None, ("x", "core"), None)
    return jax.shard_map(
        functools.partial(per_device, *sizes),
        mesh=grid,
        in_specs=in_specs,
        out_specs=out_specs,
        check_vma=False,
    )
```

```python
import functools
import math

import jax
import jax.numpy as jnp
import numpy as np
from jax import lax
from jax.experimental import pallas as pl
from jax.experimental.pallas import tpu as pltpu
from jax.sharding import Mesh, PartitionSpec as P

VMEM_LIMIT = 24 * 2**20
X_FIRST = (True, False, True, False)


def tile_lists(block_count):
    rows, cols = np.triu_indices(block_count)
    return np.stack([rows, cols], axis=1).reshape(2, 2, -1, 2)


def group_sizes(quarter):
    return [len(piece) for piece in np.array_split(np.arange(quarter), len(X_FIRST))][::-1]


def multiply_tiles(scalars, first_pair, blocks, keep_ref, send_ref, x_first):
    x, core = scalars[2], scalars[3]
    group_size = keep_ref.shape[2]
    rows_dev = keep_ref.shape[3]
    part_count = blocks.shape[1] // rows_dev

    def one_slot(slot, carry):
        for low in range(2):
            where = first_pair + 2 * (low * group_size + slot)
            tile = lax.dot_general(
                blocks[scalars[where]],
                blocks[scalars[where + 1]],
                (((1,), (1,)), ((), ())),
                preferred_element_type=jnp.float32,
            )
            parts = [tile[part * rows_dev : (part + 1) * rows_dev] for part in range(part_count)]
            for step in range(part_count // 2):
                even, odd = parts[2 * step], parts[2 * step + 1]
                target = x ^ step
                place = (target, low) if x_first else (low, target)
                keep_ref[place[0], place[1], slot] = jnp.where(core == 0, even, odd)
                send_ref[place[0], place[1], slot] = jnp.where(core == 0, odd, even)
        return carry

    lax.fori_loop(0, group_size, one_slot, 0)


def multiply_groups(scalars, first_pair, x_first, blocks, outs):
    for index, first in enumerate(x_first):
        keep_ref, send_ref = outs[2 * index : 2 * index + 2]
        multiply_tiles(scalars, first_pair, blocks, keep_ref, send_ref, first)
        first_pair += 4 * keep_ref.shape[2]


def first_kernel(layout, first_pair, x_first, scalars, *refs):
    pieces = refs[: len(layout)]
    blocks = refs[len(layout)]
    z, y = scalars[0], scalars[1]
    for (step, other, component), piece in zip(layout, pieces):
        block = (z ^ step) * 2 + (y ^ other)
        cells = piece.shape[2]
        for index in range(piece.shape[0]):
            start = (component + index) * cells
            blocks[block, :, start : start + cells] = piece[index]
    multiply_groups(scalars, first_pair, x_first, blocks, refs[len(layout) + 1 :])


def second_kernel(first_pair, x_first, scalars, blocks, *outs):
    multiply_groups(scalars, first_pair, x_first, blocks, outs)


def per_device(z_count, y_count, x_count, core_count, snapshots, tile_table):
    components, block_size, cells_dev = snapshots.shape
    block_count = z_count * y_count
    space_count = x_count * core_count
    rows_dev = block_size // space_count
    scale_factor = 1.0 / math.sqrt(components * cells_dev * space_count)
    z, y, x, core = (lax.axis_index(name) for name in ("z", "y", "x", "core"))
    low_bit = z & 1
    cells = cells_dev // z_count

    def swap(value, axis, bits):
        size = lax.axis_size(axis)
        return lax.ppermute(value, axis, [(i, i ^ bits) for i in range(size)])

    def after(value, earlier):
        return lax.optimization_barrier((value, earlier))

    lists = tile_lists(block_count)
    quarter = lists.shape[2]
    sizes = group_sizes(quarter)
    starts = np.cumsum([0] + sizes)
    ordered = np.stack(
        [
            np.concatenate(
                [
                    lists[of_y, of_bit ^ flip, start : start + size].reshape(-1)
                    for start, size in zip(starts, sizes)
                    for flip in range(2)
                ]
            )
            for of_y in range(2)
            for of_bit in range(2)
        ]
    ).astype(np.int32)
    pairs = lax.dynamic_index_in_dim(jnp.asarray(ordered), y * 2 + low_bit, 0, keepdims=False)
    scalars = jnp.concatenate([jnp.stack([z, y, x, core]).astype(jnp.int32), pairs])

    def part(step):
        return lax.dynamic_slice_in_dim(snapshots, (z ^ step) * cells, cells, 2)

    pieces = {(0, 0): part(0)}
    far = range(2, z_count)
    parts = {step: part(step) for step in far}
    for component in range(components):
        for step in far:
            piece = parts[step][component : component + 1]
            if component > 0:
                piece, pieces[step, component - 1] = after(piece, pieces[step, component - 1])
            pieces[step, component] = swap(piece, "z", step)
        if component == 0:
            pieces[1, 0] = swap(part(1), "z", 1)
    layout = [(step, 0, component) for step, component in pieces]
    layout += [(step, 1, component) for step, component in pieces]
    chunks = list(pieces.values()) + [swap(piece, "y", 1) for piece in pieces.values()]

    def sums_shape(size, x_first):
        lead = (x_count, 2) if x_first else (2, x_count)
        return jax.ShapeDtypeStruct((*lead, size, rows_dev, block_size), jnp.float32)

    def call(kernel, size, out_shape, operands, name):
        vmem = pl.BlockSpec(memory_space=pltpu.VMEM)
        return pl.pallas_call(
            kernel,
            out_shape=out_shape,
            in_specs=[pl.BlockSpec(memory_space=pltpu.SMEM)] + [vmem] * len(operands),
            out_specs=[vmem] * len(out_shape),
            compiler_params=pltpu.CompilerParams(vmem_limit_bytes=VMEM_LIMIT),
            cost_estimate=pl.CostEstimate(
                flops=4 * size * block_size * block_size * components * cells,
                bytes_accessed=4 * 2**20,
                transcendentals=0,
            ),
            name=name,
        )(scalars, *operands)

    shapes = [sums_shape(size, first) for size, first in zip(sizes, X_FIRST) for _ in range(2)]
    blocks_shape = jax.ShapeDtypeStruct(
        (block_count, block_size, components * cells), jnp.bfloat16
    )
    blocks, *sums = call(
        functools.partial(first_kernel, layout, 4, X_FIRST[:2]),
        sizes[0] + sizes[1],
        [blocks_shape] + shapes[:4],
        chunks,
        "tiles_first",
    )
    sums += call(
        functools.partial(second_kernel, 4 + 4 * (sizes[0] + sizes[1]), X_FIRST[2:]),
        sizes[2] + sizes[3],
        shapes[4:],
        [blocks],
        "tiles_second",
    )

    def over_x(value):
        total = value[0]
        for step in range(1, x_count):
            total = total + swap(value[step], "x", step)
        return total

    def over_low_bit(value):
        return value[0] + swap(value[1], "z", 1)

    def over_high_bits(value):
        bits = 2
        while bits < z_count:
            value = value + swap(value, "z", bits)
            bits *= 2
        return value * scale_factor

    flat = []
    for index, first in enumerate(X_FIRST):
        keep, send = sums[2 * index : 2 * index + 2]
        total = keep + swap(send, "core", 1)
        if first:
            held = over_high_bits(over_low_bit(over_x(total)))
            pair = jnp.stack([held, swap(held, "z", 1)])
            whole = jnp.stack([pair, swap(pair, "y", 1)])
        else:
            held = over_high_bits(over_x(over_low_bit(total)))
            pair = jnp.stack([held, swap(held, "y", 1)])
            whole = jnp.stack([pair, swap(pair, "z", 1)])
        flat.append(whole.reshape(-1, rows_dev, block_size))
    flat = jnp.concatenate(flat)

    table = tile_table[0]
    row_block = table[:, 0]
    col_block = table[:, 1]
    valid = row_block >= 0
    first = jnp.maximum(row_block, 0)
    second = jnp.maximum(col_block, 0)
    pair = first * block_count - (first * (first - 1)) // 2 + second - first
    of_list, slot = pair // quarter, pair % quarter
    off_y, off_bit = (of_list // 2) ^ y, (of_list % 2) ^ low_bit
    place = jnp.zeros_like(slot)
    for start, size, first in zip(starts, sizes, X_FIRST):
        off = off_y * 2 + off_bit if first else off_bit * 2 + off_y
        here = 4 * int(start) + off * size + slot - int(start)
        place = jnp.where((slot >= int(start)) & (slot < int(start) + size), here, place)
    result = flat[place]
    result = jnp.where(valid[:, None, None], result, jnp.zeros_like(result))
    return result[None]


def solution(mesh):
    tm, space = mesh.shape["tm"], mesh.shape["space"]
    sizes = (tm // 2, 2, space // 2, 2)
    grid = Mesh(mesh.devices.reshape(sizes), ("z", "y", "x", "core"))
    in_specs = (P(None, ("z", "y"), ("x", "core")), P(("z", "y"), None, None))
    out_specs = P(("z", "y"), None, ("x", "core"), None)
    return jax.shard_map(
        functools.partial(per_device, *sizes),
        mesh=grid,
        in_specs=in_specs,
        out_specs=out_specs,
        check_vma=False,
    )
```

```python
import functools
import math

import jax
import jax.numpy as jnp
import numpy as np
from jax import lax
from jax.experimental import pallas as pl
from jax.experimental.pallas import tpu as pltpu
from jax.sharding import Mesh, PartitionSpec as P

VMEM_LIMIT = 24 * 2**20
GROUPS = 4


def tile_lists(block_count):
    rows, cols = np.triu_indices(block_count)
    return np.stack([rows, cols], axis=1).reshape(2, 2, -1, 2)


def group_sizes(quarter):
    sizes = [len(piece) for piece in np.array_split(np.arange(quarter), GROUPS)]
    return sizes[1:-1] + sizes[:1] + sizes[-1:]


def multiply_tiles(scalars, first_pair, blocks, keep_ref, send_ref):
    x, core = scalars[2], scalars[3]
    group_size = keep_ref.shape[2]
    rows_dev = keep_ref.shape[3]
    part_count = blocks.shape[1] // rows_dev

    def one_slot(slot, carry):
        for low in range(2):
            where = first_pair + 2 * (low * group_size + slot)
            tile = lax.dot_general(
                blocks[scalars[where]],
                blocks[scalars[where + 1]],
                (((1,), (1,)), ((), ())),
                preferred_element_type=jnp.float32,
            )
            parts = [tile[part * rows_dev : (part + 1) * rows_dev] for part in range(part_count)]
            for step in range(part_count // 2):
                even, odd = parts[2 * step], parts[2 * step + 1]
                target = x ^ step
                keep_ref[target, low, slot] = jnp.where(core == 0, even, odd)
                send_ref[target, low, slot] = jnp.where(core == 0, odd, even)
        return carry

    lax.fori_loop(0, group_size, one_slot, 0)


def multiply_groups(scalars, first_pair, blocks, outs):
    for keep_ref, send_ref in zip(outs[::2], outs[1::2]):
        multiply_tiles(scalars, first_pair, blocks, keep_ref, send_ref)
        first_pair += 4 * keep_ref.shape[2]


def first_kernel(layout, first_pair, scalars, *refs):
    pieces = refs[: len(layout)]
    blocks = refs[len(layout)]
    z, y = scalars[0], scalars[1]
    for (step, other, component), piece in zip(layout, pieces):
        block = (z ^ step) * 2 + (y ^ other)
        cells = piece.shape[2]
        for index in range(piece.shape[0]):
            start = (component + index) * cells
            blocks[block, :, start : start + cells] = piece[index]
    multiply_groups(scalars, first_pair, blocks, refs[len(layout) + 1 :])


def second_kernel(first_pair, scalars, blocks, *outs):
    multiply_groups(scalars, first_pair, blocks, outs)


def per_device(z_count, y_count, x_count, core_count, snapshots, tile_table):
    components, block_size, cells_dev = snapshots.shape
    block_count = z_count * y_count
    space_count = x_count * core_count
    rows_dev = block_size // space_count
    scale_factor = 1.0 / math.sqrt(components * cells_dev * space_count)
    z, y, x, core = (lax.axis_index(name) for name in ("z", "y", "x", "core"))
    low_bit = z & 1
    cells = cells_dev // z_count

    def swap(value, axis, bits):
        size = lax.axis_size(axis)
        return lax.ppermute(value, axis, [(i, i ^ bits) for i in range(size)])

    def after(value, earlier):
        return lax.optimization_barrier((value, earlier))

    lists = tile_lists(block_count)
    quarter = lists.shape[2]
    sizes = group_sizes(quarter)
    starts = np.cumsum([0] + sizes)
    ordered = np.stack(
        [
            np.concatenate(
                [
                    lists[of_y, of_bit ^ flip, start : start + size].reshape(-1)
                    for start, size in zip(starts, sizes)
                    for flip in range(2)
                ]
            )
            for of_y in range(2)
            for of_bit in range(2)
        ]
    ).astype(np.int32)
    pairs = lax.dynamic_index_in_dim(jnp.asarray(ordered), y * 2 + low_bit, 0, keepdims=False)
    scalars = jnp.concatenate([jnp.stack([z, y, x, core]).astype(jnp.int32), pairs])

    def part(step):
        return lax.dynamic_slice_in_dim(snapshots, (z ^ step) * cells, cells, 2)

    pieces = {(0, 0): part(0)}
    for step in range(1, z_count):
        pieces[step, 0] = swap(part(step), "z", step)
    layout = [(step, 0, component) for step, component in pieces]
    layout += [(step, 1, component) for step, component in pieces]
    chunks = list(pieces.values()) + [swap(piece, "y", 1) for piece in pieces.values()]

    def sums_shape(size):
        return jax.ShapeDtypeStruct((x_count, 2, size, rows_dev, block_size), jnp.float32)

    def call(kernel, size, out_shape, operands, name):
        vmem = pl.BlockSpec(memory_space=pltpu.VMEM)
        return pl.pallas_call(
            kernel,
            out_shape=out_shape,
            in_specs=[pl.BlockSpec(memory_space=pltpu.SMEM)] + [vmem] * len(operands),
            out_specs=[vmem] * len(out_shape),
            compiler_params=pltpu.CompilerParams(vmem_limit_bytes=VMEM_LIMIT),
            cost_estimate=pl.CostEstimate(
                flops=4 * size * block_size * block_size * components * cells,
                bytes_accessed=4 * 2**20,
                transcendentals=0,
            ),
            name=name,
        )(scalars, *operands)

    shapes = [sums_shape(size) for size in sizes for _ in range(2)]
    blocks_shape = jax.ShapeDtypeStruct(
        (block_count, block_size, components * cells), jnp.bfloat16
    )
    blocks, *sums = call(
        functools.partial(first_kernel, layout, 4),
        sizes[0] + sizes[1],
        [blocks_shape] + shapes[:4],
        chunks,
        "tiles_first",
    )
    sums += call(
        functools.partial(second_kernel, 4 + 4 * (sizes[0] + sizes[1])),
        sizes[2] + sizes[3],
        shapes[4:],
        [blocks],
        "tiles_second",
    )

    flat = []
    arrived = None
    for index in range(GROUPS):
        keep, send = sums[2 * index : 2 * index + 2]
        total = keep + swap(send, "core", 1)
        held = total[0]
        for step in range(1, x_count):
            away = total[step]
            if arrived is not None:
                away, arrived = after(away, arrived)
            arrived = swap(away, "x", step)
            held = held + arrived
        held = held[0] + swap(held[1], "z", 1)
        bits = 2
        while bits < z_count:
            held = held + swap(held, "z", bits)
            bits *= 2
        held = held * scale_factor
        pair = jnp.stack([held, swap(held, "z", 1)])
        whole = jnp.stack([pair, swap(pair, "y", 1)])
        flat.append(whole.reshape(-1, rows_dev, block_size))
    flat = jnp.concatenate(flat)

    table = tile_table[0]
    row_block = table[:, 0]
    col_block = table[:, 1]
    valid = row_block >= 0
    first = jnp.maximum(row_block, 0)
    second = jnp.maximum(col_block, 0)
    pair = first * block_count - (first * (first - 1)) // 2 + second - first
    of_list, slot = pair // quarter, pair % quarter
    off_y, off_bit = (of_list // 2) ^ y, (of_list % 2) ^ low_bit
    place = jnp.zeros_like(slot)
    for start, size in zip(starts, sizes):
        off = off_y * 2 + off_bit
        here = 4 * int(start) + off * size + slot - int(start)
        place = jnp.where((slot >= int(start)) & (slot < int(start) + size), here, place)
    result = flat[place]
    result = jnp.where(valid[:, None, None], result, jnp.zeros_like(result))
    return result[None]


def solution(mesh):
    tm, space = mesh.shape["tm"], mesh.shape["space"]
    sizes = (tm // 2, 2, space // 2, 2)
    grid = Mesh(mesh.devices.reshape(sizes), ("z", "y", "x", "core"))
    in_specs = (P(None, ("z", "y"), ("x", "core")), P(("z", "y"), None, None))
    out_specs = P(("z", "y"), None, ("x", "core"), None)
    return jax.shard_map(
        functools.partial(per_device, *sizes),
        mesh=grid,
        in_specs=in_specs,
        out_specs=out_specs,
        check_vma=False,
    )
```

```python
import functools
import math

import jax
import jax.numpy as jnp
import numpy as np
from jax import lax
from jax.experimental import pallas as pl
from jax.experimental.pallas import tpu as pltpu
from jax.sharding import Mesh, PartitionSpec as P

VMEM_LIMIT = 24 * 2**20
GROUPS = 3
CODE_TOP = 32767.0


def tile_lists(block_count):
    rows, cols = np.triu_indices(block_count)
    return np.stack([rows, cols], axis=1).reshape(2, 2, -1, 2)


def group_sizes(quarter):
    return [len(piece) for piece in np.array_split(np.arange(quarter), GROUPS)]


def multiply_tiles(scalars, first_pair, blocks, keep_ref, send_ref):
    x, core = scalars[2], scalars[3]
    group_size = keep_ref.shape[2]
    rows_dev = keep_ref.shape[3]
    part_count = blocks.shape[1] // rows_dev

    def one_slot(slot, carry):
        for low in range(2):
            where = first_pair + 2 * (low * group_size + slot)
            tile = lax.dot_general(
                blocks[scalars[where]],
                blocks[scalars[where + 1]],
                (((1,), (1,)), ((), ())),
                preferred_element_type=jnp.float32,
            )
            parts = [tile[part * rows_dev : (part + 1) * rows_dev] for part in range(part_count)]
            for step in range(part_count // 2):
                even, odd = parts[2 * step], parts[2 * step + 1]
                target = x ^ step
                keep_ref[target, low, slot] = jnp.where(core == 0, even, odd)
                send_ref[target, low, slot] = jnp.where(core == 0, odd, even)
        return carry

    lax.fori_loop(0, group_size, one_slot, 0)


def multiply_groups(scalars, first_pair, blocks, outs):
    for keep_ref, send_ref in zip(outs[::2], outs[1::2]):
        multiply_tiles(scalars, first_pair, blocks, keep_ref, send_ref)
        first_pair += 4 * keep_ref.shape[2]


def first_kernel(layout, first_pair, scalars, *refs):
    pieces = refs[: len(layout)]
    blocks = refs[len(layout)]
    z, y = scalars[0], scalars[1]
    for (step, other, component), piece in zip(layout, pieces):
        block = (z ^ step) * 2 + (y ^ other)
        cells = piece.shape[2]
        for index in range(piece.shape[0]):
            start = (component + index) * cells
            blocks[block, :, start : start + cells] = piece[index]
    multiply_groups(scalars, first_pair, blocks, refs[len(layout) + 1 :])


def second_kernel(first_pair, scalars, blocks, *outs):
    multiply_groups(scalars, first_pair, blocks, outs)


def per_device(z_count, y_count, x_count, core_count, snapshots, tile_table):
    components, block_size, cells_dev = snapshots.shape
    block_count = z_count * y_count
    space_count = x_count * core_count
    rows_dev = block_size // space_count
    scale_factor = 1.0 / math.sqrt(components * cells_dev * space_count)
    z, y, x, core = (lax.axis_index(name) for name in ("z", "y", "x", "core"))
    low_bit = z & 1
    cells = cells_dev // z_count

    def swap(value, axis, bits):
        size = lax.axis_size(axis)
        return lax.ppermute(value, axis, [(i, i ^ bits) for i in range(size)])

    lists = tile_lists(block_count)
    quarter = lists.shape[2]
    sizes = group_sizes(quarter)
    starts = np.cumsum([0] + sizes)
    ordered = np.stack(
        [
            np.concatenate(
                [
                    lists[of_y, of_bit ^ flip, start : start + size].reshape(-1)
                    for start, size in zip(starts, sizes)
                    for flip in range(2)
                ]
            )
            for of_y in range(2)
            for of_bit in range(2)
        ]
    ).astype(np.int32)
    pairs = lax.dynamic_index_in_dim(jnp.asarray(ordered), y * 2 + low_bit, 0, keepdims=False)
    scalars = jnp.concatenate([jnp.stack([z, y, x, core]).astype(jnp.int32), pairs])

    def part(step):
        return lax.dynamic_slice_in_dim(snapshots, (z ^ step) * cells, cells, 2)

    pieces = {(0, 0): part(0)}
    for step in range(1, z_count):
        pieces[step, 0] = swap(part(step), "z", step)
    layout = [(step, 0, component) for step, component in pieces]
    layout += [(step, 1, component) for step, component in pieces]
    chunks = list(pieces.values()) + [swap(piece, "y", 1) for piece in pieces.values()]

    def sums_shape(size):
        return jax.ShapeDtypeStruct((x_count, 2, size, rows_dev, block_size), jnp.float32)

    def call(kernel, size, out_shape, operands, name):
        vmem = pl.BlockSpec(memory_space=pltpu.VMEM)
        return pl.pallas_call(
            kernel,
            out_shape=out_shape,
            in_specs=[pl.BlockSpec(memory_space=pltpu.SMEM)] + [vmem] * len(operands),
            out_specs=[vmem] * len(out_shape),
            compiler_params=pltpu.CompilerParams(vmem_limit_bytes=VMEM_LIMIT),
            cost_estimate=pl.CostEstimate(
                flops=4 * size * block_size * block_size * components * cells,
                bytes_accessed=4 * 2**20,
                transcendentals=0,
            ),
            name=name,
        )(scalars, *operands)

    shapes = [sums_shape(size) for size in sizes for _ in range(2)]
    blocks_shape = jax.ShapeDtypeStruct(
        (block_count, block_size, components * cells), jnp.bfloat16
    )
    blocks, *sums = call(
        functools.partial(first_kernel, layout, 4),
        sizes[0],
        [blocks_shape] + shapes[:2],
        chunks,
        "tiles_first",
    )
    sums += call(
        functools.partial(second_kernel, 4 + 4 * sizes[0]),
        sum(sizes[1:]),
        shapes[2:],
        [blocks],
        "tiles_second",
    )

    def after(value, earlier):
        return lax.optimization_barrier((value, earlier))[0]

    groups = len(sizes)
    low_arrived, y_arrived = [], []
    codes, scales = [], []
    for index, (keep, send) in enumerate(zip(sums[::2], sums[1::2])):
        total = keep + swap(send, "core", 1)
        held = total[0]
        for step in range(1, x_count):
            held = held + swap(total[step], "x", step)
        away, held = held[1], held[0]
        if index >= 2:
            away = after(away, low_arrived[index - 2])
        held = held + swap(away, "z", 1)
        if index >= 2:
            held = after(held, y_arrived[index - 2])
        bits = 2
        while bits < z_count:
            held = held + swap(held, "z", bits)
            bits *= 2
        if index == groups - 1:
            held = after(held, y_arrived[index - 1])
        top = jnp.max(jnp.abs(held), axis=2)
        factor = jnp.where(top > 0, CODE_TOP / top, 0.0)
        code = jnp.round(held * factor[:, :, None])
        code = jnp.clip(code, -CODE_TOP, CODE_TOP).astype(jnp.int16)
        low_arrived.append(swap(code, "z", 1))
        pair = jnp.stack([code, low_arrived[-1]])
        y_arrived.append(swap(pair, "y", 1))
        codes.append(jnp.stack([pair, y_arrived[-1]]).reshape(-1, rows_dev, block_size))
        scales.append(top * (scale_factor / CODE_TOP))
    codes = jnp.concatenate(codes)
    scales = after(jnp.concatenate(scales), low_arrived[-1])
    scales = jnp.stack([scales, swap(scales, "z", 1)])
    scales = jnp.stack([scales, swap(scales, "y", 1)])

    table = tile_table[0]
    row_block = table[:, 0]
    col_block = table[:, 1]
    valid = row_block >= 0
    first = jnp.maximum(row_block, 0)
    second = jnp.maximum(col_block, 0)
    pair = first * block_count - (first * (first - 1)) // 2 + second - first
    of_list, slot = pair // quarter, pair % quarter
    off = ((of_list // 2) ^ y) * 2 + ((of_list % 2) ^ low_bit)
    place = jnp.zeros_like(slot)
    for start, size in zip(starts, sizes):
        here = 4 * int(start) + off * size + slot - int(start)
        place = jnp.where((slot >= int(start)) & (slot < int(start) + size), here, place)
    scale = scales.reshape(-1, rows_dev)[off * quarter + slot]
    scale = jnp.where(valid[:, None], scale, 0.0)
    result = codes[place].astype(jnp.float32) * scale[:, :, None]
    return result[None]


def solution(mesh):
    tm, space = mesh.shape["tm"], mesh.shape["space"]
    sizes = (tm // 2, 2, space // 2, 2)
    grid = Mesh(mesh.devices.reshape(sizes), ("z", "y", "x", "core"))
    in_specs = (P(None, ("z", "y"), ("x", "core")), P(("z", "y"), None, None))
    out_specs = P(("z", "y"), None, ("x", "core"), None)
    return jax.shard_map(
        functools.partial(per_device, *sizes),
        mesh=grid,
        in_specs=in_specs,
        out_specs=out_specs,
        check_vma=False,
    )
```

```python
import functools
import math

import jax
import jax.numpy as jnp
import numpy as np
from jax import lax
from jax.experimental import pallas as pl
from jax.experimental.pallas import tpu as pltpu
from jax.sharding import Mesh, PartitionSpec as P

VMEM_LIMIT = 24 * 2**20
GROUPS = 3
ORDER = ((0, 0), (1, 0), (0, 1), (1, 1), (2, 0), (0, 2), (1, 2), (2, 1), (2, 2))
CODE_TOP = 32767.0


def tile_lists(block_count):
    rows, cols = np.triu_indices(block_count)
    return np.stack([rows, cols], axis=1).reshape(2, 2, -1, 2)


def group_sizes(quarter):
    return [len(piece) for piece in np.array_split(np.arange(quarter), GROUPS)]


def multiply_tiles(scalars, first_pair, blocks, keep_ref, send_ref):
    x, core = scalars[2], scalars[3]
    group_size = keep_ref.shape[2]
    rows_dev = keep_ref.shape[3]
    part_count = blocks.shape[1] // rows_dev

    def one_slot(slot, carry):
        for low in range(2):
            where = first_pair + 2 * (low * group_size + slot)
            tile = lax.dot_general(
                blocks[scalars[where]],
                blocks[scalars[where + 1]],
                (((1,), (1,)), ((), ())),
                preferred_element_type=jnp.float32,
            )
            parts = [tile[part * rows_dev : (part + 1) * rows_dev] for part in range(part_count)]
            for step in range(part_count // 2):
                even, odd = parts[2 * step], parts[2 * step + 1]
                target = x ^ step
                keep_ref[target, low, slot] = jnp.where(core == 0, even, odd)
                send_ref[target, low, slot] = jnp.where(core == 0, odd, even)
        return carry

    lax.fori_loop(0, group_size, one_slot, 0)


def multiply_groups(scalars, first_pair, blocks, outs):
    for keep_ref, send_ref in zip(outs[::2], outs[1::2]):
        multiply_tiles(scalars, first_pair, blocks, keep_ref, send_ref)
        first_pair += 4 * keep_ref.shape[2]


def first_kernel(layout, first_pair, scalars, *refs):
    pieces = refs[: len(layout)]
    blocks = refs[len(layout)]
    z, y = scalars[0], scalars[1]
    for (step, other, component), piece in zip(layout, pieces):
        block = (z ^ step) * 2 + (y ^ other)
        cells = piece.shape[2]
        for index in range(piece.shape[0]):
            start = (component + index) * cells
            blocks[block, :, start : start + cells] = piece[index]
    multiply_groups(scalars, first_pair, blocks, refs[len(layout) + 1 :])


def second_kernel(first_pair, scalars, blocks, *outs):
    multiply_groups(scalars, first_pair, blocks, outs)


def split_sum_kernel(left, right, *outs):
    for index, out in enumerate(outs):
        out[...] = left[index] + right[index]


def sum_kernel(left, right, out):
    out[...] = left[...] + right[...]


def code_kernel(scale_factor, left, right, code, scale):
    total = left[...] + right[...]
    top = jnp.max(jnp.abs(total), axis=2, keepdims=True)
    factor = jnp.where(top > 0, CODE_TOP / top, 0.0)
    rounded = jnp.clip(jnp.round(total * factor), -CODE_TOP, CODE_TOP)
    code[...] = rounded.astype(jnp.int32).astype(jnp.int16)
    scale[...] = jnp.max(jnp.abs(total), axis=2) * (scale_factor / CODE_TOP)


def per_device(z_count, y_count, x_count, core_count, snapshots, tile_table):
    components, block_size, cells_dev = snapshots.shape
    block_count = z_count * y_count
    space_count = x_count * core_count
    rows_dev = block_size // space_count
    scale_factor = 1.0 / math.sqrt(components * cells_dev * space_count)
    z, y, x, core = (lax.axis_index(name) for name in ("z", "y", "x", "core"))
    low_bit = z & 1
    cells = cells_dev // z_count

    def swap(value, axis, bits):
        size = lax.axis_size(axis)
        return lax.ppermute(value, axis, [(i, i ^ bits) for i in range(size)])

    lists = tile_lists(block_count)
    quarter = lists.shape[2]
    sizes = group_sizes(quarter)
    starts = np.cumsum([0] + sizes)
    ordered = np.stack(
        [
            np.concatenate(
                [
                    lists[of_y, of_bit ^ flip, start : start + size].reshape(-1)
                    for start, size in zip(starts, sizes)
                    for flip in range(2)
                ]
            )
            for of_y in range(2)
            for of_bit in range(2)
        ]
    ).astype(np.int32)
    pairs = lax.dynamic_index_in_dim(jnp.asarray(ordered), y * 2 + low_bit, 0, keepdims=False)
    scalars = jnp.concatenate([jnp.stack([z, y, x, core]).astype(jnp.int32), pairs])

    def part(step):
        return lax.dynamic_slice_in_dim(snapshots, (z ^ step) * cells, cells, 2)

    pieces = {(0, 0): part(0)}
    for step in range(1, z_count):
        pieces[step, 0] = swap(part(step), "z", step)
    layout = [(step, 0, component) for step, component in pieces]
    layout += [(step, 1, component) for step, component in pieces]
    chunks = list(pieces.values()) + [swap(piece, "y", 1) for piece in pieces.values()]

    def sums_shape(size):
        return jax.ShapeDtypeStruct((x_count, 2, size, rows_dev, block_size), jnp.float32)

    def call(kernel, size, out_shape, operands, name):
        vmem = pl.BlockSpec(memory_space=pltpu.VMEM)
        return pl.pallas_call(
            kernel,
            out_shape=out_shape,
            in_specs=[pl.BlockSpec(memory_space=pltpu.SMEM)] + [vmem] * len(operands),
            out_specs=[vmem] * len(out_shape),
            compiler_params=pltpu.CompilerParams(vmem_limit_bytes=VMEM_LIMIT),
            cost_estimate=pl.CostEstimate(
                flops=4 * size * block_size * block_size * components * cells,
                bytes_accessed=4 * 2**20,
                transcendentals=0,
            ),
            name=name,
        )(scalars, *operands)

    shapes = [sums_shape(size) for size in sizes for _ in range(2)]
    blocks_shape = jax.ShapeDtypeStruct(
        (block_count, block_size, components * cells), jnp.bfloat16
    )
    blocks, *sums = call(
        functools.partial(first_kernel, layout, 4),
        sizes[0],
        [blocks_shape] + shapes[:2],
        chunks,
        "tiles_first",
    )
    sums += call(
        functools.partial(second_kernel, 4 + 4 * sizes[0]),
        sum(sizes[1:]),
        shapes[2:],
        [blocks],
        "tiles_second",
    )

    last = []

    def step_call(kernel, out_shape, *operands, name):
        operands = lax.optimization_barrier((*operands, *last))[: len(operands)]
        vmem = pl.BlockSpec(memory_space=pltpu.VMEM)
        outs = pl.pallas_call(
            kernel,
            out_shape=out_shape,
            in_specs=[vmem] * len(operands),
            out_specs=[vmem] * len(out_shape),
            compiler_params=pltpu.CompilerParams(vmem_limit_bytes=VMEM_LIMIT),
            name=name,
        )(*operands)
        last[:] = outs[:1]
        return outs

    def float_shape(*shape):
        return jax.ShapeDtypeStruct((*shape, rows_dev, block_size), jnp.float32)

    def sum_core(index):
        keep, send = sums[2 * index], swap(sums[2 * index + 1], "core", 1)
        shapes = [float_shape(2, sizes[index])] * x_count
        mine, *away = step_call(split_sum_kernel, shapes, keep, send, name="sum_core")
        return mine, [swap(value, "x", step + 1) for step, value in enumerate(away)]

    def sum_x(index, mine, arrived):
        for value in arrived[:-1]:
            (mine,) = step_call(
                sum_kernel, [float_shape(2, sizes[index])], mine, value, name="sum_x"
            )
        shapes = [float_shape(sizes[index])] * 2
        mine, away = step_call(split_sum_kernel, shapes, mine, arrived[-1], name="sum_x")
        return mine, swap(away, "z", 1)

    def sum_low(index, mine, arrived):
        (mine,) = step_call(sum_kernel, [float_shape(sizes[index])], mine, arrived, name="sum_z")
        bits = 2
        while 2 * bits < z_count:
            (mine,) = step_call(
                sum_kernel, [float_shape(sizes[index])], mine, swap(mine, "z", bits), name="sum_z"
            )
            bits *= 2
        return mine, swap(mine, "z", bits)

    def sum_high(index, mine, arrived):
        shapes = [
            jax.ShapeDtypeStruct((sizes[index], rows_dev, block_size), jnp.int16),
            jax.ShapeDtypeStruct((sizes[index], rows_dev), jnp.float32),
        ]
        kernel = functools.partial(code_kernel, scale_factor)
        code, scale = step_call(kernel, shapes, mine, arrived, name="finish")
        return to_owners(code), scale

    def to_owners(value):
        both = [(i, i ^ (y_count + 1)) for i in range(block_count)]
        over_both = lax.ppermute(value, ("z", "y"), both)
        return [value, swap(value, "z", 1), swap(value, "y", 1), over_both]

    stages = [sum_x, sum_low, sum_high]
    state = [sum_core(index) for index in range(len(sizes))]
    for stage, index in ORDER:
        state[index] = stages[stage](index, *state[index])
    codes = jnp.concatenate([part for parts, _ in state for part in parts])
    scales = jnp.concatenate(to_owners(jnp.concatenate([scale for _, scale in state])))

    table = tile_table[0]
    row_block = table[:, 0]
    col_block = table[:, 1]
    valid = row_block >= 0
    first = jnp.maximum(row_block, 0)
    second = jnp.maximum(col_block, 0)
    pair = first * block_count - (first * (first - 1)) // 2 + second - first
    of_list, slot = pair // quarter, pair % quarter
    off = ((of_list // 2) ^ y) * 2 + ((of_list % 2) ^ low_bit)
    place = jnp.zeros_like(slot)
    for start, size in zip(starts, sizes):
        here = 4 * int(start) + off * size + slot - int(start)
        place = jnp.where((slot >= int(start)) & (slot < int(start) + size), here, place)
    scale = scales[off * quarter + slot]
    scale = jnp.where(valid[:, None], scale, 0.0)
    result = codes[place].astype(jnp.float32) * scale[:, :, None]
    return result[None]


def solution(mesh):
    tm, space = mesh.shape["tm"], mesh.shape["space"]
    sizes = (tm // 2, 2, space // 2, 2)
    grid = Mesh(mesh.devices.reshape(sizes), ("z", "y", "x", "core"))
    in_specs = (P(None, ("z", "y"), ("x", "core")), P(("z", "y"), None, None))
    out_specs = P(("z", "y"), None, ("x", "core"), None)
    return jax.shard_map(
        functools.partial(per_device, *sizes),
        mesh=grid,
        in_specs=in_specs,
        out_specs=out_specs,
        check_vma=False,
    )
```

```python
import functools
import math

import jax
import jax.numpy as jnp
import numpy as np
from jax import lax
from jax.experimental import pallas as pl
from jax.experimental.pallas import tpu as pltpu
from jax.sharding import Mesh, PartitionSpec as P

VMEM_LIMIT = 24 * 2**20
GROUPS = 3
BATCHES = ((0, 1), (2,))
ORDER = (
    ("x", 0), ("low", 0), ("x", 1), ("high", 0), ("low", 1),
    ("x", 2), ("low", 2), ("finish", BATCHES[0]), ("finish", BATCHES[1]),
)
CODE_TOP = 32767.0
SCALE_ROWS = 16
SCALE_STEPS = 8192.0


def tile_lists(block_count):
    rows, cols = np.triu_indices(block_count)
    return np.stack([rows, cols], axis=1).reshape(2, 2, -1, 2)


def group_sizes(quarter):
    return [len(piece) for piece in np.array_split(np.arange(quarter), GROUPS)]


def multiply_tiles(scalars, first_pair, blocks, keep_ref, send_ref):
    x, core = scalars[2], scalars[3]
    group_size = keep_ref.shape[2]
    rows_dev = keep_ref.shape[3]
    part_count = blocks.shape[1] // rows_dev

    def one_slot(slot, carry):
        for low in range(2):
            where = first_pair + 2 * (low * group_size + slot)
            tile = lax.dot_general(
                blocks[scalars[where]],
                blocks[scalars[where + 1]],
                (((1,), (1,)), ((), ())),
                preferred_element_type=jnp.float32,
            )
            parts = [tile[part * rows_dev : (part + 1) * rows_dev] for part in range(part_count)]
            for step in range(part_count // 2):
                even, odd = parts[2 * step], parts[2 * step + 1]
                target = x ^ step
                keep_ref[target, low, slot] = jnp.where(core == 0, even, odd)
                send_ref[target, low, slot] = jnp.where(core == 0, odd, even)
        return carry

    lax.fori_loop(0, group_size, one_slot, 0)


def multiply_groups(scalars, first_pair, blocks, outs):
    for keep_ref, send_ref in zip(outs[::2], outs[1::2]):
        multiply_tiles(scalars, first_pair, blocks, keep_ref, send_ref)
        first_pair += 4 * keep_ref.shape[2]


def first_kernel(layout, first_pair, scalars, *refs):
    pieces = refs[: len(layout)]
    blocks = refs[len(layout)]
    z, y = scalars[0], scalars[1]
    for (step, other, component), piece in zip(layout, pieces):
        block = (z ^ step) * 2 + (y ^ other)
        cells = piece.shape[2]
        for index in range(piece.shape[0]):
            start = (component + index) * cells
            blocks[block, :, start : start + cells] = piece[index]
    multiply_groups(scalars, first_pair, blocks, refs[len(layout) + 1 :])


def second_kernel(first_pair, scalars, blocks, *outs):
    multiply_groups(scalars, first_pair, blocks, outs)


def split_sum_kernel(left, right, *outs):
    for index, out in enumerate(outs):
        out[...] = left[index] + right[index]


def sum_kernel(left, right, out):
    out[...] = left[...] + right[...]


def code_kernel(sizes, pairs, *refs):
    code = refs[-1]
    refs = list(refs[:-1])
    rows, columns = refs[0].shape[1:]
    header_rows = -(-sum(sizes) * rows // columns)
    row_of = lax.broadcasted_iota(jnp.int32, (rows, columns), 0)
    lane_of = lax.broadcasted_iota(jnp.int32, (rows, columns), 1)
    place = lax.broadcasted_iota(jnp.int32, (SCALE_ROWS, columns), 0)
    header = jnp.zeros((SCALE_ROWS, columns), jnp.float32)
    slot = 0
    for size, pair in zip(sizes, pairs):
        terms = [refs.pop(0) for _ in range(pair)]
        for index in range(size):
            total = sum((term[index] for term in terms[1:]), terms[0][index])
            top = jnp.max(jnp.abs(total), axis=1, keepdims=True)
            filled = top > 0
            exponent = jnp.log(jnp.where(filled, top, 1.0)) * (1.0 / math.log(2.0))
            exponent = jnp.clip(jnp.floor(exponent), -120.0, 120.0)
            power = jnp.exp(exponent * math.log(2.0))
            steps = jnp.where(filled, jnp.ceil(top / power * SCALE_STEPS), 0.0)
            scale = steps * power * (1.0 / SCALE_STEPS)
            factor = jnp.where(filled, CODE_TOP / jnp.where(filled, scale, 1.0), 0.0)
            rounded = jnp.clip(jnp.round(total * factor), -CODE_TOP, CODE_TOP)
            start = SCALE_ROWS + slot * rows
            code[start : start + rows, :] = rounded.astype(jnp.int32).astype(jnp.int16)
            row, lane = divmod(slot * rows, columns)
            diagonal = lane_of == row_of + lane
            for at, value in ((row, exponent), (row + header_rows, steps)):
                across = jnp.sum(jnp.where(diagonal, value, 0.0), axis=0, keepdims=True)
                header += jnp.where(place == at, across, 0.0)
            slot += 1
    code[:SCALE_ROWS, :] = header.astype(jnp.int32).astype(jnp.int16)


def place_kernel(factor, scalars, *refs):
    out, codes, headers = refs[-3:]
    slots, rows, columns = out.shape
    at = 0
    for index, part in enumerate(refs[:-3]):
        count = part.shape[0] - SCALE_ROWS
        start = index * SCALE_ROWS
        headers[start : start + SCALE_ROWS, :] = (
            part[:SCALE_ROWS, :].astype(jnp.int32).astype(jnp.float32)
        )
        codes[at : at + count, :] = part[SCALE_ROWS:, :]
        at += count
    row_of = lax.broadcasted_iota(jnp.int32, (rows, columns), 0)
    lane_of = lax.broadcasted_iota(jnp.int32, (rows, columns), 1)

    def one_slot(slot, carry):
        tile, lane, exponent_row, steps_row, filled = (
            scalars[kind * slots + slot] for kind in range(5)
        )
        exponent = headers[pl.ds(exponent_row, 1), :]
        steps = headers[pl.ds(steps_row, 1), :]
        scale = steps * jnp.exp(exponent * math.log(2.0)) * factor
        scale = jnp.where(filled > 0, scale, 0.0)
        column = jnp.sum(
            jnp.where(lane_of == row_of + lane, scale, 0.0), axis=1, keepdims=True
        )
        code = codes[pl.ds(pl.multiple_of(tile * rows, rows), rows), :]
        out[slot] = code.astype(jnp.int32).astype(jnp.float32) * column
        return carry

    lax.fori_loop(0, slots, one_slot, 0)


def per_device(z_count, y_count, x_count, core_count, snapshots, tile_table):
    components, block_size, cells_dev = snapshots.shape
    block_count = z_count * y_count
    space_count = x_count * core_count
    rows_dev = block_size // space_count
    scale_factor = 1.0 / math.sqrt(components * cells_dev * space_count)
    z, y, x, core = (lax.axis_index(name) for name in ("z", "y", "x", "core"))
    low_bit = z & 1
    cells = cells_dev // z_count

    def swap(value, axis, bits):
        size = lax.axis_size(axis)
        return lax.ppermute(value, axis, [(i, i ^ bits) for i in range(size)])

    lists = tile_lists(block_count)
    quarter = lists.shape[2]
    sizes = group_sizes(quarter)
    starts = np.cumsum([0] + sizes)
    ordered = np.stack(
        [
            np.concatenate(
                [
                    lists[of_y, of_bit ^ flip, start : start + size].reshape(-1)
                    for start, size in zip(starts, sizes)
                    for flip in range(2)
                ]
            )
            for of_y in range(2)
            for of_bit in range(2)
        ]
    ).astype(np.int32)
    pairs = lax.dynamic_index_in_dim(jnp.asarray(ordered), y * 2 + low_bit, 0, keepdims=False)
    scalars = jnp.concatenate([jnp.stack([z, y, x, core]).astype(jnp.int32), pairs])

    def part(step):
        return lax.dynamic_slice_in_dim(snapshots, (z ^ step) * cells, cells, 2)

    pieces = {(0, 0): part(0)}
    for step in range(1, z_count):
        pieces[step, 0] = swap(part(step), "z", step)
    layout = [(step, 0, component) for step, component in pieces]
    layout += [(step, 1, component) for step, component in pieces]
    chunks = list(pieces.values()) + [swap(piece, "y", 1) for piece in pieces.values()]

    def sums_shape(size):
        return jax.ShapeDtypeStruct((x_count, 2, size, rows_dev, block_size), jnp.float32)

    def call(kernel, size, out_shape, operands, name):
        vmem = pl.BlockSpec(memory_space=pltpu.VMEM)
        return pl.pallas_call(
            kernel,
            out_shape=out_shape,
            in_specs=[pl.BlockSpec(memory_space=pltpu.SMEM)] + [vmem] * len(operands),
            out_specs=[vmem] * len(out_shape),
            compiler_params=pltpu.CompilerParams(vmem_limit_bytes=VMEM_LIMIT),
            cost_estimate=pl.CostEstimate(
                flops=4 * size * block_size * block_size * components * cells,
                bytes_accessed=4 * 2**20,
                transcendentals=0,
            ),
            name=name,
        )(scalars, *operands)

    shapes = [sums_shape(size) for size in sizes for _ in range(2)]
    blocks_shape = jax.ShapeDtypeStruct(
        (block_count, block_size, components * cells), jnp.bfloat16
    )
    blocks, *sums = call(
        functools.partial(first_kernel, layout, 4),
        sizes[0],
        [blocks_shape] + shapes[:2],
        chunks,
        "tiles_first",
    )
    sums += call(
        functools.partial(second_kernel, 4 + 4 * sizes[0]),
        sum(sizes[1:]),
        shapes[2:],
        [blocks],
        "tiles_second",
    )

    last = []

    def step_call(kernel, out_shape, *operands, name):
        operands = lax.optimization_barrier((*operands, *last))[: len(operands)]
        vmem = pl.BlockSpec(memory_space=pltpu.VMEM)
        outs = pl.pallas_call(
            kernel,
            out_shape=out_shape,
            in_specs=[vmem] * len(operands),
            out_specs=[vmem] * len(out_shape),
            compiler_params=pltpu.CompilerParams(vmem_limit_bytes=VMEM_LIMIT),
            cost_estimate=pl.CostEstimate(
                flops=operands[0].size, bytes_accessed=0, transcendentals=0
            ),
            name=name,
        )(*operands)
        last[:] = outs[:1]
        return outs

    def float_shape(*shape):
        return jax.ShapeDtypeStruct((*shape, rows_dev, block_size), jnp.float32)

    def sum_core(index):
        keep, send = sums[2 * index], swap(sums[2 * index + 1], "core", 1)
        shapes = [float_shape(2, sizes[index])] * x_count
        mine, *away = step_call(split_sum_kernel, shapes, keep, send, name="sum_core")
        return mine, [swap(value, "x", step + 1) for step, value in enumerate(away)]

    def sum_x(index, mine, arrived):
        for value in arrived[:-1]:
            (mine,) = step_call(
                sum_kernel, [float_shape(2, sizes[index])], mine, value, name="sum_x"
            )
        shapes = [float_shape(sizes[index])] * 2
        mine, away = step_call(split_sum_kernel, shapes, mine, arrived[-1], name="sum_x")
        return mine, swap(away, "z", 1)

    def sum_low(index, mine, arrived):
        (mine,) = step_call(sum_kernel, [float_shape(sizes[index])], mine, arrived, name="sum_z")
        bits = 2
        while 2 * bits < z_count:
            (mine,) = step_call(
                sum_kernel, [float_shape(sizes[index])], mine, swap(mine, "z", bits), name="sum_z"
            )
            bits *= 2
        return mine, swap(mine, "z", bits)

    def to_owners(value):
        both = [(i, i ^ (y_count + 1)) for i in range(block_count)]
        over_both = lax.ppermute(value, ("z", "y"), both)
        return [value, swap(value, "z", 1), swap(value, "y", 1), over_both]

    parts = []
    state = [sum_core(index) for index in range(GROUPS)]
    for stage, which in ORDER:
        if stage == "x":
            state[which] = sum_x(which, *state[which])
        elif stage == "low":
            state[which] = sum_low(which, *state[which])
        elif stage == "high":
            state[which] = step_call(
                sum_kernel, [float_shape(sizes[which])], *state[which], name="sum_high"
            )
        else:
            counts = [sizes[index] for index in which]
            shape = (SCALE_ROWS + sum(counts) * rows_dev, block_size)
            kernel = functools.partial(code_kernel, counts, [len(state[i]) for i in which])
            operands = [value for index in which for value in state[index]]
            (code,) = step_call(
                kernel, [jax.ShapeDtypeStruct(shape, jnp.int16)], *operands, name="finish"
            )
            parts += to_owners(code)

    table = tile_table[0]
    row_block = table[:, 0]
    col_block = table[:, 1]
    first = jnp.maximum(row_block, 0)
    second = jnp.maximum(col_block, 0)
    pair = first * block_count - (first * (first - 1)) // 2 + second - first
    of_list, slot = pair // quarter, pair % quarter
    off = ((of_list // 2) ^ y) * 2 + ((of_list % 2) ^ low_bit)
    tile, lane, exponent_row, steps_row = (jnp.zeros_like(slot) for _ in range(4))
    for index, batch in enumerate(BATCHES):
        start, end = int(starts[batch[0]]), int(starts[batch[-1] + 1])
        inside = (slot >= start) & (slot < end)
        header_rows = -(-(end - start) * rows_dev // block_size)
        at = (slot - start) * rows_dev
        top = (4 * index + off) * SCALE_ROWS + at // block_size
        tile = jnp.where(inside, 4 * start + off * (end - start) + slot - start, tile)
        lane = jnp.where(inside, at % block_size, lane)
        exponent_row = jnp.where(inside, top, exponent_row)
        steps_row = jnp.where(inside, top + header_rows, steps_row)
    places = jnp.concatenate(
        [tile, lane, exponent_row, steps_row, (row_block >= 0).astype(jnp.int32)]
    )
    vmem = pl.BlockSpec(memory_space=pltpu.VMEM)
    result = pl.pallas_call(
        functools.partial(place_kernel, scale_factor / (CODE_TOP * SCALE_STEPS)),
        out_shape=float_shape(table.shape[0]),
        in_specs=[pl.BlockSpec(memory_space=pltpu.SMEM)] + [vmem] * len(parts),
        out_specs=vmem,
        scratch_shapes=[
            pltpu.VMEM((4 * quarter * rows_dev, block_size), jnp.int16),
            pltpu.VMEM((len(parts) * SCALE_ROWS, block_size), jnp.float32),
        ],
        compiler_params=pltpu.CompilerParams(vmem_limit_bytes=VMEM_LIMIT),
        cost_estimate=pl.CostEstimate(
            flops=table.shape[0] * rows_dev * block_size, bytes_accessed=0, transcendentals=0
        ),
        name="place_tiles",
    )(places, *parts)
    return result[None]


def solution(mesh):
    tm, space = mesh.shape["tm"], mesh.shape["space"]
    sizes = (tm // 2, 2, space // 2, 2)
    grid = Mesh(mesh.devices.reshape(sizes), ("z", "y", "x", "core"))
    in_specs = (P(None, ("z", "y"), ("x", "core")), P(("z", "y"), None, None))
    out_specs = P(("z", "y"), None, ("x", "core"), None)
    return jax.shard_map(
        functools.partial(per_device, *sizes),
        mesh=grid,
        in_specs=in_specs,
        out_specs=out_specs,
        check_vma=False,
    )
```

```python
import functools
import math

import jax
import jax.numpy as jnp
import numpy as np
from jax import lax
from jax.experimental import pallas as pl
from jax.experimental.pallas import tpu as pltpu
from jax.sharding import Mesh, PartitionSpec as P

VMEM_LIMIT = 24 * 2**20
GROUPS = 3
BATCHES = ((0, 1), (2,))
ORDER = (
    ("tiles", None), ("core", 0), ("core", 1), ("core", 2),
    ("x", 0), ("low", 0), ("x", 1), ("high", 0), ("low", 1), ("x", 2), ("high", 1), ("low", 2),
    ("finish", BATCHES[0]), ("relay", None), ("finish", BATCHES[1]),
)
CODE_TOP = 32767.0
SCALE_ROWS = 16
SCALE_STEPS = 8192.0


def tile_lists(block_count):
    rows, cols = np.triu_indices(block_count)
    return np.stack([rows, cols], axis=1).reshape(2, 2, -1, 2)


def group_sizes(quarter):
    return [len(piece) for piece in np.array_split(np.arange(quarter), GROUPS)]


def multiply_tiles(scalars, first_pair, blocks, keep_ref, send_ref):
    x, core = scalars[2], scalars[3]
    group_size = keep_ref.shape[2]
    rows_dev = keep_ref.shape[3]
    part_count = blocks.shape[1] // rows_dev

    def one_slot(slot, carry):
        for low in range(2):
            where = first_pair + 2 * (low * group_size + slot)
            tile = lax.dot_general(
                blocks[scalars[where]],
                blocks[scalars[where + 1]],
                (((1,), (1,)), ((), ())),
                preferred_element_type=jnp.float32,
            )
            parts = [tile[part * rows_dev : (part + 1) * rows_dev] for part in range(part_count)]
            for step in range(part_count // 2):
                even, odd = parts[2 * step], parts[2 * step + 1]
                target = x ^ step
                keep_ref[target, low, slot] = jnp.where(core == 0, even, odd)
                send_ref[target, low, slot] = jnp.where(core == 0, odd, even)
        return carry

    lax.fori_loop(0, group_size, one_slot, 0)


def multiply_groups(scalars, first_pair, blocks, outs):
    for keep_ref, send_ref in zip(outs[::2], outs[1::2]):
        multiply_tiles(scalars, first_pair, blocks, keep_ref, send_ref)
        first_pair += 4 * keep_ref.shape[2]


def first_kernel(layout, first_pair, scalars, *refs):
    pieces = refs[: len(layout)]
    blocks = refs[len(layout)]
    z, y = scalars[0], scalars[1]
    for (step, other, component), piece in zip(layout, pieces):
        block = (z ^ step) * 2 + (y ^ other)
        cells = piece.shape[2]
        for index in range(piece.shape[0]):
            start = (component + index) * cells
            blocks[block, :, start : start + cells] = piece[index]
    multiply_groups(scalars, first_pair, blocks, refs[len(layout) + 1 :])


def second_kernel(first_pair, scalars, blocks, *outs):
    multiply_groups(scalars, first_pair, blocks, outs)


def split_sum_kernel(left, right, *outs):
    for index, out in enumerate(outs):
        out[...] = left[index] + right[index]


def sum_kernel(left, right, out):
    out[...] = left[...] + right[...]


def code_kernel(sizes, pairs, *refs):
    code = refs[-1]
    refs = list(refs[:-1])
    rows, columns = refs[0].shape[1:]
    header_rows = -(-sum(sizes) * rows // columns)
    row_of = lax.broadcasted_iota(jnp.int32, (rows, columns), 0)
    lane_of = lax.broadcasted_iota(jnp.int32, (rows, columns), 1)
    place = lax.broadcasted_iota(jnp.int32, (SCALE_ROWS, columns), 0)
    header = jnp.zeros((SCALE_ROWS, columns), jnp.float32)
    slot = 0
    for size, pair in zip(sizes, pairs):
        terms = [refs.pop(0) for _ in range(pair)]
        for index in range(size):
            total = sum((term[index] for term in terms[1:]), terms[0][index])
            top = jnp.max(jnp.abs(total), axis=1, keepdims=True)
            filled = top > 0
            exponent = jnp.log(jnp.where(filled, top, 1.0)) * (1.0 / math.log(2.0))
            exponent = jnp.clip(jnp.floor(exponent), -120.0, 120.0)
            power = jnp.exp(exponent * math.log(2.0))
            steps = jnp.where(filled, jnp.ceil(top / power * SCALE_STEPS), 0.0)
            scale = steps * power * (1.0 / SCALE_STEPS)
            factor = jnp.where(filled, CODE_TOP / jnp.where(filled, scale, 1.0), 0.0)
            rounded = jnp.clip(jnp.round(total * factor), -CODE_TOP, CODE_TOP)
            start = SCALE_ROWS + slot * rows
            code[start : start + rows, :] = rounded.astype(jnp.int32).astype(jnp.int16)
            row, lane = divmod(slot * rows, columns)
            diagonal = lane_of == row_of + lane
            for at, value in ((row, exponent), (row + header_rows, steps)):
                across = jnp.sum(jnp.where(diagonal, value, 0.0), axis=0, keepdims=True)
                header += jnp.where(place == at, across, 0.0)
            slot += 1
    code[:SCALE_ROWS, :] = header.astype(jnp.int32).astype(jnp.int16)


def pair_kernel(own, arrived, out):
    out[0] = own[...]
    out[1] = arrived[...]


def place_kernel(factor, scalars, *refs):
    out, codes, headers = refs[-3:]
    slots, rows, columns = out.shape
    at = 0
    parts = [part.at[index] for part in refs[:-3] for index in range(part.shape[0])]
    for index, part in enumerate(parts):
        count = part.shape[0] - SCALE_ROWS
        start = index * SCALE_ROWS
        headers[start : start + SCALE_ROWS, :] = (
            part[:SCALE_ROWS, :].astype(jnp.int32).astype(jnp.float32)
        )
        codes[at : at + count, :] = part[SCALE_ROWS:, :]
        at += count
    row_of = lax.broadcasted_iota(jnp.int32, (rows, columns), 0)
    lane_of = lax.broadcasted_iota(jnp.int32, (rows, columns), 1)

    def one_slot(slot, carry):
        tile, lane, exponent_row, steps_row, filled = (
            scalars[kind * slots + slot] for kind in range(5)
        )
        exponent = headers[pl.ds(exponent_row, 1), :]
        steps = headers[pl.ds(steps_row, 1), :]
        scale = steps * jnp.exp(exponent * math.log(2.0)) * factor
        scale = jnp.where(filled > 0, scale, 0.0)
        column = jnp.sum(
            jnp.where(lane_of == row_of + lane, scale, 0.0), axis=1, keepdims=True
        )
        code = codes[pl.ds(pl.multiple_of(tile * rows, rows), rows), :]
        out[slot] = code.astype(jnp.int32).astype(jnp.float32) * column
        return carry

    lax.fori_loop(0, slots, one_slot, 0)


def per_device(z_count, y_count, x_count, core_count, snapshots, tile_table):
    components, block_size, cells_dev = snapshots.shape
    block_count = z_count * y_count
    space_count = x_count * core_count
    rows_dev = block_size // space_count
    scale_factor = 1.0 / math.sqrt(components * cells_dev * space_count)
    z, y, x, core = (lax.axis_index(name) for name in ("z", "y", "x", "core"))
    low_bit = z & 1
    cells = cells_dev // z_count

    def swap(value, axis, bits):
        size = lax.axis_size(axis)
        return lax.ppermute(value, axis, [(i, i ^ bits) for i in range(size)])

    lists = tile_lists(block_count)
    quarter = lists.shape[2]
    sizes = group_sizes(quarter)
    starts = np.cumsum([0] + sizes)
    ordered = np.stack(
        [
            np.concatenate(
                [
                    lists[of_y, of_bit ^ flip, start : start + size].reshape(-1)
                    for start, size in zip(starts, sizes)
                    for flip in range(2)
                ]
            )
            for of_y in range(2)
            for of_bit in range(2)
        ]
    ).astype(np.int32)
    pairs = lax.dynamic_index_in_dim(jnp.asarray(ordered), y * 2 + low_bit, 0, keepdims=False)
    scalars = jnp.concatenate([jnp.stack([z, y, x, core]).astype(jnp.int32), pairs])

    def part(step):
        return lax.dynamic_slice_in_dim(snapshots, (z ^ step) * cells, cells, 2)

    pieces = {(0, 0): part(0)}
    for step in range(1, z_count):
        pieces[step, 0] = swap(part(step), "z", step)
    layout = [(step, 0, component) for step, component in pieces]
    layout += [(step, 1, component) for step, component in pieces]
    chunks = list(pieces.values()) + [swap(piece, "y", 1) for piece in pieces.values()]

    def sums_shape(size):
        return jax.ShapeDtypeStruct((x_count, 2, size, rows_dev, block_size), jnp.float32)

    def call(kernel, size, out_shape, operands, name):
        vmem = pl.BlockSpec(memory_space=pltpu.VMEM)
        return pl.pallas_call(
            kernel,
            out_shape=out_shape,
            in_specs=[pl.BlockSpec(memory_space=pltpu.SMEM)] + [vmem] * len(operands),
            out_specs=[vmem] * len(out_shape),
            compiler_params=pltpu.CompilerParams(vmem_limit_bytes=VMEM_LIMIT),
            cost_estimate=pl.CostEstimate(
                flops=4 * size * block_size * block_size * components * cells,
                bytes_accessed=0,
                transcendentals=0,
            ),
            name=name,
        )(scalars, *operands)

    shapes = [sums_shape(size) for size in sizes for _ in range(2)]
    blocks_shape = jax.ShapeDtypeStruct(
        (block_count, block_size, components * cells), jnp.bfloat16
    )
    blocks, *sums = call(
        functools.partial(first_kernel, layout, 4),
        sizes[0],
        [blocks_shape] + shapes[:2],
        chunks,
        "tiles_first",
    )
    last = []

    def step_call(kernel, out_shape, *operands, name):
        operands = lax.optimization_barrier((*operands, *last))[: len(operands)]
        vmem = pl.BlockSpec(memory_space=pltpu.VMEM)
        outs = pl.pallas_call(
            kernel,
            out_shape=out_shape,
            in_specs=[vmem] * len(operands),
            out_specs=[vmem] * len(out_shape),
            compiler_params=pltpu.CompilerParams(vmem_limit_bytes=VMEM_LIMIT),
            cost_estimate=pl.CostEstimate(
                flops=operands[0].size, bytes_accessed=0, transcendentals=0
            ),
            name=name,
        )(*operands)
        last[:] = outs[:1]
        return outs

    def float_shape(*shape):
        return jax.ShapeDtypeStruct((*shape, rows_dev, block_size), jnp.float32)

    def sum_core(index):
        keep, send = sums[2 * index : 2 * index + 2]
        send = swap(send, "core", 1)
        shapes = [float_shape(2, sizes[index])] * x_count
        mine, *away = step_call(split_sum_kernel, shapes, keep, send, name="sum_core")
        return mine, [swap(value, "x", step + 1) for step, value in enumerate(away)]

    def sum_x(index, mine, arrived):
        for value in arrived[:-1]:
            (mine,) = step_call(
                sum_kernel, [float_shape(2, sizes[index])], mine, value, name="sum_x"
            )
        shapes = [float_shape(sizes[index])] * 2
        mine, away = step_call(split_sum_kernel, shapes, mine, arrived[-1], name="sum_x")
        return mine, swap(away, "z", 1)

    def sum_low(index, mine, arrived):
        (mine,) = step_call(sum_kernel, [float_shape(sizes[index])], mine, arrived, name="sum_z")
        bits = 2
        while 2 * bits < z_count:
            (mine,) = step_call(
                sum_kernel, [float_shape(sizes[index])], mine, swap(mine, "z", bits), name="sum_z"
            )
            bits *= 2
        return mine, swap(mine, "z", bits)

    parts = []
    state = {}
    for stage, which in ORDER:
        if stage == "core":
            state[which] = sum_core(which)
        elif stage == "tiles":
            sums += call(
                functools.partial(second_kernel, 4 + 4 * sizes[0]),
                sum(sizes[1:]),
                shapes[2:],
                [blocks],
                "tiles_second",
            )
        elif stage == "x":
            state[which] = sum_x(which, *state[which])
        elif stage == "low":
            state[which] = sum_low(which, *state[which])
        elif stage == "high":
            state[which] = step_call(
                sum_kernel, [float_shape(sizes[which])], *state[which], name="sum_high"
            )
        elif stage == "finish":
            counts = [sizes[index] for index in which]
            shape = (SCALE_ROWS + sum(counts) * rows_dev, block_size)
            kernel = functools.partial(code_kernel, counts, [len(state[i]) for i in which])
            operands = [value for index in which for value in state[index]]
            (code,) = step_call(
                kernel, [jax.ShapeDtypeStruct(shape, jnp.int16)], *operands, name="finish"
            )
            over_z = swap(code, "z", 1)
            if which == BATCHES[-1]:
                both = [(i, i ^ (y_count + 1)) for i in range(block_count)]
                over_both = lax.ppermute(code, ("z", "y"), both)
                parts += [part[None] for part in (code, over_z, swap(code, "y", 1), over_both)]
        else:
            shape = jax.ShapeDtypeStruct((2, *code.shape), code.dtype)
            (pair,) = step_call(pair_kernel, [shape], code, over_z, name="pair")
            parts += [pair, swap(pair, "y", 1)]

    table = tile_table[0]
    row_block = table[:, 0]
    col_block = table[:, 1]
    first = jnp.maximum(row_block, 0)
    second = jnp.maximum(col_block, 0)
    pair = first * block_count - (first * (first - 1)) // 2 + second - first
    of_list, slot = pair // quarter, pair % quarter
    off = ((of_list // 2) ^ y) * 2 + ((of_list % 2) ^ low_bit)
    tile, lane, exponent_row, steps_row = (jnp.zeros_like(slot) for _ in range(4))
    for index, batch in enumerate(BATCHES):
        start, end = int(starts[batch[0]]), int(starts[batch[-1] + 1])
        inside = (slot >= start) & (slot < end)
        header_rows = -(-(end - start) * rows_dev // block_size)
        at = (slot - start) * rows_dev
        top = (4 * index + off) * SCALE_ROWS + at // block_size
        tile = jnp.where(inside, 4 * start + off * (end - start) + slot - start, tile)
        lane = jnp.where(inside, at % block_size, lane)
        exponent_row = jnp.where(inside, top, exponent_row)
        steps_row = jnp.where(inside, top + header_rows, steps_row)
    places = jnp.concatenate(
        [tile, lane, exponent_row, steps_row, (row_block >= 0).astype(jnp.int32)]
    )
    vmem = pl.BlockSpec(memory_space=pltpu.VMEM)
    result = pl.pallas_call(
        functools.partial(place_kernel, scale_factor / (CODE_TOP * SCALE_STEPS)),
        out_shape=float_shape(table.shape[0]),
        in_specs=[pl.BlockSpec(memory_space=pltpu.SMEM)] + [vmem] * len(parts),
        out_specs=vmem,
        scratch_shapes=[
            pltpu.VMEM((4 * quarter * rows_dev, block_size), jnp.int16),
            pltpu.VMEM((4 * len(BATCHES) * SCALE_ROWS, block_size), jnp.float32),
        ],
        compiler_params=pltpu.CompilerParams(vmem_limit_bytes=VMEM_LIMIT),
        cost_estimate=pl.CostEstimate(
            flops=table.shape[0] * rows_dev * block_size, bytes_accessed=0, transcendentals=0
        ),
        name="place_tiles",
    )(places, *parts)
    return result[None]


def solution(mesh):
    tm, space = mesh.shape["tm"], mesh.shape["space"]
    sizes = (tm // 2, 2, space // 2, 2)
    grid = Mesh(mesh.devices.reshape(sizes), ("z", "y", "x", "core"))
    in_specs = (P(None, ("z", "y"), ("x", "core")), P(("z", "y"), None, None))
    out_specs = P(("z", "y"), None, ("x", "core"), None)
    return jax.shard_map(
        functools.partial(per_device, *sizes),
        mesh=grid,
        in_specs=in_specs,
        out_specs=out_specs,
        check_vma=False,
    )
```

```python
import functools
import math

import jax
import jax.numpy as jnp
import numpy as np
from jax import lax
from jax.experimental import pallas as pl
from jax.experimental.pallas import tpu as pltpu
from jax.sharding import Mesh, PartitionSpec as P

Z = ("z_high", "z_low")
VMEM_LIMIT = 24 * 2**20
GROUPS = 3
BATCHES = ((0,), (1,), (2,))
ORDER = (
    ("x", 0), ("low", 0), ("x", 1), ("finish", BATCHES[0]), ("low", 1),
    ("x", 2), ("high", 1), ("low", 2),
    ("finish", BATCHES[1]), ("finish", BATCHES[2]),
)
CODE_TOP = 32767.0
SCALE_ROWS = 8
SCALE_STEPS = 8192.0


def tile_lists(block_count):
    rows, cols = np.triu_indices(block_count)
    return np.stack([rows, cols], axis=1).reshape(2, 2, -1, 2)


def group_sizes(quarter):
    return [len(piece) for piece in np.array_split(np.arange(quarter), GROUPS)]


def multiply_tiles(scalars, first_pair, blocks, keep_ref, send_ref):
    x, core = scalars[2], scalars[3]
    group_size = keep_ref.shape[2]
    rows_dev = keep_ref.shape[3]
    part_count = blocks.shape[1] // rows_dev

    def one_slot(slot, carry):
        for low in range(2):
            where = first_pair + 2 * (low * group_size + slot)
            tile = lax.dot_general(
                blocks[scalars[where]],
                blocks[scalars[where + 1]],
                (((1,), (1,)), ((), ())),
                preferred_element_type=jnp.float32,
            )
            parts = [tile[part * rows_dev : (part + 1) * rows_dev] for part in range(part_count)]
            for step in range(part_count // 2):
                even, odd = parts[2 * step], parts[2 * step + 1]
                target = x ^ step
                keep_ref[target, low, slot] = jnp.where(core == 0, even, odd)
                send_ref[target, low, slot] = jnp.where(core == 0, odd, even)
        return carry

    lax.fori_loop(0, group_size, one_slot, 0)


def multiply_groups(scalars, first_pair, blocks, outs):
    for keep_ref, send_ref in zip(outs[::2], outs[1::2]):
        multiply_tiles(scalars, first_pair, blocks, keep_ref, send_ref)
        first_pair += 4 * keep_ref.shape[2]


def first_kernel(layout, first_pair, scalars, *refs):
    pieces = refs[: len(layout)]
    blocks = refs[len(layout)]
    z, y = scalars[0], scalars[1]
    for (step, other, component), piece in zip(layout, pieces):
        block = (z ^ step) * 2 + (y ^ other)
        cells = piece.shape[2]
        for index in range(piece.shape[0]):
            start = (component + index) * cells
            blocks[block, :, start : start + cells] = piece[index]
    multiply_groups(scalars, first_pair, blocks, refs[len(layout) + 1 :])


def second_kernel(first_pair, scalars, blocks, *outs):
    multiply_groups(scalars, first_pair, blocks, outs)


def split_sum_kernel(left, right, *outs):
    for index, out in enumerate(outs):
        out[...] = left[index] + right[index]


def sum_kernel(left, right, out):
    out[...] = left[...] + right[...]


def code_kernel(sizes, pairs, *refs):
    code = refs[-1]
    refs = list(refs[:-1])
    rows, columns = refs[0].shape[1:]
    header_rows = -(-sum(sizes) * rows // columns)
    row_of = lax.broadcasted_iota(jnp.int32, (rows, columns), 0)
    lane_of = lax.broadcasted_iota(jnp.int32, (rows, columns), 1)
    place = lax.broadcasted_iota(jnp.int32, (SCALE_ROWS, columns), 0)
    header = jnp.zeros((SCALE_ROWS, columns), jnp.float32)
    slot = 0
    for size, pair in zip(sizes, pairs):
        terms = [refs.pop(0) for _ in range(pair)]
        for index in range(size):
            total = sum((term[index] for term in terms[1:]), terms[0][index])
            top = jnp.max(jnp.abs(total), axis=1, keepdims=True)
            filled = top > 0
            exponent = jnp.log(jnp.where(filled, top, 1.0)) * (1.0 / math.log(2.0))
            exponent = jnp.clip(jnp.floor(exponent), -120.0, 120.0)
            power = jnp.exp(exponent * math.log(2.0))
            steps = jnp.where(filled, jnp.ceil(top / power * SCALE_STEPS), 0.0)
            scale = steps * power * (1.0 / SCALE_STEPS)
            factor = jnp.where(filled, CODE_TOP / jnp.where(filled, scale, 1.0), 0.0)
            rounded = jnp.clip(jnp.round(total * factor), -CODE_TOP, CODE_TOP)
            rounded = rounded.astype(jnp.int32)
            start, half = SCALE_ROWS + slot * (rows // 2), rows // 2
            code[start : start + half, :] = (rounded[:half] << 16) | (rounded[half:] & 0xFFFF)
            row, lane = divmod(slot * rows, columns)
            diagonal = lane_of == row_of + lane
            for at, value in ((row, exponent), (row + header_rows, steps)):
                across = jnp.sum(jnp.where(diagonal, value, 0.0), axis=0, keepdims=True)
                header += jnp.where(place == at, across, 0.0)
            slot += 1
    code[:SCALE_ROWS, :] = header.astype(jnp.int32)


def place_kernel(factor, scalars, *refs):
    out, codes, headers = refs[-3:]
    slots, rows, columns = out.shape
    at = 0
    parts = [part.at[index] for part in refs[:-3] for index in range(part.shape[0])]
    for index, part in enumerate(parts):
        count = part.shape[0] - SCALE_ROWS
        start = index * SCALE_ROWS
        headers[start : start + SCALE_ROWS, :] = part[:SCALE_ROWS, :].astype(jnp.float32)
        codes[at : at + count, :] = part[SCALE_ROWS:, :]
        at += count
    row_of = lax.broadcasted_iota(jnp.int32, (rows, columns), 0)
    lane_of = lax.broadcasted_iota(jnp.int32, (rows, columns), 1)

    def one_slot(slot, carry):
        tile, lane, exponent_row, steps_row, filled = (
            scalars[kind * slots + slot] for kind in range(5)
        )
        exponent = headers[pl.ds(exponent_row, 1), :]
        steps = headers[pl.ds(steps_row, 1), :]
        scale = steps * jnp.exp(exponent * math.log(2.0)) * factor
        scale = jnp.where(filled > 0, scale, 0.0)
        column = jnp.sum(
            jnp.where(lane_of == row_of + lane, scale, 0.0), axis=1, keepdims=True
        )
        half = rows // 2
        code = codes[pl.ds(pl.multiple_of(tile * half, half), half), :]
        out[slot, :half] = (code >> 16).astype(jnp.float32) * column[:half]
        out[slot, half:] = ((code << 16) >> 16).astype(jnp.float32) * column[half:]
        return carry

    lax.fori_loop(0, slots, one_slot, 0)


def per_device(z_count, y_count, x_count, core_count, snapshots, tile_table):
    components, block_size, cells_dev = snapshots.shape
    block_count = z_count * y_count
    space_count = x_count * core_count
    rows_dev = block_size // space_count
    scale_factor = 1.0 / math.sqrt(components * cells_dev * space_count)
    low_bit, y, x, core = (lax.axis_index(name) for name in ("z_low", "y", "x", "core"))
    z = lax.axis_index(Z)
    cells = cells_dev // z_count

    def swap(value, axis, bits):
        size = lax.axis_size(axis)
        return lax.ppermute(value, axis, [(i, i ^ bits) for i in range(size)])

    lists = tile_lists(block_count)
    quarter = lists.shape[2]
    sizes = group_sizes(quarter)
    starts = np.cumsum([0] + sizes)
    ordered = np.stack(
        [
            np.concatenate(
                [
                    lists[of_y, of_bit ^ flip, start : start + size].reshape(-1)
                    for start, size in zip(starts, sizes)
                    for flip in range(2)
                ]
            )
            for of_y in range(2)
            for of_bit in range(2)
        ]
    ).astype(np.int32)
    pairs = lax.dynamic_index_in_dim(jnp.asarray(ordered), y * 2 + low_bit, 0, keepdims=False)
    scalars = jnp.concatenate([jnp.stack([z, y, x, core]).astype(jnp.int32), pairs])

    def part(step):
        return lax.dynamic_slice_in_dim(snapshots, (z ^ step) * cells, cells, 2)

    pieces = {(0, 0): part(0)}
    for step in range(1, z_count):
        pieces[step, 0] = swap(part(step), Z, step)
    layout = [(step, 0, component) for step, component in pieces]
    layout += [(step, 1, component) for step, component in pieces]
    chunks = list(pieces.values()) + [swap(piece, "y", 1) for piece in pieces.values()]

    def sums_shape(size):
        return jax.ShapeDtypeStruct((x_count, 2, size, rows_dev, block_size), jnp.float32)

    def call(kernel, size, out_shape, operands, name):
        vmem = pl.BlockSpec(memory_space=pltpu.VMEM)
        return pl.pallas_call(
            kernel,
            out_shape=out_shape,
            in_specs=[pl.BlockSpec(memory_space=pltpu.SMEM)] + [vmem] * len(operands),
            out_specs=[vmem] * len(out_shape),
            compiler_params=pltpu.CompilerParams(vmem_limit_bytes=VMEM_LIMIT),
            cost_estimate=pl.CostEstimate(
                flops=4 * size * block_size * block_size * components * cells,
                bytes_accessed=0,
                transcendentals=0,
            ),
            name=name,
        )(scalars, *operands)

    shapes = [sums_shape(size) for size in sizes for _ in range(2)]
    blocks_shape = jax.ShapeDtypeStruct(
        (block_count, block_size, components * cells), jnp.bfloat16
    )
    blocks, *sums = call(
        functools.partial(first_kernel, layout, 4),
        sizes[0],
        [blocks_shape] + shapes[:2],
        chunks,
        "tiles_first",
    )
    sums += call(
        functools.partial(second_kernel, 4 + 4 * sizes[0]),
        sum(sizes[1:]),
        shapes[2:],
        [blocks],
        "tiles_second",
    )

    last = []

    def step_call(kernel, out_shape, *operands, name):
        operands = lax.optimization_barrier((*operands, *last))[: len(operands)]
        vmem = pl.BlockSpec(memory_space=pltpu.VMEM)
        outs = pl.pallas_call(
            kernel,
            out_shape=out_shape,
            in_specs=[vmem] * len(operands),
            out_specs=[vmem] * len(out_shape),
            compiler_params=pltpu.CompilerParams(vmem_limit_bytes=VMEM_LIMIT),
            cost_estimate=pl.CostEstimate(
                flops=operands[0].size, bytes_accessed=0, transcendentals=0
            ),
            name=name,
        )(*operands)
        last[:] = outs[:1]
        return outs

    def float_shape(*shape):
        return jax.ShapeDtypeStruct((*shape, rows_dev, block_size), jnp.float32)

    def sum_core(index):
        keep, send = sums[2 * index], swap(sums[2 * index + 1], "core", 1)
        shapes = [float_shape(2, sizes[index])] * x_count
        mine, *away = step_call(split_sum_kernel, shapes, keep, send, name="sum_core")
        return mine, [swap(value, "x", step + 1) for step, value in enumerate(away)]

    def sum_x(index, mine, arrived):
        for value in arrived[:-1]:
            (mine,) = step_call(
                sum_kernel, [float_shape(2, sizes[index])], mine, value, name="sum_x"
            )
        shapes = [float_shape(sizes[index])] * 2
        mine, away = step_call(split_sum_kernel, shapes, mine, arrived[-1], name="sum_x")
        return mine, swap(away, Z, 1)

    def sum_low(index, mine, arrived):
        (mine,) = step_call(sum_kernel, [float_shape(sizes[index])], mine, arrived, name="sum_z")
        bits = 2
        while 2 * bits < z_count:
            (mine,) = step_call(
                sum_kernel, [float_shape(sizes[index])], mine, swap(mine, Z, bits), name="sum_z"
            )
            bits *= 2
        return mine, swap(mine, Z, bits)

    def to_owners(value, last_batch):
        if not last_batch:
            return [lax.all_gather(value, ("z_low", "y"))]
        both = [(i, i ^ (y_count + 1)) for i in range(block_count)]
        over_both = lax.ppermute(value, (*Z, "y"), both)
        parts = [value, swap(value, Z, 1), swap(value, "y", 1), over_both]
        return [part[None] for part in parts]

    parts = []
    state = [sum_core(index) for index in range(GROUPS)]
    for stage, which in ORDER:
        if stage == "x":
            state[which] = sum_x(which, *state[which])
        elif stage == "low":
            state[which] = sum_low(which, *state[which])
        elif stage == "high":
            state[which] = step_call(
                sum_kernel, [float_shape(sizes[which])], *state[which], name="sum_high"
            )
        else:
            counts = [sizes[index] for index in which]
            shape = (SCALE_ROWS + sum(counts) * rows_dev // 2, block_size)
            kernel = functools.partial(code_kernel, counts, [len(state[i]) for i in which])
            operands = [value for index in which for value in state[index]]
            (code,) = step_call(
                kernel, [jax.ShapeDtypeStruct(shape, jnp.int32)], *operands, name="finish"
            )
            parts += to_owners(code, which == BATCHES[-1])

    table = tile_table[0]
    row_block = table[:, 0]
    col_block = table[:, 1]
    first = jnp.maximum(row_block, 0)
    second = jnp.maximum(col_block, 0)
    pair = first * block_count - (first * (first - 1)) // 2 + second - first
    of_list, slot = pair // quarter, pair % quarter
    of_y, of_bit = of_list // 2, of_list % 2
    tile, lane, exponent_row, steps_row = (jnp.zeros_like(slot) for _ in range(4))
    for index, batch in enumerate(BATCHES):
        off = of_bit * 2 + of_y
        if batch == BATCHES[-1]:
            off = (of_y ^ y) * 2 + (of_bit ^ low_bit)
        start, end = int(starts[batch[0]]), int(starts[batch[-1] + 1])
        inside = (slot >= start) & (slot < end)
        header_rows = -(-(end - start) * rows_dev // block_size)
        at = (slot - start) * rows_dev
        top = (4 * index + off) * SCALE_ROWS + at // block_size
        tile = jnp.where(inside, 4 * start + off * (end - start) + slot - start, tile)
        lane = jnp.where(inside, at % block_size, lane)
        exponent_row = jnp.where(inside, top, exponent_row)
        steps_row = jnp.where(inside, top + header_rows, steps_row)
    places = jnp.concatenate(
        [tile, lane, exponent_row, steps_row, (row_block >= 0).astype(jnp.int32)]
    )
    vmem = pl.BlockSpec(memory_space=pltpu.VMEM)
    result = pl.pallas_call(
        functools.partial(place_kernel, scale_factor / (CODE_TOP * SCALE_STEPS)),
        out_shape=float_shape(table.shape[0]),
        in_specs=[pl.BlockSpec(memory_space=pltpu.SMEM)] + [vmem] * len(parts),
        out_specs=vmem,
        scratch_shapes=[
            pltpu.VMEM((4 * quarter * rows_dev // 2, block_size), jnp.int32),
            pltpu.VMEM((4 * len(BATCHES) * SCALE_ROWS, block_size), jnp.float32),
        ],
        compiler_params=pltpu.CompilerParams(vmem_limit_bytes=VMEM_LIMIT),
        cost_estimate=pl.CostEstimate(
            flops=table.shape[0] * rows_dev * block_size, bytes_accessed=0, transcendentals=0
        ),
        name="place_tiles",
    )(places, *parts)
    return result[None]


def solution(mesh):
    tm, space = mesh.shape["tm"], mesh.shape["space"]
    sizes = (tm // 2, 2, space // 2, 2)
    grid = Mesh(mesh.devices.reshape((tm // 4, 2, *sizes[1:])), (*Z, "y", "x", "core"))
    in_specs = (P(None, (*Z, "y"), ("x", "core")), P((*Z, "y"), None, None))
    out_specs = P((*Z, "y"), None, ("x", "core"), None)
    return jax.shard_map(
        functools.partial(per_device, *sizes),
        mesh=grid,
        in_specs=in_specs,
        out_specs=out_specs,
        check_vma=False,
    )
```

```python
import functools
import math

import jax
import jax.numpy as jnp
import numpy as np
from jax import lax
from jax.experimental import pallas as pl
from jax.experimental.pallas import tpu as pltpu
from jax.sharding import Mesh, PartitionSpec as P

VMEM_LIMIT = 24 * 2**20
GROUPS = 3
BATCHES = ((0, 1), (2,))
LOW_FIRST = (0,)
ORDER = (
    ("core", 0), ("core", 1), ("x", 1), ("low", 0), ("low", 1), ("core", 2), ("x", 0),
    ("x", 2), ("high", 1), ("low", 2), ("finish", BATCHES[0]), ("finish", BATCHES[1]),
)
CODE_TOP = 32767.0
SCALE_ROWS = 16
SCALE_STEPS = 8192.0


def tile_lists(block_count):
    rows, cols = np.triu_indices(block_count)
    return np.stack([rows, cols], axis=1).reshape(2, 2, -1, 2)


def group_sizes(quarter):
    return [len(piece) for piece in np.array_split(np.arange(quarter), GROUPS)]


def multiply_tiles(scalars, first_pair, blocks, keep_ref, send_ref, low_first):
    x, core = scalars[2], scalars[3]
    group_size = keep_ref.shape[2]
    rows_dev = keep_ref.shape[3]
    part_count = blocks.shape[1] // rows_dev

    def one_slot(slot, carry):
        for low in range(2):
            where = first_pair + 2 * (low * group_size + slot)
            tile = lax.dot_general(
                blocks[scalars[where]],
                blocks[scalars[where + 1]],
                (((1,), (1,)), ((), ())),
                preferred_element_type=jnp.float32,
            )
            parts = [tile[part * rows_dev : (part + 1) * rows_dev] for part in range(part_count)]
            for step in range(part_count // 2):
                even, odd = parts[2 * step], parts[2 * step + 1]
                target = x ^ step
                place = (low, target) if low_first else (target, low)
                keep_ref[place[0], place[1], slot] = jnp.where(core == 0, even, odd)
                send_ref[place[0], place[1], slot] = jnp.where(core == 0, odd, even)
        return carry

    lax.fori_loop(0, group_size, one_slot, 0)


def multiply_groups(scalars, first_pair, blocks, groups, outs):
    for index, keep_ref, send_ref in zip(groups, outs[::2], outs[1::2]):
        multiply_tiles(scalars, first_pair, blocks, keep_ref, send_ref, index in LOW_FIRST)
        first_pair += 4 * keep_ref.shape[2]


def first_kernel(layout, first_pair, scalars, *refs):
    pieces = refs[: len(layout)]
    blocks = refs[len(layout)]
    z, y = scalars[0], scalars[1]
    for (step, other, component), piece in zip(layout, pieces):
        block = (z ^ step) * 2 + (y ^ other)
        cells = piece.shape[2]
        for index in range(piece.shape[0]):
            start = (component + index) * cells
            blocks[block, :, start : start + cells] = piece[index]
    multiply_groups(scalars, first_pair, blocks, range(1), refs[len(layout) + 1 :])


def second_kernel(first_pair, scalars, blocks, *outs):
    multiply_groups(scalars, first_pair, blocks, range(1, GROUPS), outs)


def split_sum_kernel(left, right, *outs):
    for index, out in enumerate(outs):
        out[...] = left[index] + right[index]


def sum_kernel(left, right, out):
    out[...] = left[...] + right[...]


def code_kernel(sizes, pairs, *refs):
    code = refs[-1]
    refs = list(refs[:-1])
    rows, columns = refs[0].shape[1:]
    header_rows = -(-sum(sizes) * rows // columns)
    row_of = lax.broadcasted_iota(jnp.int32, (rows, columns), 0)
    lane_of = lax.broadcasted_iota(jnp.int32, (rows, columns), 1)
    place = lax.broadcasted_iota(jnp.int32, (SCALE_ROWS, columns), 0)
    header = jnp.zeros((SCALE_ROWS, columns), jnp.float32)
    slot = 0
    for size, pair in zip(sizes, pairs):
        terms = [refs.pop(0) for _ in range(pair)]
        for index in range(size):
            total = sum((term[index] for term in terms[1:]), terms[0][index])
            top = jnp.max(jnp.abs(total), axis=1, keepdims=True)
            filled = top > 0
            exponent = jnp.log(jnp.where(filled, top, 1.0)) * (1.0 / math.log(2.0))
            exponent = jnp.clip(jnp.floor(exponent), -120.0, 120.0)
            power = jnp.exp(exponent * math.log(2.0))
            steps = jnp.where(filled, jnp.ceil(top / power * SCALE_STEPS), 0.0)
            scale = steps * power * (1.0 / SCALE_STEPS)
            factor = jnp.where(filled, CODE_TOP / jnp.where(filled, scale, 1.0), 0.0)
            rounded = jnp.clip(jnp.round(total * factor), -CODE_TOP, CODE_TOP)
            start = SCALE_ROWS + slot * rows
            code[start : start + rows, :] = rounded.astype(jnp.int32).astype(jnp.int16)
            row, lane = divmod(slot * rows, columns)
            diagonal = lane_of == row_of + lane
            for at, value in ((row, exponent), (row + header_rows, steps)):
                across = jnp.sum(jnp.where(diagonal, value, 0.0), axis=0, keepdims=True)
                header += jnp.where(place == at, across, 0.0)
            slot += 1
    code[:SCALE_ROWS, :] = header.astype(jnp.int32).astype(jnp.int16)


def place_kernel(factor, scalars, *refs):
    out, codes, headers = refs[-3:]
    slots, rows, columns = out.shape
    at = 0
    for index, part in enumerate(refs[:-3]):
        count = part.shape[0] - SCALE_ROWS
        start = index * SCALE_ROWS
        headers[start : start + SCALE_ROWS, :] = (
            part[:SCALE_ROWS, :].astype(jnp.int32).astype(jnp.float32)
        )
        codes[at : at + count, :] = part[SCALE_ROWS:, :]
        at += count
    row_of = lax.broadcasted_iota(jnp.int32, (rows, columns), 0)
    lane_of = lax.broadcasted_iota(jnp.int32, (rows, columns), 1)

    def one_slot(slot, carry):
        tile, lane, exponent_row, steps_row, filled = (
            scalars[kind * slots + slot] for kind in range(5)
        )
        exponent = headers[pl.ds(exponent_row, 1), :]
        steps = headers[pl.ds(steps_row, 1), :]
        scale = steps * jnp.exp(exponent * math.log(2.0)) * factor
        scale = jnp.where(filled > 0, scale, 0.0)
        column = jnp.sum(
            jnp.where(lane_of == row_of + lane, scale, 0.0), axis=1, keepdims=True
        )
        code = codes[pl.ds(pl.multiple_of(tile * rows, rows), rows), :]
        out[slot] = code.astype(jnp.int32).astype(jnp.float32) * column
        return carry

    lax.fori_loop(0, slots, one_slot, 0)


def per_device(z_count, y_count, x_count, core_count, snapshots, tile_table):
    components, block_size, cells_dev = snapshots.shape
    block_count = z_count * y_count
    space_count = x_count * core_count
    rows_dev = block_size // space_count
    scale_factor = 1.0 / math.sqrt(components * cells_dev * space_count)
    z, y, x, core = (lax.axis_index(name) for name in ("z", "y", "x", "core"))
    low_bit = z & 1
    cells = cells_dev // z_count

    def swap(value, axis, bits):
        size = lax.axis_size(axis)
        return lax.ppermute(value, axis, [(i, i ^ bits) for i in range(size)])

    lists = tile_lists(block_count)
    quarter = lists.shape[2]
    sizes = group_sizes(quarter)
    starts = np.cumsum([0] + sizes)
    ordered = np.stack(
        [
            np.concatenate(
                [
                    lists[of_y, of_bit ^ flip, start : start + size].reshape(-1)
                    for start, size in zip(starts, sizes)
                    for flip in range(2)
                ]
            )
            for of_y in range(2)
            for of_bit in range(2)
        ]
    ).astype(np.int32)
    pairs = lax.dynamic_index_in_dim(jnp.asarray(ordered), y * 2 + low_bit, 0, keepdims=False)
    scalars = jnp.concatenate([jnp.stack([z, y, x, core]).astype(jnp.int32), pairs])

    def part(step):
        return lax.dynamic_slice_in_dim(snapshots, (z ^ step) * cells, cells, 2)

    pieces = {(0, 0): part(0)}
    for step in range(1, z_count):
        pieces[step, 0] = swap(part(step), "z", step)
    layout = [(step, 0, component) for step, component in pieces]
    layout += [(step, 1, component) for step, component in pieces]
    chunks = list(pieces.values()) + [swap(piece, "y", 1) for piece in pieces.values()]

    def sums_shape(index):
        lead = (2, x_count) if index in LOW_FIRST else (x_count, 2)
        return jax.ShapeDtypeStruct((*lead, sizes[index], rows_dev, block_size), jnp.float32)

    def call(kernel, size, out_shape, operands, name):
        vmem = pl.BlockSpec(memory_space=pltpu.VMEM)
        return pl.pallas_call(
            kernel,
            out_shape=out_shape,
            in_specs=[pl.BlockSpec(memory_space=pltpu.SMEM)] + [vmem] * len(operands),
            out_specs=[vmem] * len(out_shape),
            compiler_params=pltpu.CompilerParams(vmem_limit_bytes=VMEM_LIMIT),
            cost_estimate=pl.CostEstimate(
                flops=4 * size * block_size * block_size * components * cells,
                bytes_accessed=0,
                transcendentals=0,
            ),
            name=name,
        )(scalars, *operands)

    shapes = [sums_shape(index) for index in range(GROUPS) for _ in range(2)]
    blocks_shape = jax.ShapeDtypeStruct(
        (block_count, block_size, components * cells), jnp.bfloat16
    )
    blocks, *sums = call(
        functools.partial(first_kernel, layout, 4),
        sizes[0],
        [blocks_shape] + shapes[:2],
        chunks,
        "tiles_first",
    )
    sums += call(
        functools.partial(second_kernel, 4 + 4 * sizes[0]),
        sum(sizes[1:]),
        shapes[2:],
        [blocks],
        "tiles_second",
    )

    last = []

    def step_call(kernel, out_shape, *operands, name):
        operands = lax.optimization_barrier((*operands, *last))[: len(operands)]
        vmem = pl.BlockSpec(memory_space=pltpu.VMEM)
        outs = pl.pallas_call(
            kernel,
            out_shape=out_shape,
            in_specs=[vmem] * len(operands),
            out_specs=[vmem] * len(out_shape),
            compiler_params=pltpu.CompilerParams(vmem_limit_bytes=VMEM_LIMIT),
            cost_estimate=pl.CostEstimate(
                flops=operands[0].size, bytes_accessed=0, transcendentals=0
            ),
            name=name,
        )(*operands)
        last[:] = outs[:1]
        return outs

    def float_shape(*shape):
        return jax.ShapeDtypeStruct((*shape, rows_dev, block_size), jnp.float32)

    def split_sum(shape, left, right, name):
        shapes = [float_shape(*shape[1:])] * shape[0]
        mine, *away = step_call(split_sum_kernel, shapes, left, right, name=name)
        return mine, away

    def plain_sum(left, right, name):
        shape = jax.ShapeDtypeStruct(left.shape, left.dtype)
        return step_call(sum_kernel, [shape], left, right, name=name)[0]

    def over_x(away):
        return [swap(value, "x", step + 1) for step, value in enumerate(away)]

    def over_high(mine):
        bits = 2
        while 2 * bits < z_count:
            mine = plain_sum(mine, swap(mine, "z", bits), "sum_z")
            bits *= 2
        return mine, swap(mine, "z", bits)

    def sum_core(index):
        keep, send = sums[2 * index : 2 * index + 2]
        send = swap(send, "core", 1)
        if index in LOW_FIRST:
            mine, away = split_sum((2, x_count, sizes[index]), keep, send, "sum_core")
            return mine, swap(away[0], "z", 1)
        mine, away = split_sum((x_count, 2, sizes[index]), keep, send, "sum_core")
        if index > 1:
            arrived = state[0][1]
            away = lax.optimization_barrier((*away, *arrived))[: len(away)]
        return mine, over_x(away)

    def sum_x(index, mine, arrived):
        for value in arrived[:-1]:
            mine = plain_sum(mine, value, "sum_x")
        if index in LOW_FIRST:
            return over_high(plain_sum(mine, arrived[-1], "sum_x"))
        mine, away = split_sum((2, sizes[index]), mine, arrived[-1], "sum_x")
        return mine, swap(away[0], "z", 1)

    def sum_low(index, mine, arrived):
        if index in LOW_FIRST:
            mine, away = split_sum((x_count, sizes[index]), mine, arrived, "sum_z")
            return mine, over_x(away)
        return over_high(plain_sum(mine, arrived, "sum_z"))

    def to_owners(value):
        both = [(i, i ^ (y_count + 1)) for i in range(block_count)]
        over_both = lax.ppermute(value, ("z", "y"), both)
        return [value, swap(value, "z", 1), swap(value, "y", 1), over_both]

    parts = []
    state = {}
    for stage, which in ORDER:
        if stage == "core":
            state[which] = sum_core(which)
        elif stage == "x":
            state[which] = sum_x(which, *state[which])
        elif stage == "low":
            state[which] = sum_low(which, *state[which])
        elif stage == "high":
            state[which] = [plain_sum(*state[which], "sum_high")]
        else:
            counts = [sizes[index] for index in which]
            shape = (SCALE_ROWS + sum(counts) * rows_dev, block_size)
            kernel = functools.partial(code_kernel, counts, [len(state[i]) for i in which])
            operands = [value for index in which for value in state[index]]
            (code,) = step_call(
                kernel, [jax.ShapeDtypeStruct(shape, jnp.int16)], *operands, name="finish"
            )
            parts += to_owners(code)

    table = tile_table[0]
    row_block = table[:, 0]
    col_block = table[:, 1]
    first = jnp.maximum(row_block, 0)
    second = jnp.maximum(col_block, 0)
    pair = first * block_count - (first * (first - 1)) // 2 + second - first
    of_list, slot = pair // quarter, pair % quarter
    off = ((of_list // 2) ^ y) * 2 + ((of_list % 2) ^ low_bit)
    tile, lane, exponent_row, steps_row = (jnp.zeros_like(slot) for _ in range(4))
    for index, batch in enumerate(BATCHES):
        start, end = int(starts[batch[0]]), int(starts[batch[-1] + 1])
        inside = (slot >= start) & (slot < end)
        header_rows = -(-(end - start) * rows_dev // block_size)
        at = (slot - start) * rows_dev
        top = (4 * index + off) * SCALE_ROWS + at // block_size
        tile = jnp.where(inside, 4 * start + off * (end - start) + slot - start, tile)
        lane = jnp.where(inside, at % block_size, lane)
        exponent_row = jnp.where(inside, top, exponent_row)
        steps_row = jnp.where(inside, top + header_rows, steps_row)
    places = jnp.concatenate(
        [tile, lane, exponent_row, steps_row, (row_block >= 0).astype(jnp.int32)]
    )
    vmem = pl.BlockSpec(memory_space=pltpu.VMEM)
    result = pl.pallas_call(
        functools.partial(place_kernel, scale_factor / (CODE_TOP * SCALE_STEPS)),
        out_shape=float_shape(table.shape[0]),
        in_specs=[pl.BlockSpec(memory_space=pltpu.SMEM)] + [vmem] * len(parts),
        out_specs=vmem,
        scratch_shapes=[
            pltpu.VMEM((4 * quarter * rows_dev, block_size), jnp.int16),
            pltpu.VMEM((len(parts) * SCALE_ROWS, block_size), jnp.float32),
        ],
        compiler_params=pltpu.CompilerParams(vmem_limit_bytes=VMEM_LIMIT),
        cost_estimate=pl.CostEstimate(
            flops=table.shape[0] * rows_dev * block_size, bytes_accessed=0, transcendentals=0
        ),
        name="place_tiles",
    )(places, *parts)
    return result[None]


def solution(mesh):
    tm, space = mesh.shape["tm"], mesh.shape["space"]
    sizes = (tm // 2, 2, space // 2, 2)
    grid = Mesh(mesh.devices.reshape(sizes), ("z", "y", "x", "core"))
    in_specs = (P(None, ("z", "y"), ("x", "core")), P(("z", "y"), None, None))
    out_specs = P(("z", "y"), None, ("x", "core"), None)
    return jax.shard_map(
        functools.partial(per_device, *sizes),
        mesh=grid,
        in_specs=in_specs,
        out_specs=out_specs,
        check_vma=False,
    )
```

```python
import functools
import math

import jax
import jax.numpy as jnp
import numpy as np
from jax import lax
from jax.experimental import pallas as pl
from jax.experimental.pallas import tpu as pltpu
from jax.sharding import Mesh, PartitionSpec as P

VMEM_LIMIT = 24 * 2**20
GROUPS = 3
BATCHES = ((0, 1), (2,))
CALLS = ((0, 1), (2,))
LOW_FIRST = (0,)
ORDER = (
    ("core", 0), ("x", 1), ("low", 0), ("low", 1), ("core", 1), ("x", 0),
    ("x", 2), ("high", 1), ("low", 2), ("finish", BATCHES[0]), ("finish", BATCHES[1]),
    ("stack", None),
)
CODE_TOP = 32767.0
SCALE_ROWS = 16
SCALE_STEPS = 8192.0


def tile_lists(block_count):
    rows, cols = np.triu_indices(block_count)
    return np.stack([rows, cols], axis=1).reshape(2, 2, -1, 2)


def group_sizes(quarter):
    return [len(piece) for piece in np.array_split(np.arange(quarter), GROUPS)]


def multiply_tiles(scalars, first_pair, blocks, keep_ref, send_ref, offset, size, low_first):
    x, core = scalars[2], scalars[3]
    rows_dev = keep_ref.shape[2]
    part_count = blocks.shape[1] // rows_dev

    def one_slot(slot, carry):
        for low in range(2):
            where = first_pair + 2 * (low * size + slot)
            tile = lax.dot_general(
                blocks[scalars[where]],
                blocks[scalars[where + 1]],
                (((1,), (1,)), ((), ())),
                preferred_element_type=jnp.float32,
            )
            parts = [tile[part * rows_dev : (part + 1) * rows_dev] for part in range(part_count)]
            for step in range(part_count // 2):
                even, odd = parts[2 * step], parts[2 * step + 1]
                target = x ^ step
                place = low * (part_count // 2) + target if low_first else 2 * target + low
                keep_ref[place, offset + slot] = jnp.where(core == 0, even, odd)
                send_ref[place, offset + slot] = jnp.where(core == 0, odd, even)
        return carry

    lax.fori_loop(0, size, one_slot, 0)


def multiply_groups(scalars, first_pair, sizes, blocks, groups, outs):
    offset = 0
    for index in groups:
        multiply_tiles(
            scalars, first_pair, blocks, *outs, offset, sizes[index], index in LOW_FIRST
        )
        first_pair += 4 * sizes[index]
        offset += sizes[index]


def first_kernel(layout, first_pair, sizes, scalars, *refs):
    pieces = refs[: len(layout)]
    blocks = refs[len(layout)]
    z, y = scalars[0], scalars[1]
    for (step, other, component), piece in zip(layout, pieces):
        block = (z ^ step) * 2 + (y ^ other)
        cells = piece.shape[2]
        for index in range(piece.shape[0]):
            start = (component + index) * cells
            blocks[block, :, start : start + cells] = piece[index]
    multiply_groups(scalars, first_pair, sizes, blocks, CALLS[0], refs[len(layout) + 1 :])


def second_kernel(first_pair, sizes, scalars, blocks, *outs):
    multiply_groups(scalars, first_pair, sizes, blocks, CALLS[1], outs)


def core_sum_kernel(cuts, keep, send, *outs):
    outs = list(outs)
    for offset, size, block in cuts:
        for start in range(0, keep.shape[0], block):
            place = (slice(start, start + block), slice(offset, offset + size))
            outs.pop(0)[...] = keep[place] + send[place]


def split_sum_kernel(left, right, *outs):
    for index, out in enumerate(outs):
        out[...] = left[index] + right[index]


def sum_kernel(left, right, out):
    out[...] = left[...] + right[...]


def code_kernel(sizes, pairs, *refs):
    code = refs[-1]
    refs = list(refs[:-1])
    rows, columns = refs[0].shape[1:]
    header_rows = -(-sum(sizes) * rows // columns)
    row_of = lax.broadcasted_iota(jnp.int32, (rows, columns), 0)
    lane_of = lax.broadcasted_iota(jnp.int32, (rows, columns), 1)
    place = lax.broadcasted_iota(jnp.int32, (SCALE_ROWS, columns), 0)
    header = jnp.zeros((SCALE_ROWS, columns), jnp.float32)
    slot = 0
    for size, pair in zip(sizes, pairs):
        terms = [refs.pop(0) for _ in range(pair)]
        for index in range(size):
            total = sum((term[index] for term in terms[1:]), terms[0][index])
            top = jnp.max(jnp.abs(total), axis=1, keepdims=True)
            filled = top > 0
            exponent = jnp.log(jnp.where(filled, top, 1.0)) * (1.0 / math.log(2.0))
            exponent = jnp.clip(jnp.floor(exponent), -120.0, 120.0)
            power = jnp.exp(exponent * math.log(2.0))
            steps = jnp.where(filled, jnp.ceil(top / power * SCALE_STEPS), 0.0)
            scale = steps * power * (1.0 / SCALE_STEPS)
            factor = jnp.where(filled, CODE_TOP / jnp.where(filled, scale, 1.0), 0.0)
            rounded = jnp.clip(jnp.round(total * factor), -CODE_TOP, CODE_TOP)
            start = SCALE_ROWS + slot * rows
            code[start : start + rows, :] = rounded.astype(jnp.int32).astype(jnp.int16)
            row, lane = divmod(slot * rows, columns)
            diagonal = lane_of == row_of + lane
            for at, value in ((row, exponent), (row + header_rows, steps)):
                across = jnp.sum(jnp.where(diagonal, value, 0.0), axis=0, keepdims=True)
                header += jnp.where(place == at, across, 0.0)
            slot += 1
    code[:SCALE_ROWS, :] = header.astype(jnp.int32).astype(jnp.int16)


def stack_kernel(*refs):
    out = refs[-1]
    for index, part in enumerate(refs[:-1]):
        out[index] = part[...]


def place_kernel(factor, batch_count, scalars, *refs):
    out, headers = refs[-2 - batch_count : -batch_count]
    stacks = list(refs[-batch_count:])
    slots, rows, columns = out.shape
    refs = list(refs[: -2 - batch_count])
    for index in range(batch_count):
        if len(refs[0].shape) == 3:
            stacks[index] = refs.pop(0)
            parts = [stacks[index].at[part] for part in range(4)]
        else:
            parts, refs = refs[:4], refs[4:]
            for part, ref in enumerate(parts):
                stacks[index][part] = ref[...]
        for part, ref in enumerate(parts):
            start = (4 * index + part) * SCALE_ROWS
            headers[start : start + SCALE_ROWS, :] = (
                ref[:SCALE_ROWS, :].astype(jnp.int32).astype(jnp.float32)
            )
    row_of = lax.broadcasted_iota(jnp.int32, (rows, columns), 0)
    lane_of = lax.broadcasted_iota(jnp.int32, (rows, columns), 1)

    def one_slot(slot, carry):
        batch, part, row, lane, exponent_row, steps_row, filled = (
            scalars[kind * slots + slot] for kind in range(7)
        )
        exponent = headers[pl.ds(exponent_row, 1), :]
        steps = headers[pl.ds(steps_row, 1), :]
        scale = steps * jnp.exp(exponent * math.log(2.0)) * factor
        scale = jnp.where(filled > 0, scale, 0.0)
        column = jnp.sum(
            jnp.where(lane_of == row_of + lane, scale, 0.0), axis=1, keepdims=True
        )
        for index, stack in enumerate(stacks):

            @pl.when(batch == index)
            def _():
                code = stack[part, pl.ds(pl.multiple_of(row, SCALE_ROWS), rows), :]
                out[slot] = code.astype(jnp.int32).astype(jnp.float32) * column

        return carry

    lax.fori_loop(0, slots, one_slot, 0)


def per_device(z_count, y_count, x_count, core_count, snapshots, tile_table):
    components, block_size, cells_dev = snapshots.shape
    block_count = z_count * y_count
    space_count = x_count * core_count
    rows_dev = block_size // space_count
    scale_factor = 1.0 / math.sqrt(components * cells_dev * space_count)
    z, y, x, core = (lax.axis_index(name) for name in ("z", "y", "x", "core"))
    low_bit = z & 1
    cells = cells_dev // z_count

    def swap(value, axis, bits):
        size = lax.axis_size(axis)
        return lax.ppermute(value, axis, [(i, i ^ bits) for i in range(size)])

    lists = tile_lists(block_count)
    quarter = lists.shape[2]
    sizes = group_sizes(quarter)
    starts = np.cumsum([0] + sizes)
    ordered = np.stack(
        [
            np.concatenate(
                [
                    lists[of_y, of_bit ^ flip, start : start + size].reshape(-1)
                    for start, size in zip(starts, sizes)
                    for flip in range(2)
                ]
            )
            for of_y in range(2)
            for of_bit in range(2)
        ]
    ).astype(np.int32)
    pairs = lax.dynamic_index_in_dim(jnp.asarray(ordered), y * 2 + low_bit, 0, keepdims=False)
    scalars = jnp.concatenate([jnp.stack([z, y, x, core]).astype(jnp.int32), pairs])

    def part(step, values):
        return lax.dynamic_slice_in_dim(values, (z ^ step) * cells, cells, 2)

    cut = {step: part(step, snapshots) for step in range(1, z_count, 2)}
    again = lax.optimization_barrier((snapshots, *cut.values()))[0]
    cut.update({step: part(step, again) for step in range(0, z_count, 2)})
    pieces = {(0, 0): cut[0]}
    for step in range(1, z_count):
        pieces[step, 0] = swap(cut[step], "z", step)
    layout = [(step, 0, component) for step, component in pieces]
    layout += [(step, 1, component) for step, component in pieces]
    chunks = list(pieces.values()) + [swap(piece, "y", 1) for piece in pieces.values()]

    def sums_shape(groups):
        count = sum(sizes[index] for index in groups)
        return jax.ShapeDtypeStruct((2 * x_count, count, rows_dev, block_size), jnp.float32)

    def call(kernel, size, out_shape, operands, name):
        vmem = pl.BlockSpec(memory_space=pltpu.VMEM)
        return pl.pallas_call(
            kernel,
            out_shape=out_shape,
            in_specs=[pl.BlockSpec(memory_space=pltpu.SMEM)] + [vmem] * len(operands),
            out_specs=[vmem] * len(out_shape),
            compiler_params=pltpu.CompilerParams(vmem_limit_bytes=VMEM_LIMIT),
            cost_estimate=pl.CostEstimate(
                flops=4 * size * block_size * block_size * components * cells,
                bytes_accessed=0,
                transcendentals=0,
            ),
            name=name,
        )(scalars, *operands)

    blocks_shape = jax.ShapeDtypeStruct(
        (block_count, block_size, components * cells), jnp.bfloat16
    )
    counts = [sum(sizes[index] for index in groups) for groups in CALLS]
    blocks, *sums = call(
        functools.partial(first_kernel, layout, 4, sizes),
        counts[0],
        [blocks_shape] + [sums_shape(CALLS[0])] * 2,
        chunks,
        "tiles_first",
    )
    sums += call(
        functools.partial(second_kernel, 4 + 4 * counts[0], sizes),
        counts[1],
        [sums_shape(CALLS[1])] * 2,
        [blocks],
        "tiles_second",
    )

    last = []

    def step_call(kernel, out_shape, *operands, name):
        operands = lax.optimization_barrier((*operands, *last))[: len(operands)]
        vmem = pl.BlockSpec(memory_space=pltpu.VMEM)
        outs = pl.pallas_call(
            kernel,
            out_shape=out_shape,
            in_specs=[vmem] * len(operands),
            out_specs=[vmem] * len(out_shape),
            compiler_params=pltpu.CompilerParams(vmem_limit_bytes=VMEM_LIMIT),
            cost_estimate=pl.CostEstimate(
                flops=operands[0].size, bytes_accessed=0, transcendentals=0
            ),
            name=name,
        )(*operands)
        last[:] = outs[:1]
        return outs

    def float_shape(*shape):
        return jax.ShapeDtypeStruct((*shape, rows_dev, block_size), jnp.float32)

    def split_sum(shape, left, right, name):
        shapes = [float_shape(*shape[1:])] * shape[0]
        mine, *away = step_call(split_sum_kernel, shapes, left, right, name=name)
        return mine, away

    def plain_sum(left, right, name):
        shape = jax.ShapeDtypeStruct(left.shape, left.dtype)
        return step_call(sum_kernel, [shape], left, right, name=name)[0]

    def over_x(away):
        return [swap(value, "x", step + 1) for step, value in enumerate(away)]

    def over_high(mine):
        bits = 2
        while 2 * bits < z_count:
            mine = plain_sum(mine, swap(mine, "z", bits), "sum_z")
            bits *= 2
        return mine, swap(mine, "z", bits)

    def sum_core(which):
        keep, send = sums[2 * which : 2 * which + 2]
        send = swap(send, "core", 1)
        cuts, shapes, offset = [], [], 0
        for index in CALLS[which]:
            block = x_count if index in LOW_FIRST else 2
            cuts.append((offset, sizes[index], block))
            shapes += [float_shape(block, sizes[index])] * (2 * x_count // block)
            offset += sizes[index]
        outs = list(
            step_call(
                functools.partial(core_sum_kernel, cuts), shapes, keep, send, name="sum_core"
            )
        )
        for index, (_, _, block) in zip(CALLS[which], cuts):
            count = 2 * x_count // block
            (mine, *away), outs = outs[:count], outs[count:]
            if index in LOW_FIRST:
                state[index] = mine, swap(away[0], "z", 1)
                continue
            if which > 0:
                away = lax.optimization_barrier((*away, *state[0][1]))[: len(away)]
            state[index] = mine, over_x(away)

    def sum_x(index, mine, arrived):
        for value in arrived[:-1]:
            mine = plain_sum(mine, value, "sum_x")
        if index in LOW_FIRST:
            return over_high(plain_sum(mine, arrived[-1], "sum_x"))
        mine, away = split_sum((2, sizes[index]), mine, arrived[-1], "sum_x")
        return mine, swap(away[0], "z", 1)

    def sum_low(index, mine, arrived):
        if index in LOW_FIRST:
            mine, away = split_sum((x_count, sizes[index]), mine, arrived, "sum_z")
            return mine, over_x(away)
        return over_high(plain_sum(mine, arrived, "sum_z"))

    def to_owners(value):
        both = [(i, i ^ (y_count + 1)) for i in range(block_count)]
        over_both = lax.ppermute(value, ("z", "y"), both)
        return [value, swap(value, "z", 1), swap(value, "y", 1), over_both]

    parts = []
    state = {}
    for stage, which in ORDER:
        if stage == "core":
            sum_core(which)
        elif stage == "x":
            state[which] = sum_x(which, *state[which])
        elif stage == "low":
            state[which] = sum_low(which, *state[which])
        elif stage == "high":
            state[which] = [plain_sum(*state[which], "sum_high")]
        elif stage == "stack":
            shape = jax.ShapeDtypeStruct((4, *parts[0].shape), parts[0].dtype)
            parts[:4] = step_call(stack_kernel, [shape], *parts[:4], name="stack")
        else:
            counts = [sizes[index] for index in which]
            shape = (SCALE_ROWS + sum(counts) * rows_dev, block_size)
            kernel = functools.partial(code_kernel, counts, [len(state[i]) for i in which])
            operands = [value for index in which for value in state[index]]
            (code,) = step_call(
                kernel, [jax.ShapeDtypeStruct(shape, jnp.int16)], *operands, name="finish"
            )
            parts += to_owners(code)

    table = tile_table[0]
    row_block = table[:, 0]
    col_block = table[:, 1]
    first = jnp.maximum(row_block, 0)
    second = jnp.maximum(col_block, 0)
    pair = first * block_count - (first * (first - 1)) // 2 + second - first
    of_list, slot = pair // quarter, pair % quarter
    off = ((of_list // 2) ^ y) * 2 + ((of_list % 2) ^ low_bit)
    in_batch, row, lane, exponent_row, steps_row = (jnp.zeros_like(slot) for _ in range(5))
    for index, batch in enumerate(BATCHES):
        start, end = int(starts[batch[0]]), int(starts[batch[-1] + 1])
        inside = (slot >= start) & (slot < end)
        header_rows = -(-(end - start) * rows_dev // block_size)
        at = (slot - start) * rows_dev
        top = (4 * index + off) * SCALE_ROWS + at // block_size
        in_batch = jnp.where(inside, index, in_batch)
        row = jnp.where(inside, SCALE_ROWS + at, row)
        lane = jnp.where(inside, at % block_size, lane)
        exponent_row = jnp.where(inside, top, exponent_row)
        steps_row = jnp.where(inside, top + header_rows, steps_row)
    filled = (row_block >= 0).astype(jnp.int32)
    places = jnp.concatenate([in_batch, off, row, lane, exponent_row, steps_row, filled])
    vmem = pl.BlockSpec(memory_space=pltpu.VMEM)
    result = pl.pallas_call(
        functools.partial(
            place_kernel, scale_factor / (CODE_TOP * SCALE_STEPS), len(BATCHES)
        ),
        out_shape=float_shape(table.shape[0]),
        in_specs=[pl.BlockSpec(memory_space=pltpu.SMEM)] + [vmem] * len(parts),
        out_specs=vmem,
        scratch_shapes=[
            pltpu.VMEM((4 * len(BATCHES) * SCALE_ROWS, block_size), jnp.float32)
        ] + [
            pltpu.VMEM(
                (4, SCALE_ROWS + sum(sizes[index] for index in batch) * rows_dev, block_size),
                jnp.int16,
            )
            for batch in BATCHES
        ],
        compiler_params=pltpu.CompilerParams(vmem_limit_bytes=VMEM_LIMIT),
        cost_estimate=pl.CostEstimate(
            flops=table.shape[0] * rows_dev * block_size, bytes_accessed=0, transcendentals=0
        ),
        name="place_tiles",
    )(places, *parts)
    return result[None]


def solution(mesh):
    tm, space = mesh.shape["tm"], mesh.shape["space"]
    sizes = (tm // 2, 2, space // 2, 2)
    grid = Mesh(mesh.devices.reshape(sizes), ("z", "y", "x", "core"))
    in_specs = (P(None, ("z", "y"), ("x", "core")), P(("z", "y"), None, None))
    out_specs = P(("z", "y"), None, ("x", "core"), None)
    return jax.shard_map(
        functools.partial(per_device, *sizes),
        mesh=grid,
        in_specs=in_specs,
        out_specs=out_specs,
        check_vma=False,
    )
```

```python
import functools
import math

import jax
import jax.numpy as jnp
import numpy as np
from jax import lax
from jax.experimental import pallas as pl
from jax.experimental.pallas import tpu as pltpu
from jax.sharding import Mesh, PartitionSpec as P

UNROLL = 4
VMEM_LIMIT = 24 * 2**20
GROUPS = 3
BATCHES = ((0, 1), (2,))
CALLS = ((0, 1), (2,))
LOW_FIRST = (0,)
ORDER = (
    ("core", 0), ("x", 1), ("low", 0), ("low", 1), ("core", 1), ("x", 0),
    ("x", 2), ("high", 1), ("low", 2), ("finish", BATCHES[0]), ("finish", BATCHES[1]),
    ("place", 0), ("place", 1),
)
CODE_TOP = 32767.0
SCALE_ROWS = 16
SCALE_STEPS = 8192.0


def tile_lists(block_count):
    rows, cols = np.triu_indices(block_count)
    return np.stack([rows, cols], axis=1).reshape(2, 2, -1, 2)


def group_sizes(quarter):
    return [len(piece) for piece in np.array_split(np.arange(quarter), GROUPS)]


def multiply_tiles(scalars, first_pair, blocks, keep_ref, send_ref, offset, size, low_first):
    x, core = scalars[2], scalars[3]
    rows_dev = keep_ref.shape[2]
    part_count = blocks.shape[1] // rows_dev

    def one_slot(slot, carry):
        for low in range(2):
            where = first_pair + 2 * (low * size + slot)
            tile = lax.dot_general(
                blocks[scalars[where]],
                blocks[scalars[where + 1]],
                (((1,), (1,)), ((), ())),
                preferred_element_type=jnp.float32,
            )
            parts = [tile[part * rows_dev : (part + 1) * rows_dev] for part in range(part_count)]
            for step in range(part_count // 2):
                even, odd = parts[2 * step], parts[2 * step + 1]
                target = x ^ step
                place = low * (part_count // 2) + target if low_first else 2 * target + low
                keep_ref[place, offset + slot] = jnp.where(core == 0, even, odd)
                send_ref[place, offset + slot] = jnp.where(core == 0, odd, even)
        return carry

    lax.fori_loop(0, size, one_slot, 0, unroll=size <= UNROLL)


def multiply_groups(scalars, first_pair, sizes, blocks, groups, outs):
    offset = 0
    for index in groups:
        multiply_tiles(
            scalars, first_pair, blocks, *outs, offset, sizes[index], index in LOW_FIRST
        )
        first_pair += 4 * sizes[index]
        offset += sizes[index]


def first_kernel(layout, first_pair, sizes, scalars, *refs):
    pieces = refs[: len(layout)]
    blocks = refs[len(layout)]
    z, y = scalars[0], scalars[1]
    for (step, other, component), piece in zip(layout, pieces):
        block = (z ^ step) * 2 + (y ^ other)
        cells = piece.shape[2]
        for index in range(piece.shape[0]):
            start = (component + index) * cells
            blocks[block, :, start : start + cells] = piece[index]
    multiply_groups(scalars, first_pair, sizes, blocks, CALLS[0], refs[len(layout) + 1 :])


def second_kernel(first_pair, sizes, scalars, blocks, *outs):
    multiply_groups(scalars, first_pair, sizes, blocks, CALLS[1], outs)


def core_sum_kernel(cuts, keep, send, *outs):
    outs = list(outs)
    for offset, size, block in cuts:
        for start in range(0, keep.shape[0], block):
            place = (slice(start, start + block), slice(offset, offset + size))
            outs.pop(0)[...] = keep[place] + send[place]


def split_sum_kernel(left, right, *outs):
    for index, out in enumerate(outs):
        out[...] = left[index] + right[index]


def sum_kernel(left, right, out):
    out[...] = left[...] + right[...]


def code_kernel(sizes, pairs, *refs):
    code = refs[-1]
    refs = list(refs[:-1])
    rows, columns = refs[0].shape[1:]
    header_rows = -(-sum(sizes) * rows // columns)
    row_of = lax.broadcasted_iota(jnp.int32, (rows, columns), 0)
    lane_of = lax.broadcasted_iota(jnp.int32, (rows, columns), 1)
    place = lax.broadcasted_iota(jnp.int32, (SCALE_ROWS, columns), 0)
    header = jnp.zeros((SCALE_ROWS, columns), jnp.float32)
    slot = 0
    for size, pair in zip(sizes, pairs):
        terms = [refs.pop(0) for _ in range(pair)]
        for index in range(size):
            total = sum((term[index] for term in terms[1:]), terms[0][index])
            top = jnp.max(jnp.abs(total), axis=1, keepdims=True)
            filled = top > 0
            exponent = jnp.log(jnp.where(filled, top, 1.0)) * (1.0 / math.log(2.0))
            exponent = jnp.clip(jnp.floor(exponent), -120.0, 120.0)
            power = jnp.exp(exponent * math.log(2.0))
            steps = jnp.where(filled, jnp.ceil(top / power * SCALE_STEPS), 0.0)
            scale = steps * power * (1.0 / SCALE_STEPS)
            factor = jnp.where(filled, CODE_TOP / jnp.where(filled, scale, 1.0), 0.0)
            rounded = jnp.clip(jnp.round(total * factor), -CODE_TOP, CODE_TOP)
            start = SCALE_ROWS + slot * rows
            code[start : start + rows, :] = rounded.astype(jnp.int32).astype(jnp.int16)
            row, lane = divmod(slot * rows, columns)
            diagonal = lane_of == row_of + lane
            for at, value in ((row, exponent), (row + header_rows, steps)):
                across = jnp.sum(jnp.where(diagonal, value, 0.0), axis=0, keepdims=True)
                header += jnp.where(place == at, across, 0.0)
            slot += 1
    code[:SCALE_ROWS, :] = header.astype(jnp.int32).astype(jnp.int16)


def place_kernel(factor, batch, scalars, *refs):
    parts, before = refs[:4], refs[4:-3]
    out, headers, stack = refs[-3:]
    slots, rows, columns = out.shape
    for index, part in enumerate(parts):
        start = index * SCALE_ROWS
        headers[start : start + SCALE_ROWS, :] = (
            part[:SCALE_ROWS, :].astype(jnp.int32).astype(jnp.float32)
        )
        stack[index] = part[...]
    out[...] = before[0][...] if before else jnp.zeros_like(out)
    row_of = lax.broadcasted_iota(jnp.int32, (rows, columns), 0)
    lane_of = lax.broadcasted_iota(jnp.int32, (rows, columns), 1)

    def one_slot(slot, carry):
        batch_of, part, row, lane, exponent_row, steps_row = (
            scalars[kind * slots + slot] for kind in range(6)
        )

        @pl.when(batch_of == batch)
        def _():
            exponent = headers[pl.ds(exponent_row, 1), :]
            steps = headers[pl.ds(steps_row, 1), :]
            scale = steps * jnp.exp(exponent * math.log(2.0)) * factor
            column = jnp.sum(
                jnp.where(lane_of == row_of + lane, scale, 0.0), axis=1, keepdims=True
            )
            code = stack[part, pl.ds(pl.multiple_of(row, SCALE_ROWS), rows), :]
            out[slot] = code.astype(jnp.int32).astype(jnp.float32) * column

        return carry

    lax.fori_loop(0, slots, one_slot, 0)


def per_device(z_count, y_count, x_count, core_count, snapshots, tile_table):
    components, block_size, cells_dev = snapshots.shape
    block_count = z_count * y_count
    space_count = x_count * core_count
    rows_dev = block_size // space_count
    scale_factor = 1.0 / math.sqrt(components * cells_dev * space_count)
    z, y, x, core = (lax.axis_index(name) for name in ("z", "y", "x", "core"))
    low_bit = z & 1
    cells = cells_dev // z_count

    def swap(value, axis, bits):
        size = lax.axis_size(axis)
        return lax.ppermute(value, axis, [(i, i ^ bits) for i in range(size)])

    lists = tile_lists(block_count)
    quarter = lists.shape[2]
    sizes = group_sizes(quarter)
    starts = np.cumsum([0] + sizes)
    ordered = np.stack(
        [
            np.concatenate(
                [
                    lists[of_y, of_bit ^ flip, start : start + size].reshape(-1)
                    for start, size in zip(starts, sizes)
                    for flip in range(2)
                ]
            )
            for of_y in range(2)
            for of_bit in range(2)
        ]
    ).astype(np.int32)
    pairs = lax.dynamic_index_in_dim(jnp.asarray(ordered), y * 2 + low_bit, 0, keepdims=False)
    scalars = jnp.concatenate([jnp.stack([z, y, x, core]).astype(jnp.int32), pairs])

    def part(step, values):
        return lax.dynamic_slice_in_dim(values, (z ^ step) * cells, cells, 2)

    cut = {step: part(step, snapshots) for step in range(1, z_count, 2)}
    again = lax.optimization_barrier((snapshots, *cut.values()))[0]
    cut.update({step: part(step, again) for step in range(0, z_count, 2)})
    pieces = {(0, 0): cut[0]}
    for step in range(1, z_count):
        pieces[step, 0] = swap(cut[step], "z", step)
    layout = [(step, 0, component) for step, component in pieces]
    layout += [(step, 1, component) for step, component in pieces]
    chunks = list(pieces.values()) + [swap(piece, "y", 1) for piece in pieces.values()]

    def sums_shape(groups):
        count = sum(sizes[index] for index in groups)
        return jax.ShapeDtypeStruct((2 * x_count, count, rows_dev, block_size), jnp.float32)

    def call(kernel, size, out_shape, operands, name):
        vmem = pl.BlockSpec(memory_space=pltpu.VMEM)
        return pl.pallas_call(
            kernel,
            out_shape=out_shape,
            in_specs=[pl.BlockSpec(memory_space=pltpu.SMEM)] + [vmem] * len(operands),
            out_specs=[vmem] * len(out_shape),
            compiler_params=pltpu.CompilerParams(vmem_limit_bytes=VMEM_LIMIT),
            cost_estimate=pl.CostEstimate(
                flops=4 * size * block_size * block_size * components * cells,
                bytes_accessed=0,
                transcendentals=0,
            ),
            name=name,
        )(scalars, *operands)

    blocks_shape = jax.ShapeDtypeStruct(
        (block_count, block_size, components * cells), jnp.bfloat16
    )
    counts = [sum(sizes[index] for index in groups) for groups in CALLS]
    blocks, *sums = call(
        functools.partial(first_kernel, layout, 4, sizes),
        counts[0],
        [blocks_shape] + [sums_shape(CALLS[0])] * 2,
        chunks,
        "tiles_first",
    )
    sums += call(
        functools.partial(second_kernel, 4 + 4 * counts[0], sizes),
        counts[1],
        [sums_shape(CALLS[1])] * 2,
        [blocks],
        "tiles_second",
    )

    last = []

    def step_call(kernel, out_shape, *operands, name):
        operands = lax.optimization_barrier((*operands, *last))[: len(operands)]
        vmem = pl.BlockSpec(memory_space=pltpu.VMEM)
        outs = pl.pallas_call(
            kernel,
            out_shape=out_shape,
            in_specs=[vmem] * len(operands),
            out_specs=[vmem] * len(out_shape),
            compiler_params=pltpu.CompilerParams(vmem_limit_bytes=VMEM_LIMIT),
            cost_estimate=pl.CostEstimate(
                flops=operands[0].size, bytes_accessed=0, transcendentals=0
            ),
            name=name,
        )(*operands)
        last[:] = outs[:1]
        return outs

    def float_shape(*shape):
        return jax.ShapeDtypeStruct((*shape, rows_dev, block_size), jnp.float32)

    def split_sum(shape, left, right, name):
        shapes = [float_shape(*shape[1:])] * shape[0]
        mine, *away = step_call(split_sum_kernel, shapes, left, right, name=name)
        return mine, away

    def plain_sum(left, right, name):
        shape = jax.ShapeDtypeStruct(left.shape, left.dtype)
        return step_call(sum_kernel, [shape], left, right, name=name)[0]

    def over_x(away):
        return [swap(value, "x", step + 1) for step, value in enumerate(away)]

    def over_high(mine):
        bits = 2
        while 2 * bits < z_count:
            mine = plain_sum(mine, swap(mine, "z", bits), "sum_z")
            bits *= 2
        return mine, swap(mine, "z", bits)

    def sum_core(which):
        keep, send = sums[2 * which : 2 * which + 2]
        send = swap(send, "core", 1)
        cuts, shapes, offset = [], [], 0
        for index in CALLS[which]:
            block = x_count if index in LOW_FIRST else 2
            cuts.append((offset, sizes[index], block))
            shapes += [float_shape(block, sizes[index])] * (2 * x_count // block)
            offset += sizes[index]
        outs = list(
            step_call(
                functools.partial(core_sum_kernel, cuts), shapes, keep, send, name="sum_core"
            )
        )
        for index, (_, _, block) in zip(CALLS[which], cuts):
            count = 2 * x_count // block
            (mine, *away), outs = outs[:count], outs[count:]
            if index in LOW_FIRST:
                state[index] = mine, swap(away[0], "z", 1)
                continue
            if which > 0:
                away = lax.optimization_barrier((*away, *state[0][1]))[: len(away)]
            state[index] = mine, over_x(away)

    def sum_x(index, mine, arrived):
        for value in arrived[:-1]:
            mine = plain_sum(mine, value, "sum_x")
        if index in LOW_FIRST:
            return over_high(plain_sum(mine, arrived[-1], "sum_x"))
        mine, away = split_sum((2, sizes[index]), mine, arrived[-1], "sum_x")
        return mine, swap(away[0], "z", 1)

    def sum_low(index, mine, arrived):
        if index in LOW_FIRST:
            mine, away = split_sum((x_count, sizes[index]), mine, arrived, "sum_z")
            return mine, over_x(away)
        return over_high(plain_sum(mine, arrived, "sum_z"))

    def to_owners(value):
        both = [(i, i ^ (y_count + 1)) for i in range(block_count)]
        over_both = lax.ppermute(value, ("z", "y"), both)
        return [value, swap(value, "z", 1), swap(value, "y", 1), over_both]

    table = tile_table[0]
    row_block = table[:, 0]
    col_block = table[:, 1]
    first = jnp.maximum(row_block, 0)
    second = jnp.maximum(col_block, 0)
    pair = first * block_count - (first * (first - 1)) // 2 + second - first
    of_list, slot = pair // quarter, pair % quarter
    off = ((of_list // 2) ^ y) * 2 + ((of_list % 2) ^ low_bit)
    in_batch, row, lane, exponent_row, steps_row = (jnp.zeros_like(slot) for _ in range(5))
    for index, batch in enumerate(BATCHES):
        start, end = int(starts[batch[0]]), int(starts[batch[-1] + 1])
        inside = (slot >= start) & (slot < end)
        header_rows = -(-(end - start) * rows_dev // block_size)
        at = (slot - start) * rows_dev
        top = off * SCALE_ROWS + at // block_size
        in_batch = jnp.where(inside, index, in_batch)
        row = jnp.where(inside, SCALE_ROWS + at, row)
        lane = jnp.where(inside, at % block_size, lane)
        exponent_row = jnp.where(inside, top, exponent_row)
        steps_row = jnp.where(inside, top + header_rows, steps_row)
    in_batch = jnp.where(row_block >= 0, in_batch, -1)
    places = jnp.concatenate([in_batch, off, row, lane, exponent_row, steps_row])

    parts, result = [], []
    state = {}
    for stage, which in ORDER:
        if stage == "core":
            sum_core(which)
        elif stage == "x":
            state[which] = sum_x(which, *state[which])
        elif stage == "low":
            state[which] = sum_low(which, *state[which])
        elif stage == "high":
            state[which] = [plain_sum(*state[which], "sum_high")]
        elif stage == "place":
            four = parts[4 * which : 4 * which + 4]
            operands = lax.optimization_barrier((places, *four, *result, *last))[:-1]
            vmem = pl.BlockSpec(memory_space=pltpu.VMEM)
            result = [
                pl.pallas_call(
                    functools.partial(
                        place_kernel, scale_factor / (CODE_TOP * SCALE_STEPS), which
                    ),
                    out_shape=float_shape(table.shape[0]),
                    in_specs=[pl.BlockSpec(memory_space=pltpu.SMEM)]
                    + [vmem] * (len(operands) - 1),
                    out_specs=vmem,
                    scratch_shapes=[
                        pltpu.VMEM((4 * SCALE_ROWS, block_size), jnp.float32),
                        pltpu.VMEM((4, *four[0].shape), jnp.int16),
                    ],
                    compiler_params=pltpu.CompilerParams(vmem_limit_bytes=VMEM_LIMIT),
                    cost_estimate=pl.CostEstimate(
                        flops=table.shape[0] * rows_dev * block_size,
                        bytes_accessed=0,
                        transcendentals=0,
                    ),
                    name="place_tiles",
                )(*operands)
            ]
        else:
            counts = [sizes[index] for index in which]
            shape = (SCALE_ROWS + sum(counts) * rows_dev, block_size)
            kernel = functools.partial(code_kernel, counts, [len(state[i]) for i in which])
            operands = [value for index in which for value in state[index]]
            (code,) = step_call(
                kernel, [jax.ShapeDtypeStruct(shape, jnp.int16)], *operands, name="finish"
            )
            parts += to_owners(code)

    return result[0][None]


def solution(mesh):
    tm, space = mesh.shape["tm"], mesh.shape["space"]
    sizes = (tm // 2, 2, space // 2, 2)
    grid = Mesh(mesh.devices.reshape(sizes), ("z", "y", "x", "core"))
    in_specs = (P(None, ("z", "y"), ("x", "core")), P(("z", "y"), None, None))
    out_specs = P(("z", "y"), None, ("x", "core"), None)
    return jax.shard_map(
        functools.partial(per_device, *sizes),
        mesh=grid,
        in_specs=in_specs,
        out_specs=out_specs,
        check_vma=False,
    )
```

```python
import functools
import math

import jax
import jax.numpy as jnp
import numpy as np
from jax import lax
from jax.experimental import pallas as pl
from jax.experimental.pallas import tpu as pltpu
from jax.sharding import Mesh, PartitionSpec as P

UNROLL = 4
VMEM_LIMIT = 24 * 2**20
GROUPS = 3
BATCHES = ((0, 1), (2,))
CALLS = ((0, 1), (2,))
LOW_FIRST = (0,)
ORDER = (
    ("core", 0), ("x", 1), ("low", 0), ("low", 1), ("core", 1), ("x", 0),
    ("x", 2), ("high", 1), ("low", 2), ("finish", BATCHES[0]), ("finish", BATCHES[1]),
    ("place", 0), ("place", 1),
)
CODE_TOP = 32767.0
SCALE_ROWS = 16
SCALE_STEPS = 8192.0


def tile_lists(block_count):
    rows, cols = np.triu_indices(block_count)
    return np.stack([rows, cols], axis=1).reshape(2, 2, -1, 2)


def group_sizes(quarter):
    return [len(piece) for piece in np.array_split(np.arange(quarter), GROUPS)]


def multiply_tiles(scalars, first_pair, blocks, keep_ref, send_ref, offset, size, low_first):
    x, core = scalars[2], scalars[3]
    rows_dev = keep_ref.shape[2]
    part_count = blocks.shape[1] // rows_dev

    def one_slot(slot, carry):
        for low in range(2):
            where = first_pair + 2 * (low * size + slot)
            tile = lax.dot_general(
                blocks[scalars[where]],
                blocks[scalars[where + 1]],
                (((1,), (1,)), ((), ())),
                preferred_element_type=jnp.float32,
            )
            parts = [tile[part * rows_dev : (part + 1) * rows_dev] for part in range(part_count)]
            for step in range(part_count // 2):
                even, odd = parts[2 * step], parts[2 * step + 1]
                target = x ^ step
                place = low * (part_count // 2) + target if low_first else 2 * target + low
                keep_ref[place, offset + slot] = jnp.where(core == 0, even, odd)
                send_ref[place, offset + slot] = jnp.where(core == 0, odd, even)
        return carry

    lax.fori_loop(0, size, one_slot, 0, unroll=size <= UNROLL)


def multiply_groups(scalars, first_pair, sizes, blocks, groups, outs):
    offset = 0
    for index in groups:
        multiply_tiles(
            scalars, first_pair, blocks, *outs, offset, sizes[index], index in LOW_FIRST
        )
        first_pair += 4 * sizes[index]
        offset += sizes[index]


def first_kernel(layout, first_pair, sizes, scalars, *refs):
    pieces = refs[: len(layout)]
    blocks = refs[len(layout)]
    z, y = scalars[0], scalars[1]
    for (step, other, component), piece in zip(layout, pieces):
        block = (z ^ step) * 2 + (y ^ other)
        cells = piece.shape[2]
        for index in range(piece.shape[0]):
            start = (component + index) * cells
            blocks[block, :, start : start + cells] = piece[index]
    multiply_groups(scalars, first_pair, sizes, blocks, CALLS[0], refs[len(layout) + 1 :])


def second_kernel(first_pair, sizes, scalars, blocks, *outs):
    multiply_groups(scalars, first_pair, sizes, blocks, CALLS[1], outs)


def copy_kernel(value, out):
    out[...] = value[...]


def core_sum_kernel(cuts, keep, send, *outs):
    outs = list(outs)
    for offset, size, block in cuts:
        for start in range(0, keep.shape[0], block):
            place = (slice(start, start + block), slice(offset, offset + size))
            outs.pop(0)[...] = keep[place] + send[place]


def split_sum_kernel(left, right, *outs):
    for index, out in enumerate(outs):
        out[...] = left[index] + right[index]


def sum_kernel(left, right, out):
    out[...] = left[...] + right[...]


def code_kernel(sizes, pairs, *refs):
    code = refs[-1]
    refs = list(refs[:-1])
    rows, columns = refs[0].shape[1:]
    header_rows = -(-sum(sizes) * rows // columns)
    row_of = lax.broadcasted_iota(jnp.int32, (rows, columns), 0)
    lane_of = lax.broadcasted_iota(jnp.int32, (rows, columns), 1)
    place = lax.broadcasted_iota(jnp.int32, (SCALE_ROWS, columns), 0)
    header = jnp.zeros((SCALE_ROWS, columns), jnp.float32)
    slot = 0
    for size, pair in zip(sizes, pairs):
        terms = [refs.pop(0) for _ in range(pair)]
        for index in range(size):
            total = sum((term[index] for term in terms[1:]), terms[0][index])
            top = jnp.max(jnp.abs(total), axis=1, keepdims=True)
            filled = top > 0
            exponent = jnp.log(jnp.where(filled, top, 1.0)) * (1.0 / math.log(2.0))
            exponent = jnp.clip(jnp.floor(exponent), -120.0, 120.0)
            power = jnp.exp(exponent * math.log(2.0))
            steps = jnp.where(filled, jnp.ceil(top / power * SCALE_STEPS), 0.0)
            scale = steps * power * (1.0 / SCALE_STEPS)
            factor = jnp.where(filled, CODE_TOP / jnp.where(filled, scale, 1.0), 0.0)
            rounded = jnp.clip(jnp.round(total * factor), -CODE_TOP, CODE_TOP)
            start = SCALE_ROWS + slot * rows
            code[start : start + rows, :] = rounded.astype(jnp.int32).astype(jnp.int16)
            row, lane = divmod(slot * rows, columns)
            diagonal = lane_of == row_of + lane
            for at, value in ((row, exponent), (row + header_rows, steps)):
                across = jnp.sum(jnp.where(diagonal, value, 0.0), axis=0, keepdims=True)
                header += jnp.where(place == at, across, 0.0)
            slot += 1
    code[:SCALE_ROWS, :] = header.astype(jnp.int32).astype(jnp.int16)


def place_kernel(factor, batch, scalars, *refs):
    parts, before = refs[:4], refs[4:-3]
    out, headers, stack = refs[-3:]
    slots, rows, columns = out.shape
    for index, part in enumerate(parts):
        start = index * SCALE_ROWS
        headers[start : start + SCALE_ROWS, :] = (
            part[:SCALE_ROWS, :].astype(jnp.int32).astype(jnp.float32)
        )
        stack[index] = part[...]
    out[...] = before[0][...] if before else jnp.zeros_like(out)
    row_of = lax.broadcasted_iota(jnp.int32, (rows, columns), 0)
    lane_of = lax.broadcasted_iota(jnp.int32, (rows, columns), 1)

    def one_slot(slot, carry):
        batch_of, part, row, lane, exponent_row, steps_row = (
            scalars[kind * slots + slot] for kind in range(6)
        )

        @pl.when(batch_of == batch)
        def _():
            exponent = headers[pl.ds(exponent_row, 1), :]
            steps = headers[pl.ds(steps_row, 1), :]
            scale = steps * jnp.exp(exponent * math.log(2.0)) * factor
            column = jnp.sum(
                jnp.where(lane_of == row_of + lane, scale, 0.0), axis=1, keepdims=True
            )
            code = stack[part, pl.ds(pl.multiple_of(row, SCALE_ROWS), rows), :]
            out[slot] = code.astype(jnp.int32).astype(jnp.float32) * column

        return carry

    lax.fori_loop(0, slots, one_slot, 0)


def per_device(z_count, y_count, x_count, core_count, snapshots, tile_table):
    components, block_size, cells_dev = snapshots.shape
    block_count = z_count * y_count
    space_count = x_count * core_count
    rows_dev = block_size // space_count
    scale_factor = 1.0 / math.sqrt(components * cells_dev * space_count)
    z, y, x, core = (lax.axis_index(name) for name in ("z", "y", "x", "core"))
    low_bit = z & 1
    cells = cells_dev // z_count

    def swap(value, axis, bits):
        size = lax.axis_size(axis)
        return lax.ppermute(value, axis, [(i, i ^ bits) for i in range(size)])

    lists = tile_lists(block_count)
    quarter = lists.shape[2]
    sizes = group_sizes(quarter)
    starts = np.cumsum([0] + sizes)
    ordered = np.stack(
        [
            np.concatenate(
                [
                    lists[of_y, of_bit ^ flip, start : start + size].reshape(-1)
                    for start, size in zip(starts, sizes)
                    for flip in range(2)
                ]
            )
            for of_y in range(2)
            for of_bit in range(2)
        ]
    ).astype(np.int32)
    pairs = lax.dynamic_index_in_dim(jnp.asarray(ordered), y * 2 + low_bit, 0, keepdims=False)
    scalars = jnp.concatenate([jnp.stack([z, y, x, core]).astype(jnp.int32), pairs])

    def part(step, values):
        return lax.dynamic_slice_in_dim(values, (z ^ step) * cells, cells, 2)

    cut = {step: part(step, snapshots) for step in range(1, z_count, 2)}
    again = lax.optimization_barrier((snapshots, *cut.values()))[0]
    cut.update({step: part(step, again) for step in range(0, z_count, 2)})
    head = (2 * components) // 3
    sent = [(1, 0, cut[1][:head]), (z_count - 1, 0, cut[z_count - 1]), (1, head, cut[1][head:])]
    sent += [(step, 0, cut[step]) for step in range(2, z_count - 1)]
    near = 3
    pieces, over_y, earlier = {(0, 0): cut[0]}, {}, []

    def arrived(value):
        value, *_ = lax.optimization_barrier((value, *earlier))
        earlier[:] = [
            pl.pallas_call(
                copy_kernel,
                out_shape=jax.ShapeDtypeStruct(value.shape, value.dtype),
                in_specs=[pl.BlockSpec(memory_space=pltpu.VMEM)],
                out_specs=pl.BlockSpec(memory_space=pltpu.VMEM),
                compiler_params=pltpu.CompilerParams(vmem_limit_bytes=VMEM_LIMIT),
                cost_estimate=pl.CostEstimate(flops=0, bytes_accessed=0, transcendentals=0),
                name="arrived",
            )(value)
        ]
        return earlier[0]

    over_y[0, 0] = swap(cut[0], "y", 1)
    early = {1: [(0, 0)], near: [(1, 0), (1, head)]}
    for index, (step, at, value) in enumerate(sent):
        for key in early.get(index, []):
            over_y[key] = arrived(over_y[key])
        pieces[step, at] = arrived(swap(value, "z", step))
        over_y[step, at] = swap(pieces[step, at], "y", 1)
    layout = [(step, 0, component) for step, component in pieces]
    layout += [(step, 1, component) for step, component in pieces]
    chunks = list(pieces.values()) + [over_y[key] for key in pieces]

    def sums_shape(groups):
        count = sum(sizes[index] for index in groups)
        return jax.ShapeDtypeStruct((2 * x_count, count, rows_dev, block_size), jnp.float32)

    def call(kernel, size, out_shape, operands, name):
        vmem = pl.BlockSpec(memory_space=pltpu.VMEM)
        return pl.pallas_call(
            kernel,
            out_shape=out_shape,
            in_specs=[pl.BlockSpec(memory_space=pltpu.SMEM)] + [vmem] * len(operands),
            out_specs=[vmem] * len(out_shape),
            compiler_params=pltpu.CompilerParams(vmem_limit_bytes=VMEM_LIMIT),
            cost_estimate=pl.CostEstimate(
                flops=4 * size * block_size * block_size * components * cells,
                bytes_accessed=0,
                transcendentals=0,
            ),
            name=name,
        )(scalars, *operands)

    blocks_shape = jax.ShapeDtypeStruct(
        (block_count, block_size, components * cells), jnp.bfloat16
    )
    counts = [sum(sizes[index] for index in groups) for groups in CALLS]
    blocks, *sums = call(
        functools.partial(first_kernel, layout, 4, sizes),
        counts[0],
        [blocks_shape] + [sums_shape(CALLS[0])] * 2,
        chunks,
        "tiles_first",
    )
    sums += call(
        functools.partial(second_kernel, 4 + 4 * counts[0], sizes),
        counts[1],
        [sums_shape(CALLS[1])] * 2,
        [blocks],
        "tiles_second",
    )

    last = []

    def step_call(kernel, out_shape, *operands, name):
        operands = lax.optimization_barrier((*operands, *last))[: len(operands)]
        vmem = pl.BlockSpec(memory_space=pltpu.VMEM)
        outs = pl.pallas_call(
            kernel,
            out_shape=out_shape,
            in_specs=[vmem] * len(operands),
            out_specs=[vmem] * len(out_shape),
            compiler_params=pltpu.CompilerParams(vmem_limit_bytes=VMEM_LIMIT),
            cost_estimate=pl.CostEstimate(
                flops=operands[0].size, bytes_accessed=0, transcendentals=0
            ),
            name=name,
        )(*operands)
        last[:] = outs[:1]
        return outs

    def float_shape(*shape):
        return jax.ShapeDtypeStruct((*shape, rows_dev, block_size), jnp.float32)

    def split_sum(shape, left, right, name):
        shapes = [float_shape(*shape[1:])] * shape[0]
        mine, *away = step_call(split_sum_kernel, shapes, left, right, name=name)
        return mine, away

    def plain_sum(left, right, name):
        shape = jax.ShapeDtypeStruct(left.shape, left.dtype)
        return step_call(sum_kernel, [shape], left, right, name=name)[0]

    def over_x(away):
        return [swap(value, "x", step + 1) for step, value in enumerate(away)]

    def over_high(mine):
        bits = 2
        while 2 * bits < z_count:
            mine = plain_sum(mine, swap(mine, "z", bits), "sum_z")
            bits *= 2
        return mine, swap(mine, "z", bits)

    def sum_core(which):
        keep, send = sums[2 * which : 2 * which + 2]
        send = swap(send, "core", 1)
        cuts, shapes, offset = [], [], 0
        for index in CALLS[which]:
            block = x_count if index in LOW_FIRST else 2
            cuts.append((offset, sizes[index], block))
            shapes += [float_shape(block, sizes[index])] * (2 * x_count // block)
            offset += sizes[index]
        outs = list(
            step_call(
                functools.partial(core_sum_kernel, cuts), shapes, keep, send, name="sum_core"
            )
        )
        for index, (_, _, block) in zip(CALLS[which], cuts):
            count = 2 * x_count // block
            (mine, *away), outs = outs[:count], outs[count:]
            if index in LOW_FIRST:
                state[index] = mine, swap(away[0], "z", 1)
                continue
            if which > 0:
                away = lax.optimization_barrier((*away, *state[0][1]))[: len(away)]
            state[index] = mine, over_x(away)

    def sum_x(index, mine, arrived):
        for value in arrived[:-1]:
            mine = plain_sum(mine, value, "sum_x")
        if index in LOW_FIRST:
            return over_high(plain_sum(mine, arrived[-1], "sum_x"))
        mine, away = split_sum((2, sizes[index]), mine, arrived[-1], "sum_x")
        return mine, swap(away[0], "z", 1)

    def sum_low(index, mine, arrived):
        if index in LOW_FIRST:
            mine, away = split_sum((x_count, sizes[index]), mine, arrived, "sum_z")
            return mine, over_x(away)
        return over_high(plain_sum(mine, arrived, "sum_z"))

    def to_owners(value):
        both = [(i, i ^ (y_count + 1)) for i in range(block_count)]
        over_both = lax.ppermute(value, ("z", "y"), both)
        return [value, swap(value, "z", 1), swap(value, "y", 1), over_both]

    table = tile_table[0]
    row_block = table[:, 0]
    col_block = table[:, 1]
    first = jnp.maximum(row_block, 0)
    second = jnp.maximum(col_block, 0)
    pair = first * block_count - (first * (first - 1)) // 2 + second - first
    of_list, slot = pair // quarter, pair % quarter
    off = ((of_list // 2) ^ y) * 2 + ((of_list % 2) ^ low_bit)
    in_batch, row, lane, exponent_row, steps_row = (jnp.zeros_like(slot) for _ in range(5))
    for index, batch in enumerate(BATCHES):
        start, end = int(starts[batch[0]]), int(starts[batch[-1] + 1])
        inside = (slot >= start) & (slot < end)
        header_rows = -(-(end - start) * rows_dev // block_size)
        at = (slot - start) * rows_dev
        top = off * SCALE_ROWS + at // block_size
        in_batch = jnp.where(inside, index, in_batch)
        row = jnp.where(inside, SCALE_ROWS + at, row)
        lane = jnp.where(inside, at % block_size, lane)
        exponent_row = jnp.where(inside, top, exponent_row)
        steps_row = jnp.where(inside, top + header_rows, steps_row)
    in_batch = jnp.where(row_block >= 0, in_batch, -1)
    places = jnp.concatenate([in_batch, off, row, lane, exponent_row, steps_row])

    parts, result = [], []
    state = {}
    for stage, which in ORDER:
        if stage == "core":
            sum_core(which)
        elif stage == "x":
            state[which] = sum_x(which, *state[which])
        elif stage == "low":
            state[which] = sum_low(which, *state[which])
        elif stage == "high":
            state[which] = [plain_sum(*state[which], "sum_high")]
        elif stage == "place":
            four = parts[4 * which : 4 * which + 4]
            operands = lax.optimization_barrier((places, *four, *result, *last))[:-1]
            vmem = pl.BlockSpec(memory_space=pltpu.VMEM)
            result = [
                pl.pallas_call(
                    functools.partial(
                        place_kernel, scale_factor / (CODE_TOP * SCALE_STEPS), which
                    ),
                    out_shape=float_shape(table.shape[0]),
                    in_specs=[pl.BlockSpec(memory_space=pltpu.SMEM)]
                    + [vmem] * (len(operands) - 1),
                    out_specs=vmem,
                    scratch_shapes=[
                        pltpu.VMEM((4 * SCALE_ROWS, block_size), jnp.float32),
                        pltpu.VMEM((4, *four[0].shape), jnp.int16),
                    ],
                    compiler_params=pltpu.CompilerParams(vmem_limit_bytes=VMEM_LIMIT),
                    cost_estimate=pl.CostEstimate(
                        flops=table.shape[0] * rows_dev * block_size,
                        bytes_accessed=0,
                        transcendentals=0,
                    ),
                    name="place_tiles",
                )(*operands)
            ]
        else:
            counts = [sizes[index] for index in which]
            shape = (SCALE_ROWS + sum(counts) * rows_dev, block_size)
            kernel = functools.partial(code_kernel, counts, [len(state[i]) for i in which])
            operands = [value for index in which for value in state[index]]
            (code,) = step_call(
                kernel, [jax.ShapeDtypeStruct(shape, jnp.int16)], *operands, name="finish"
            )
            parts += to_owners(code)

    return result[0][None]


def solution(mesh):
    tm, space = mesh.shape["tm"], mesh.shape["space"]
    sizes = (tm // 2, 2, space // 2, 2)
    grid = Mesh(mesh.devices.reshape(sizes), ("z", "y", "x", "core"))
    in_specs = (P(None, ("z", "y"), ("x", "core")), P(("z", "y"), None, None))
    out_specs = P(("z", "y"), None, ("x", "core"), None)
    return jax.shard_map(
        functools.partial(per_device, *sizes),
        mesh=grid,
        in_specs=in_specs,
        out_specs=out_specs,
        check_vma=False,
    )
```

```python
import functools
import math

import jax
import jax.numpy as jnp
import numpy as np
from jax import lax
from jax.experimental import pallas as pl
from jax.experimental.pallas import tpu as pltpu
from jax.sharding import Mesh, PartitionSpec as P

UNROLL = 4
VMEM_LIMIT = 24 * 2**20
GROUPS = 3
BATCHES = ((0, 1), (2,))
CALLS = ((0, 1), (2,))
LOW_FIRST = (0,)
ORDER = (
    ("core", 0), ("core", 1), ("x", 1), ("low", 0), ("low", 1), ("x", 2),
    ("high", 1), ("low", 2), ("finish", BATCHES[0]), ("finish", BATCHES[1]),
    ("place", 0), ("place", 1),
)
CODE_TOP = 32767.0
SCALE_ROWS = 16
SCALE_STEPS = 8192.0


def tile_lists(block_count):
    rows, cols = np.triu_indices(block_count)
    return np.stack([rows, cols], axis=1).reshape(2, 2, -1, 2)


def group_sizes(quarter):
    return [len(piece) for piece in np.array_split(np.arange(quarter), GROUPS)]


def multiply_tiles(scalars, first_pair, blocks, keep_ref, send_ref, offset, size, low_first):
    x, core = scalars[2], scalars[3]
    rows_dev = keep_ref.shape[2]
    part_count = blocks.shape[1] // rows_dev

    def one_slot(slot, carry):
        for low in range(2):
            where = first_pair + 2 * (low * size + slot)
            tile = lax.dot_general(
                blocks[scalars[where]],
                blocks[scalars[where + 1]],
                (((1,), (1,)), ((), ())),
                preferred_element_type=jnp.float32,
            )
            parts = [tile[part * rows_dev : (part + 1) * rows_dev] for part in range(part_count)]
            for step in range(part_count // 2):
                even, odd = parts[2 * step], parts[2 * step + 1]
                target = x ^ step
                place = low * (part_count // 2) + target if low_first else 2 * target + low
                keep_ref[place, offset + slot] = jnp.where(core == 0, even, odd)
                send_ref[place, offset + slot] = jnp.where(core == 0, odd, even)
        return carry

    lax.fori_loop(0, size, one_slot, 0, unroll=size <= UNROLL)


def multiply_groups(scalars, first_pair, sizes, blocks, groups, outs):
    offset = 0
    for index in groups:
        multiply_tiles(
            scalars, first_pair, blocks, *outs, offset, sizes[index], index in LOW_FIRST
        )
        first_pair += 4 * sizes[index]
        offset += sizes[index]


def first_kernel(layout, first_pair, sizes, scalars, *refs):
    pieces = refs[: len(layout)]
    blocks = refs[len(layout)]
    z, y = scalars[0], scalars[1]
    for (step, other, component), piece in zip(layout, pieces):
        block = (z ^ step) * 2 + (y ^ other)
        cells = piece.shape[2]
        for index in range(piece.shape[0]):
            start = (component + index) * cells
            blocks[block, :, start : start + cells] = piece[index]
    multiply_groups(scalars, first_pair, sizes, blocks, CALLS[0], refs[len(layout) + 1 :])


def second_kernel(first_pair, sizes, scalars, blocks, *outs):
    multiply_groups(scalars, first_pair, sizes, blocks, CALLS[1], outs)


def core_sum_kernel(cuts, keep, send, *outs):
    outs = list(outs)
    for offset, size, block in cuts:
        for start in range(0, keep.shape[0], block):
            place = (slice(start, start + block), slice(offset, offset + size))
            outs.pop(0)[...] = keep[place] + send[place]


def low_first_kernel(left, right, *refs):
    count = len(refs) // 2
    others, mine, merged = refs[:count], refs[count], refs[count + 1 :]
    size = mine.shape[0]
    mine[...] = left[0] + right[0]
    for step, (other, out) in enumerate(zip(others, merged)):
        out[:size] = left[step + 1] + right[step + 1]
        for index in range(other.shape[0]):
            start = size + index * other.shape[1]
            out[start : start + other.shape[1]] = other[index]


def merged_x_kernel(first, second, *refs):
    arrived, (out, mine, away) = refs[:-3], refs[-3:]
    size, other = first.shape[0], second.shape[1]

    def total(value, start):
        return sum((ref[start : start + value.shape[0]] for ref in arrived), value)

    out[...] = total(first[...], 0)
    mine[...] = total(second[0], size)
    away[...] = total(second[1], size + other)


def split_sum_kernel(left, right, *outs):
    for index, out in enumerate(outs):
        out[...] = left[index] + right[index]


def sum_kernel(left, right, out):
    out[...] = left[...] + right[...]


def code_kernel(sizes, pairs, *refs):
    code = refs[-1]
    refs = list(refs[:-1])
    rows, columns = refs[0].shape[1:]
    header_rows = -(-sum(sizes) * rows // columns)
    row_of = lax.broadcasted_iota(jnp.int32, (rows, columns), 0)
    lane_of = lax.broadcasted_iota(jnp.int32, (rows, columns), 1)
    place = lax.broadcasted_iota(jnp.int32, (SCALE_ROWS, columns), 0)
    header = jnp.zeros((SCALE_ROWS, columns), jnp.float32)
    slot = 0
    for size, pair in zip(sizes, pairs):
        terms = [refs.pop(0) for _ in range(pair)]
        for index in range(size):
            total = sum((term[index] for term in terms[1:]), terms[0][index])
            top = jnp.max(jnp.abs(total), axis=1, keepdims=True)
            filled = top > 0
            exponent = jnp.log(jnp.where(filled, top, 1.0)) * (1.0 / math.log(2.0))
            exponent = jnp.clip(jnp.floor(exponent), -120.0, 120.0)
            power = jnp.exp(exponent * math.log(2.0))
            steps = jnp.where(filled, jnp.ceil(top / power * SCALE_STEPS), 0.0)
            scale = steps * power * (1.0 / SCALE_STEPS)
            factor = jnp.where(filled, CODE_TOP / jnp.where(filled, scale, 1.0), 0.0)
            rounded = jnp.clip(jnp.round(total * factor), -CODE_TOP, CODE_TOP)
            start = SCALE_ROWS + slot * rows
            code[start : start + rows, :] = rounded.astype(jnp.int32).astype(jnp.int16)
            row, lane = divmod(slot * rows, columns)
            diagonal = lane_of == row_of + lane
            for at, value in ((row, exponent), (row + header_rows, steps)):
                across = jnp.sum(jnp.where(diagonal, value, 0.0), axis=0, keepdims=True)
                header += jnp.where(place == at, across, 0.0)
            slot += 1
    code[:SCALE_ROWS, :] = header.astype(jnp.int32).astype(jnp.int16)


def place_kernel(factor, batch, scalars, *refs):
    parts, before = refs[:4], refs[4:-3]
    out, headers, stack = refs[-3:]
    slots, rows, columns = out.shape
    for index, part in enumerate(parts):
        start = index * SCALE_ROWS
        headers[start : start + SCALE_ROWS, :] = (
            part[:SCALE_ROWS, :].astype(jnp.int32).astype(jnp.float32)
        )
        stack[index] = part[...]
    out[...] = before[0][...] if before else jnp.zeros_like(out)
    row_of = lax.broadcasted_iota(jnp.int32, (rows, columns), 0)
    lane_of = lax.broadcasted_iota(jnp.int32, (rows, columns), 1)

    def one_slot(slot, carry):
        batch_of, part, row, lane, exponent_row, steps_row = (
            scalars[kind * slots + slot] for kind in range(6)
        )

        @pl.when(batch_of == batch)
        def _():
            exponent = headers[pl.ds(exponent_row, 1), :]
            steps = headers[pl.ds(steps_row, 1), :]
            scale = steps * jnp.exp(exponent * math.log(2.0)) * factor
            column = jnp.sum(
                jnp.where(lane_of == row_of + lane, scale, 0.0), axis=1, keepdims=True
            )
            code = stack[part, pl.ds(pl.multiple_of(row, SCALE_ROWS), rows), :]
            out[slot] = code.astype(jnp.int32).astype(jnp.float32) * column

        return carry

    lax.fori_loop(0, slots, one_slot, 0)


def per_device(z_count, y_count, x_count, core_count, snapshots, tile_table):
    components, block_size, cells_dev = snapshots.shape
    block_count = z_count * y_count
    space_count = x_count * core_count
    rows_dev = block_size // space_count
    scale_factor = 1.0 / math.sqrt(components * cells_dev * space_count)
    z, y, x, core = (lax.axis_index(name) for name in ("z", "y", "x", "core"))
    low_bit = z & 1
    cells = cells_dev // z_count

    def swap(value, axis, bits):
        size = lax.axis_size(axis)
        return lax.ppermute(value, axis, [(i, i ^ bits) for i in range(size)])

    lists = tile_lists(block_count)
    quarter = lists.shape[2]
    sizes = group_sizes(quarter)
    starts = np.cumsum([0] + sizes)
    ordered = np.stack(
        [
            np.concatenate(
                [
                    lists[of_y, of_bit ^ flip, start : start + size].reshape(-1)
                    for start, size in zip(starts, sizes)
                    for flip in range(2)
                ]
            )
            for of_y in range(2)
            for of_bit in range(2)
        ]
    ).astype(np.int32)
    pairs = lax.dynamic_index_in_dim(jnp.asarray(ordered), y * 2 + low_bit, 0, keepdims=False)
    scalars = jnp.concatenate([jnp.stack([z, y, x, core]).astype(jnp.int32), pairs])

    def part(step, values):
        return lax.dynamic_slice_in_dim(values, (z ^ step) * cells, cells, 2)

    cut = {step: part(step, snapshots) for step in range(1, z_count, 2)}
    again = lax.optimization_barrier((snapshots, *cut.values()))[0]
    cut.update({step: part(step, again) for step in range(0, z_count, 2)})
    pieces = {(0, 0): cut[0]}
    for step in range(1, z_count):
        pieces[step, 0] = swap(cut[step], "z", step)
    layout = [(step, 0, component) for step, component in pieces]
    layout += [(step, 1, component) for step, component in pieces]
    chunks = list(pieces.values()) + [swap(piece, "y", 1) for piece in pieces.values()]

    def sums_shape(groups):
        count = sum(sizes[index] for index in groups)
        return jax.ShapeDtypeStruct((2 * x_count, count, rows_dev, block_size), jnp.float32)

    def call(kernel, size, out_shape, operands, name):
        vmem = pl.BlockSpec(memory_space=pltpu.VMEM)
        return pl.pallas_call(
            kernel,
            out_shape=out_shape,
            in_specs=[pl.BlockSpec(memory_space=pltpu.SMEM)] + [vmem] * len(operands),
            out_specs=[vmem] * len(out_shape),
            compiler_params=pltpu.CompilerParams(vmem_limit_bytes=VMEM_LIMIT),
            cost_estimate=pl.CostEstimate(
                flops=4 * size * block_size * block_size * components * cells,
                bytes_accessed=0,
                transcendentals=0,
            ),
            name=name,
        )(scalars, *operands)

    blocks_shape = jax.ShapeDtypeStruct(
        (block_count, block_size, components * cells), jnp.bfloat16
    )
    counts = [sum(sizes[index] for index in groups) for groups in CALLS]
    blocks, *sums = call(
        functools.partial(first_kernel, layout, 4, sizes),
        counts[0],
        [blocks_shape] + [sums_shape(CALLS[0])] * 2,
        chunks,
        "tiles_first",
    )
    sums += call(
        functools.partial(second_kernel, 4 + 4 * counts[0], sizes),
        counts[1],
        [sums_shape(CALLS[1])] * 2,
        [blocks],
        "tiles_second",
    )

    last = []

    def step_call(kernel, out_shape, *operands, name):
        operands = lax.optimization_barrier((*operands, *last))[: len(operands)]
        vmem = pl.BlockSpec(memory_space=pltpu.VMEM)
        outs = pl.pallas_call(
            kernel,
            out_shape=out_shape,
            in_specs=[vmem] * len(operands),
            out_specs=[vmem] * len(out_shape),
            compiler_params=pltpu.CompilerParams(vmem_limit_bytes=VMEM_LIMIT),
            cost_estimate=pl.CostEstimate(
                flops=operands[0].size, bytes_accessed=0, transcendentals=0
            ),
            name=name,
        )(*operands)
        last[:] = outs[:1]
        return outs

    def float_shape(*shape):
        return jax.ShapeDtypeStruct((*shape, rows_dev, block_size), jnp.float32)

    def split_sum(shape, left, right, name):
        shapes = [float_shape(*shape[1:])] * shape[0]
        mine, *away = step_call(split_sum_kernel, shapes, left, right, name=name)
        return mine, away

    def plain_sum(left, right, name):
        shape = jax.ShapeDtypeStruct(left.shape, left.dtype)
        return step_call(sum_kernel, [shape], left, right, name=name)[0]

    def over_x(away):
        return [swap(value, "x", step + 1) for step, value in enumerate(away)]

    def over_high(mine):
        bits = 2
        while 2 * bits < z_count:
            mine = plain_sum(mine, swap(mine, "z", bits), "sum_z")
            bits *= 2
        return mine, swap(mine, "z", bits)

    def sum_core(which):
        keep, send = sums[2 * which : 2 * which + 2]
        send = swap(send, "core", 1)
        cuts, shapes, offset = [], [], 0
        for index in CALLS[which]:
            block = x_count if index in LOW_FIRST else 2
            cuts.append((offset, sizes[index], block))
            shapes += [float_shape(block, sizes[index])] * (2 * x_count // block)
            offset += sizes[index]
        outs = list(
            step_call(
                functools.partial(core_sum_kernel, cuts), shapes, keep, send, name="sum_core"
            )
        )
        for index, (_, _, block) in zip(CALLS[which], cuts):
            count = 2 * x_count // block
            (mine, *away), outs = outs[:count], outs[count:]
            if index in LOW_FIRST:
                state[index] = mine, swap(away[0], "z", 1)
                continue
            state[index] = mine, away if which > 0 else over_x(away)

    def sum_x(index, mine, arrived):
        if index == 2:
            shapes = [float_shape(sizes[0])] + [float_shape(sizes[2])] * 2
            first, mine, away = step_call(
                merged_x_kernel, shapes, state[0][0], mine, *arrived, name="sum_x"
            )
            state[0] = over_high(first)
            return mine, swap(away, "z", 1)
        for value in arrived[:-1]:
            mine = plain_sum(mine, value, "sum_x")
        mine, away = split_sum((2, sizes[index]), mine, arrived[-1], "sum_x")
        return mine, swap(away[0], "z", 1)

    def sum_low(index, mine, arrived):
        if index in LOW_FIRST:
            others = state[2][1]
            merged = float_shape(sizes[0] + 2 * sizes[2])
            shapes = [float_shape(sizes[0])] + [merged] * (x_count - 1)
            mine, *away = step_call(
                low_first_kernel, shapes, mine, arrived, *others, name="sum_z"
            )
            state[2] = state[2][0], over_x(away)
            return (mine,)
        return over_high(plain_sum(mine, arrived, "sum_z"))

    def to_owners(value):
        both = [(i, i ^ (y_count + 1)) for i in range(block_count)]
        over_both = lax.ppermute(value, ("z", "y"), both)
        return [value, swap(value, "z", 1), swap(value, "y", 1), over_both]

    table = tile_table[0]
    row_block = table[:, 0]
    col_block = table[:, 1]
    first = jnp.maximum(row_block, 0)
    second = jnp.maximum(col_block, 0)
    pair = first * block_count - (first * (first - 1)) // 2 + second - first
    of_list, slot = pair // quarter, pair % quarter
    off = ((of_list // 2) ^ y) * 2 + ((of_list % 2) ^ low_bit)
    in_batch, row, lane, exponent_row, steps_row = (jnp.zeros_like(slot) for _ in range(5))
    for index, batch in enumerate(BATCHES):
        start, end = int(starts[batch[0]]), int(starts[batch[-1] + 1])
        inside = (slot >= start) & (slot < end)
        header_rows = -(-(end - start) * rows_dev // block_size)
        at = (slot - start) * rows_dev
        top = off * SCALE_ROWS + at // block_size
        in_batch = jnp.where(inside, index, in_batch)
        row = jnp.where(inside, SCALE_ROWS + at, row)
        lane = jnp.where(inside, at % block_size, lane)
        exponent_row = jnp.where(inside, top, exponent_row)
        steps_row = jnp.where(inside, top + header_rows, steps_row)
    in_batch = jnp.where(row_block >= 0, in_batch, -1)
    places = jnp.concatenate([in_batch, off, row, lane, exponent_row, steps_row])

    parts, result = [], []
    state = {}
    for stage, which in ORDER:
        if stage == "core":
            sum_core(which)
        elif stage == "x":
            state[which] = sum_x(which, *state[which])
        elif stage == "low":
            state[which] = sum_low(which, *state[which])
        elif stage == "high":
            state[which] = [plain_sum(*state[which], "sum_high")]
        elif stage == "place":
            four = parts[4 * which : 4 * which + 4]
            operands = lax.optimization_barrier((places, *four, *result, *last))[:-1]
            vmem = pl.BlockSpec(memory_space=pltpu.VMEM)
            result = [
                pl.pallas_call(
                    functools.partial(
                        place_kernel, scale_factor / (CODE_TOP * SCALE_STEPS), which
                    ),
                    out_shape=float_shape(table.shape[0]),
                    in_specs=[pl.BlockSpec(memory_space=pltpu.SMEM)]
                    + [vmem] * (len(operands) - 1),
                    out_specs=vmem,
                    scratch_shapes=[
                        pltpu.VMEM((4 * SCALE_ROWS, block_size), jnp.float32),
                        pltpu.VMEM((4, *four[0].shape), jnp.int16),
                    ],
                    compiler_params=pltpu.CompilerParams(vmem_limit_bytes=VMEM_LIMIT),
                    cost_estimate=pl.CostEstimate(
                        flops=table.shape[0] * rows_dev * block_size,
                        bytes_accessed=0,
                        transcendentals=0,
                    ),
                    name="place_tiles",
                )(*operands)
            ]
        else:
            counts = [sizes[index] for index in which]
            shape = (SCALE_ROWS + sum(counts) * rows_dev, block_size)
            kernel = functools.partial(code_kernel, counts, [len(state[i]) for i in which])
            operands = [value for index in which for value in state[index]]
            (code,) = step_call(
                kernel, [jax.ShapeDtypeStruct(shape, jnp.int16)], *operands, name="finish"
            )
            parts += to_owners(code)

    return result[0][None]


def solution(mesh):
    tm, space = mesh.shape["tm"], mesh.shape["space"]
    sizes = (tm // 2, 2, space // 2, 2)
    grid = Mesh(mesh.devices.reshape(sizes), ("z", "y", "x", "core"))
    in_specs = (P(None, ("z", "y"), ("x", "core")), P(("z", "y"), None, None))
    out_specs = P(("z", "y"), None, ("x", "core"), None)
    return jax.shard_map(
        functools.partial(per_device, *sizes),
        mesh=grid,
        in_specs=in_specs,
        out_specs=out_specs,
        check_vma=False,
    )
```

```python
import functools
import math

import jax
import jax.numpy as jnp
import numpy as np
from jax import lax
from jax.experimental import pallas as pl
from jax.experimental.pallas import tpu as pltpu
from jax.sharding import Mesh, PartitionSpec as P

UNROLL = 4
VMEM_LIMIT = 24 * 2**20
GROUPS = 3
BATCHES = ((0, 1), (2,))
CALLS = ((0, 1), (2,))
LOW_FIRST = (0,)
ORDER = (
    ("core", 0), ("core", 1), ("x", 1), ("low", 0), ("low", 1), ("x", 2),
    ("high", 1), ("low", 2), ("finish", BATCHES[0]), ("finish", BATCHES[1]),
    ("place", 0), ("place", 1),
)
CODE_TOP = 32767.0
SCALE_ROWS = 16
SCALE_STEPS = 8192.0


def tile_lists(block_count):
    rows, cols = np.triu_indices(block_count)
    return np.stack([rows, cols], axis=1).reshape(2, 2, -1, 2)


def group_sizes(quarter):
    sizes = [len(piece) for piece in np.array_split(np.arange(quarter), GROUPS)]
    return [sizes[0] + 1, *sizes[1:-1], sizes[-1] - 1]


def multiply_tiles(scalars, first_pair, blocks, keep_ref, send_ref, offset, size, low_first):
    x, core = scalars[2], scalars[3]
    rows_dev = keep_ref.shape[2]
    part_count = blocks.shape[1] // rows_dev

    def one_slot(slot, carry):
        for low in range(2):
            where = first_pair + 2 * (low * size + slot)
            tile = lax.dot_general(
                blocks[scalars[where]],
                blocks[scalars[where + 1]],
                (((1,), (1,)), ((), ())),
                preferred_element_type=jnp.float32,
            )
            parts = [tile[part * rows_dev : (part + 1) * rows_dev] for part in range(part_count)]
            for step in range(part_count // 2):
                even, odd = parts[2 * step], parts[2 * step + 1]
                target = x ^ step
                place = low * (part_count // 2) + target if low_first else 2 * target + low
                keep_ref[place, offset + slot] = jnp.where(core == 0, even, odd)
                send_ref[place, offset + slot] = jnp.where(core == 0, odd, even)
        return carry

    lax.fori_loop(0, size, one_slot, 0, unroll=size <= UNROLL)


def multiply_groups(scalars, first_pair, sizes, blocks, groups, outs):
    offset = 0
    for index in groups:
        multiply_tiles(
            scalars, first_pair, blocks, *outs, offset, sizes[index], index in LOW_FIRST
        )
        first_pair += 4 * sizes[index]
        offset += sizes[index]


def first_kernel(layout, first_pair, sizes, scalars, *refs):
    pieces = refs[: len(layout)]
    blocks = refs[len(layout)]
    z, y = scalars[0], scalars[1]
    for (step, other, component), piece in zip(layout, pieces):
        block = (z ^ step) * 2 + (y ^ other)
        cells = piece.shape[2]
        for index in range(piece.shape[0]):
            start = (component + index) * cells
            blocks[block, :, start : start + cells] = piece[index]
    multiply_groups(scalars, first_pair, sizes, blocks, CALLS[0], refs[len(layout) + 1 :])


def second_kernel(first_pair, sizes, scalars, blocks, *outs):
    multiply_groups(scalars, first_pair, sizes, blocks, CALLS[1], outs)


def core_sum_kernel(cuts, keep, send, *outs):
    outs = list(outs)
    for offset, size, block in cuts:
        for start in range(0, keep.shape[0], block):
            place = (slice(start, start + block), slice(offset, offset + size))
            outs.pop(0)[...] = keep[place] + send[place]


def low_first_kernel(left, right, *refs):
    count = len(refs) // 2
    others, mine, merged = refs[:count], refs[count], refs[count + 1 :]
    size = mine.shape[0]
    mine[...] = left[0] + right[0]
    for step, (other, out) in enumerate(zip(others, merged)):
        out[:size] = left[step + 1] + right[step + 1]
        for index in range(other.shape[0]):
            start = size + index * other.shape[1]
            out[start : start + other.shape[1]] = other[index]


def merged_x_kernel(first, second, *refs):
    arrived, (out, mine, away) = refs[:-3], refs[-3:]
    size, other = first.shape[0], second.shape[1]

    def total(value, start):
        return sum((ref[start : start + value.shape[0]] for ref in arrived), value)

    out[...] = total(first[...], 0)
    mine[...] = total(second[0], size)
    away[...] = total(second[1], size + other)


def split_sum_kernel(left, right, *outs):
    for index, out in enumerate(outs):
        out[...] = left[index] + right[index]


def sum_kernel(left, right, out):
    out[...] = left[...] + right[...]


def code_kernel(sizes, pairs, *refs):
    code = refs[-1]
    refs = list(refs[:-1])
    rows, columns = refs[0].shape[1:]
    header_rows = -(-sum(sizes) * rows // columns)
    row_of = lax.broadcasted_iota(jnp.int32, (rows, columns), 0)
    lane_of = lax.broadcasted_iota(jnp.int32, (rows, columns), 1)
    place = lax.broadcasted_iota(jnp.int32, (SCALE_ROWS, columns), 0)
    header = jnp.zeros((SCALE_ROWS, columns), jnp.float32)
    slot = 0
    for size, pair in zip(sizes, pairs):
        terms = [refs.pop(0) for _ in range(pair)]
        for index in range(size):
            total = sum((term[index] for term in terms[1:]), terms[0][index])
            top = jnp.max(jnp.abs(total), axis=1, keepdims=True)
            filled = top > 0
            exponent = jnp.log(jnp.where(filled, top, 1.0)) * (1.0 / math.log(2.0))
            exponent = jnp.clip(jnp.floor(exponent), -120.0, 120.0)
            power = jnp.exp(exponent * math.log(2.0))
            steps = jnp.where(filled, jnp.ceil(top / power * SCALE_STEPS), 0.0)
            scale = steps * power * (1.0 / SCALE_STEPS)
            factor = jnp.where(filled, CODE_TOP / jnp.where(filled, scale, 1.0), 0.0)
            rounded = jnp.clip(jnp.round(total * factor), -CODE_TOP, CODE_TOP)
            start = SCALE_ROWS + slot * rows
            code[start : start + rows, :] = rounded.astype(jnp.int32).astype(jnp.int16)
            row, lane = divmod(slot * rows, columns)
            diagonal = lane_of == row_of + lane
            for at, value in ((row, exponent), (row + header_rows, steps)):
                across = jnp.sum(jnp.where(diagonal, value, 0.0), axis=0, keepdims=True)
                header += jnp.where(place == at, across, 0.0)
            slot += 1
    code[:SCALE_ROWS, :] = header.astype(jnp.int32).astype(jnp.int16)


def place_kernel(factor, batch, scalars, *refs):
    parts, before = refs[:4], refs[4:-3]
    out, headers, stack = refs[-3:]
    slots, rows, columns = out.shape
    for index, part in enumerate(parts):
        start = index * SCALE_ROWS
        headers[start : start + SCALE_ROWS, :] = (
            part[:SCALE_ROWS, :].astype(jnp.int32).astype(jnp.float32)
        )
        stack[index] = part[...]
    out[...] = before[0][...] if before else jnp.zeros_like(out)
    row_of = lax.broadcasted_iota(jnp.int32, (rows, columns), 0)
    lane_of = lax.broadcasted_iota(jnp.int32, (rows, columns), 1)

    def one_slot(slot, carry):
        batch_of, part, row, lane, exponent_row, steps_row = (
            scalars[kind * slots + slot] for kind in range(6)
        )

        @pl.when(batch_of == batch)
        def _():
            exponent = headers[pl.ds(exponent_row, 1), :]
            steps = headers[pl.ds(steps_row, 1), :]
            scale = steps * jnp.exp(exponent * math.log(2.0)) * factor
            column = jnp.sum(
                jnp.where(lane_of == row_of + lane, scale, 0.0), axis=1, keepdims=True
            )
            code = stack[part, pl.ds(pl.multiple_of(row, SCALE_ROWS), rows), :]
            out[slot] = code.astype(jnp.int32).astype(jnp.float32) * column

        return carry

    lax.fori_loop(0, slots, one_slot, 0)


def per_device(z_count, y_count, x_count, core_count, snapshots, tile_table):
    components, block_size, cells_dev = snapshots.shape
    block_count = z_count * y_count
    space_count = x_count * core_count
    rows_dev = block_size // space_count
    scale_factor = 1.0 / math.sqrt(components * cells_dev * space_count)
    z, y, x, core = (lax.axis_index(name) for name in ("z", "y", "x", "core"))
    low_bit = z & 1
    cells = cells_dev // z_count

    def swap(value, axis, bits):
        size = lax.axis_size(axis)
        return lax.ppermute(value, axis, [(i, i ^ bits) for i in range(size)])

    lists = tile_lists(block_count)
    quarter = lists.shape[2]
    sizes = group_sizes(quarter)
    starts = np.cumsum([0] + sizes)
    ordered = np.stack(
        [
            np.concatenate(
                [
                    lists[of_y, of_bit ^ flip, start : start + size].reshape(-1)
                    for start, size in zip(starts, sizes)
                    for flip in range(2)
                ]
            )
            for of_y in range(2)
            for of_bit in range(2)
        ]
    ).astype(np.int32)
    pairs = lax.dynamic_index_in_dim(jnp.asarray(ordered), y * 2 + low_bit, 0, keepdims=False)
    scalars = jnp.concatenate([jnp.stack([z, y, x, core]).astype(jnp.int32), pairs])

    def part(step, values):
        return lax.dynamic_slice_in_dim(values, (z ^ step) * cells, cells, 2)

    cut = {step: part(step, snapshots) for step in range(1, z_count, 2)}
    again = lax.optimization_barrier((snapshots, *cut.values()))[0]
    cut.update({step: part(step, again) for step in range(0, z_count, 2)})
    pieces = {(0, 0): cut[0]}
    for step in range(1, z_count):
        pieces[step, 0] = swap(cut[step], "z", step)
    layout = [(step, 0, component) for step, component in pieces]
    layout += [(step, 1, component) for step, component in pieces]
    chunks = list(pieces.values()) + [swap(piece, "y", 1) for piece in pieces.values()]

    def sums_shape(groups):
        count = sum(sizes[index] for index in groups)
        return jax.ShapeDtypeStruct((2 * x_count, count, rows_dev, block_size), jnp.float32)

    def call(kernel, size, out_shape, operands, name):
        vmem = pl.BlockSpec(memory_space=pltpu.VMEM)
        return pl.pallas_call(
            kernel,
            out_shape=out_shape,
            in_specs=[pl.BlockSpec(memory_space=pltpu.SMEM)] + [vmem] * len(operands),
            out_specs=[vmem] * len(out_shape),
            compiler_params=pltpu.CompilerParams(vmem_limit_bytes=VMEM_LIMIT),
            cost_estimate=pl.CostEstimate(
                flops=4 * size * block_size * block_size * components * cells,
                bytes_accessed=0,
                transcendentals=0,
            ),
            name=name,
        )(scalars, *operands)

    blocks_shape = jax.ShapeDtypeStruct(
        (block_count, block_size, components * cells), jnp.bfloat16
    )
    counts = [sum(sizes[index] for index in groups) for groups in CALLS]
    blocks, *sums = call(
        functools.partial(first_kernel, layout, 4, sizes),
        counts[0],
        [blocks_shape] + [sums_shape(CALLS[0])] * 2,
        chunks,
        "tiles_first",
    )
    sums += call(
        functools.partial(second_kernel, 4 + 4 * counts[0], sizes),
        counts[1],
        [sums_shape(CALLS[1])] * 2,
        [blocks],
        "tiles_second",
    )

    last = []

    def step_call(kernel, out_shape, *operands, name):
        operands = lax.optimization_barrier((*operands, *last))[: len(operands)]
        vmem = pl.BlockSpec(memory_space=pltpu.VMEM)
        outs = pl.pallas_call(
            kernel,
            out_shape=out_shape,
            in_specs=[vmem] * len(operands),
            out_specs=[vmem] * len(out_shape),
            compiler_params=pltpu.CompilerParams(vmem_limit_bytes=VMEM_LIMIT),
            cost_estimate=pl.CostEstimate(
                flops=operands[0].size, bytes_accessed=0, transcendentals=0
            ),
            name=name,
        )(*operands)
        last[:] = outs[:1]
        return outs

    def float_shape(*shape):
        return jax.ShapeDtypeStruct((*shape, rows_dev, block_size), jnp.float32)

    def split_sum(shape, left, right, name):
        shapes = [float_shape(*shape[1:])] * shape[0]
        mine, *away = step_call(split_sum_kernel, shapes, left, right, name=name)
        return mine, away

    def plain_sum(left, right, name):
        shape = jax.ShapeDtypeStruct(left.shape, left.dtype)
        return step_call(sum_kernel, [shape], left, right, name=name)[0]

    def over_x(away):
        return [swap(value, "x", step + 1) for step, value in enumerate(away)]

    def over_high(mine):
        bits = 2
        while 2 * bits < z_count:
            mine = plain_sum(mine, swap(mine, "z", bits), "sum_z")
            bits *= 2
        return mine, swap(mine, "z", bits)

    def sum_core(which):
        keep, send = sums[2 * which : 2 * which + 2]
        send = swap(send, "core", 1)
        cuts, shapes, offset = [], [], 0
        for index in CALLS[which]:
            block = x_count if index in LOW_FIRST else 2
            cuts.append((offset, sizes[index], block))
            shapes += [float_shape(block, sizes[index])] * (2 * x_count // block)
            offset += sizes[index]
        outs = list(
            step_call(
                functools.partial(core_sum_kernel, cuts), shapes, keep, send, name="sum_core"
            )
        )
        for index, (_, _, block) in zip(CALLS[which], cuts):
            count = 2 * x_count // block
            (mine, *away), outs = outs[:count], outs[count:]
            if index in LOW_FIRST:
                state[index] = mine, swap(away[0], "z", 1)
                continue
            state[index] = mine, away if which > 0 else over_x(away)

    def sum_x(index, mine, arrived):
        if index == 2:
            shapes = [float_shape(sizes[0])] + [float_shape(sizes[2])] * 2
            first, mine, away = step_call(
                merged_x_kernel, shapes, state[0][0], mine, *arrived, name="sum_x"
            )
            state[0] = over_high(first)
            return mine, swap(away, "z", 1)
        for value in arrived[:-1]:
            mine = plain_sum(mine, value, "sum_x")
        mine, away = split_sum((2, sizes[index]), mine, arrived[-1], "sum_x")
        return mine, swap(away[0], "z", 1)

    def sum_low(index, mine, arrived):
        if index in LOW_FIRST:
            others = state[2][1]
            merged = float_shape(sizes[0] + 2 * sizes[2])
            shapes = [float_shape(sizes[0])] + [merged] * (x_count - 1)
            mine, *away = step_call(
                low_first_kernel, shapes, mine, arrived, *others, name="sum_z"
            )
            state[2] = state[2][0], over_x(away)
            return (mine,)
        return over_high(plain_sum(mine, arrived, "sum_z"))

    def to_owners(value):
        both = [(i, i ^ (y_count + 1)) for i in range(block_count)]
        over_both = lax.ppermute(value, ("z", "y"), both)
        return [value, swap(value, "z", 1), swap(value, "y", 1), over_both]

    table = tile_table[0]
    row_block = table[:, 0]
    col_block = table[:, 1]
    first = jnp.maximum(row_block, 0)
    second = jnp.maximum(col_block, 0)
    pair = first * block_count - (first * (first - 1)) // 2 + second - first
    of_list, slot = pair // quarter, pair % quarter
    off = ((of_list // 2) ^ y) * 2 + ((of_list % 2) ^ low_bit)
    in_batch, row, lane, exponent_row, steps_row = (jnp.zeros_like(slot) for _ in range(5))
    for index, batch in enumerate(BATCHES):
        start, end = int(starts[batch[0]]), int(starts[batch[-1] + 1])
        inside = (slot >= start) & (slot < end)
        header_rows = -(-(end - start) * rows_dev // block_size)
        at = (slot - start) * rows_dev
        top = off * SCALE_ROWS + at // block_size
        in_batch = jnp.where(inside, index, in_batch)
        row = jnp.where(inside, SCALE_ROWS + at, row)
        lane = jnp.where(inside, at % block_size, lane)
        exponent_row = jnp.where(inside, top, exponent_row)
        steps_row = jnp.where(inside, top + header_rows, steps_row)
    in_batch = jnp.where(row_block >= 0, in_batch, -1)
    places = jnp.concatenate([in_batch, off, row, lane, exponent_row, steps_row])

    parts, result = [], []
    state = {}
    for stage, which in ORDER:
        if stage == "core":
            sum_core(which)
        elif stage == "x":
            state[which] = sum_x(which, *state[which])
        elif stage == "low":
            state[which] = sum_low(which, *state[which])
        elif stage == "high":
            state[which] = [plain_sum(*state[which], "sum_high")]
        elif stage == "place":
            four = parts[4 * which : 4 * which + 4]
            operands = lax.optimization_barrier((places, *four, *result, *last))[:-1]
            vmem = pl.BlockSpec(memory_space=pltpu.VMEM)
            result = [
                pl.pallas_call(
                    functools.partial(
                        place_kernel, scale_factor / (CODE_TOP * SCALE_STEPS), which
                    ),
                    out_shape=float_shape(table.shape[0]),
                    in_specs=[pl.BlockSpec(memory_space=pltpu.SMEM)]
                    + [vmem] * (len(operands) - 1),
                    out_specs=vmem,
                    scratch_shapes=[
                        pltpu.VMEM((4 * SCALE_ROWS, block_size), jnp.float32),
                        pltpu.VMEM((4, *four[0].shape), jnp.int16),
                    ],
                    compiler_params=pltpu.CompilerParams(vmem_limit_bytes=VMEM_LIMIT),
                    cost_estimate=pl.CostEstimate(
                        flops=table.shape[0] * rows_dev * block_size,
                        bytes_accessed=0,
                        transcendentals=0,
                    ),
                    name="place_tiles",
                )(*operands)
            ]
        else:
            counts = [sizes[index] for index in which]
            shape = (SCALE_ROWS + sum(counts) * rows_dev, block_size)
            kernel = functools.partial(code_kernel, counts, [len(state[i]) for i in which])
            operands = [value for index in which for value in state[index]]
            (code,) = step_call(
                kernel, [jax.ShapeDtypeStruct(shape, jnp.int16)], *operands, name="finish"
            )
            parts += to_owners(code)

    return result[0][None]


def solution(mesh):
    tm, space = mesh.shape["tm"], mesh.shape["space"]
    sizes = (tm // 2, 2, space // 2, 2)
    grid = Mesh(mesh.devices.reshape(sizes), ("z", "y", "x", "core"))
    in_specs = (P(None, ("z", "y"), ("x", "core")), P(("z", "y"), None, None))
    out_specs = P(("z", "y"), None, ("x", "core"), None)
    return jax.shard_map(
        functools.partial(per_device, *sizes),
        mesh=grid,
        in_specs=in_specs,
        out_specs=out_specs,
        check_vma=False,
    )
```

```python
import functools
import math

import jax
import jax.numpy as jnp
import numpy as np
from jax import lax
from jax.experimental import pallas as pl
from jax.experimental.pallas import tpu as pltpu
from jax.sharding import Mesh, PartitionSpec as P

UNROLL = 4
UNROLL_SLOTS = 10
VMEM_LIMIT = 24 * 2**20
GROUPS = 3
BATCHES = ((0, 1), (2,))
CALLS = ((0, 1), (2,))
LOW_FIRST = (0,)
ORDER = (
    ("core", 0), ("x", 1), ("low", 0), ("low", 1), ("core", 1), ("x", 0),
    ("x", 2), ("high", 1), ("low", 2), ("finish", BATCHES[0]), ("finish", BATCHES[1]),
    ("place", 0), ("place", 1),
)
CODE_TOP = 32767.0
SCALE_ROWS = 16
SCALE_STEPS = 8192.0


def tile_lists(block_count):
    rows, cols = np.triu_indices(block_count)
    return np.stack([rows, cols], axis=1).reshape(2, 2, -1, 2)


def group_sizes(quarter):
    return [len(piece) for piece in np.array_split(np.arange(quarter), GROUPS)]


def multiply_tiles(scalars, first_pair, blocks, keep_ref, send_ref, offset, size, low_first):
    x, core = scalars[2], scalars[3]
    rows_dev = keep_ref.shape[2]
    part_count = blocks.shape[1] // rows_dev

    def one_slot(slot, carry):
        for low in range(2):
            where = first_pair + 2 * (low * size + slot)
            tile = lax.dot_general(
                blocks[scalars[where]],
                blocks[scalars[where + 1]],
                (((1,), (1,)), ((), ())),
                preferred_element_type=jnp.float32,
            )
            parts = [tile[part * rows_dev : (part + 1) * rows_dev] for part in range(part_count)]
            for step in range(part_count // 2):
                even, odd = parts[2 * step], parts[2 * step + 1]
                target = x ^ step
                place = low * (part_count // 2) + target if low_first else 2 * target + low
                keep_ref[place, offset + slot] = jnp.where(core == 0, even, odd)
                send_ref[place, offset + slot] = jnp.where(core == 0, odd, even)
        return carry

    lax.fori_loop(0, size, one_slot, 0, unroll=size <= UNROLL)


def multiply_groups(scalars, first_pair, sizes, blocks, groups, outs):
    offset = 0
    for index in groups:
        multiply_tiles(
            scalars, first_pair, blocks, *outs, offset, sizes[index], index in LOW_FIRST
        )
        first_pair += 4 * sizes[index]
        offset += sizes[index]


def first_kernel(layout, first_pair, sizes, scalars, *refs):
    pieces = refs[: len(layout)]
    blocks = refs[len(layout)]
    z, y = scalars[0], scalars[1]
    for (step, other, component), piece in zip(layout, pieces):
        block = (z ^ step) * 2 + (y ^ other)
        cells = piece.shape[2]
        for index in range(piece.shape[0]):
            start = (component + index) * cells
            blocks[block, :, start : start + cells] = piece[index]
    multiply_groups(scalars, first_pair, sizes, blocks, CALLS[0], refs[len(layout) + 1 :])


def second_kernel(first_pair, sizes, scalars, blocks, *outs):
    multiply_groups(scalars, first_pair, sizes, blocks, CALLS[1], outs)


def core_sum_kernel(cuts, keep, send, *outs):
    outs = list(outs)
    for offset, size, block in cuts:
        for start in range(0, keep.shape[0], block):
            place = (slice(start, start + block), slice(offset, offset + size))
            outs.pop(0)[...] = keep[place] + send[place]


def split_sum_kernel(left, right, *outs):
    for index, out in enumerate(outs):
        out[...] = left[index] + right[index]


def sum_kernel(left, right, out):
    out[...] = left[...] + right[...]


def code_kernel(sizes, pairs, *refs):
    code = refs[-1]
    refs = list(refs[:-1])
    rows, columns = refs[0].shape[1:]
    header_rows = -(-sum(sizes) * rows // columns)
    row_of = lax.broadcasted_iota(jnp.int32, (rows, columns), 0)
    lane_of = lax.broadcasted_iota(jnp.int32, (rows, columns), 1)
    place = lax.broadcasted_iota(jnp.int32, (SCALE_ROWS, columns), 0)
    header = jnp.zeros((SCALE_ROWS, columns), jnp.float32)
    slot = 0
    for size, pair in zip(sizes, pairs):
        terms = [refs.pop(0) for _ in range(pair)]
        for index in range(size):
            total = sum((term[index] for term in terms[1:]), terms[0][index])
            top = jnp.max(jnp.abs(total), axis=1, keepdims=True)
            filled = top > 0
            exponent = jnp.log(jnp.where(filled, top, 1.0)) * (1.0 / math.log(2.0))
            exponent = jnp.clip(jnp.floor(exponent), -120.0, 120.0)
            power = jnp.exp(exponent * math.log(2.0))
            steps = jnp.where(filled, jnp.ceil(top / power * SCALE_STEPS), 0.0)
            scale = steps * power * (1.0 / SCALE_STEPS)
            factor = jnp.where(filled, CODE_TOP / jnp.where(filled, scale, 1.0), 0.0)
            rounded = jnp.clip(jnp.round(total * factor), -CODE_TOP, CODE_TOP)
            start = SCALE_ROWS + slot * rows
            code[start : start + rows, :] = rounded.astype(jnp.int32).astype(jnp.int16)
            row, lane = divmod(slot * rows, columns)
            diagonal = lane_of == row_of + lane
            for at, value in ((row, exponent), (row + header_rows, steps)):
                across = jnp.sum(jnp.where(diagonal, value, 0.0), axis=0, keepdims=True)
                header += jnp.where(place == at, across, 0.0)
            slot += 1
    code[:SCALE_ROWS, :] = header.astype(jnp.int32).astype(jnp.int16)


def place_kernel(factor, batch, scalars, *refs):
    parts, before = refs[:4], refs[4:-3]
    out, headers, stack = refs[-3:]
    slots, rows, columns = out.shape
    for index, part in enumerate(parts):
        start = index * SCALE_ROWS
        headers[start : start + SCALE_ROWS, :] = (
            part[:SCALE_ROWS, :].astype(jnp.int32).astype(jnp.float32)
        )
        stack[index] = part[...]
    out[...] = before[0][...] if before else jnp.zeros_like(out)
    row_of = lax.broadcasted_iota(jnp.int32, (rows, columns), 0)
    lane_of = lax.broadcasted_iota(jnp.int32, (rows, columns), 1)

    def one_slot(slot, carry):
        batch_of, part, row, lane, exponent_row, steps_row = (
            scalars[kind * slots + slot] for kind in range(6)
        )

        @pl.when(batch_of == batch)
        def _():
            exponent = headers[pl.ds(exponent_row, 1), :]
            steps = headers[pl.ds(steps_row, 1), :]
            scale = steps * jnp.exp(exponent * math.log(2.0)) * factor
            column = jnp.sum(
                jnp.where(lane_of == row_of + lane, scale, 0.0), axis=1, keepdims=True
            )
            code = stack[part, pl.ds(pl.multiple_of(row, SCALE_ROWS), rows), :]
            out[slot] = code.astype(jnp.int32).astype(jnp.float32) * column

        return carry

    lax.fori_loop(0, slots, one_slot, 0, unroll=slots <= UNROLL_SLOTS)


def per_device(z_count, y_count, x_count, core_count, snapshots, tile_table):
    components, block_size, cells_dev = snapshots.shape
    block_count = z_count * y_count
    space_count = x_count * core_count
    rows_dev = block_size // space_count
    scale_factor = 1.0 / math.sqrt(components * cells_dev * space_count)
    z, y, x, core = (lax.axis_index(name) for name in ("z", "y", "x", "core"))
    low_bit = z & 1
    cells = cells_dev // z_count

    def swap(value, axis, bits):
        size = lax.axis_size(axis)
        return lax.ppermute(value, axis, [(i, i ^ bits) for i in range(size)])

    lists = tile_lists(block_count)
    quarter = lists.shape[2]
    sizes = group_sizes(quarter)
    starts = np.cumsum([0] + sizes)
    ordered = np.stack(
        [
            np.concatenate(
                [
                    lists[of_y, of_bit ^ flip, start : start + size].reshape(-1)
                    for start, size in zip(starts, sizes)
                    for flip in range(2)
                ]
            )
            for of_y in range(2)
            for of_bit in range(2)
        ]
    ).astype(np.int32)
    pairs = lax.dynamic_index_in_dim(jnp.asarray(ordered), y * 2 + low_bit, 0, keepdims=False)
    scalars = jnp.concatenate([jnp.stack([z, y, x, core]).astype(jnp.int32), pairs])

    def part(step, values):
        return lax.dynamic_slice_in_dim(values, (z ^ step) * cells, cells, 2)

    cut = {step: part(step, snapshots) for step in range(1, z_count, 2)}
    again = lax.optimization_barrier((snapshots, *cut.values()))[0]
    cut.update({step: part(step, again) for step in range(0, z_count, 2)})
    pieces = {(0, 0): cut[0]}
    for step in range(1, z_count):
        pieces[step, 0] = swap(cut[step], "z", step)
    layout = [(step, 0, component) for step, component in pieces]
    layout += [(step, 1, component) for step, component in pieces]
    chunks = list(pieces.values()) + [swap(piece, "y", 1) for piece in pieces.values()]

    def sums_shape(groups):
        count = sum(sizes[index] for index in groups)
        return jax.ShapeDtypeStruct((2 * x_count, count, rows_dev, block_size), jnp.float32)

    def call(kernel, size, out_shape, operands, name):
        vmem = pl.BlockSpec(memory_space=pltpu.VMEM)
        return pl.pallas_call(
            kernel,
            out_shape=out_shape,
            in_specs=[pl.BlockSpec(memory_space=pltpu.SMEM)] + [vmem] * len(operands),
            out_specs=[vmem] * len(out_shape),
            compiler_params=pltpu.CompilerParams(vmem_limit_bytes=VMEM_LIMIT),
            cost_estimate=pl.CostEstimate(
                flops=4 * size * block_size * block_size * components * cells,
                bytes_accessed=0,
                transcendentals=0,
            ),
            name=name,
        )(scalars, *operands)

    blocks_shape = jax.ShapeDtypeStruct(
        (block_count, block_size, components * cells), jnp.bfloat16
    )
    counts = [sum(sizes[index] for index in groups) for groups in CALLS]
    blocks, *sums = call(
        functools.partial(first_kernel, layout, 4, sizes),
        counts[0],
        [blocks_shape] + [sums_shape(CALLS[0])] * 2,
        chunks,
        "tiles_first",
    )
    sums += call(
        functools.partial(second_kernel, 4 + 4 * counts[0], sizes),
        counts[1],
        [sums_shape(CALLS[1])] * 2,
        [blocks],
        "tiles_second",
    )

    last = []

    def step_call(kernel, out_shape, *operands, name):
        operands = lax.optimization_barrier((*operands, *last))[: len(operands)]
        vmem = pl.BlockSpec(memory_space=pltpu.VMEM)
        outs = pl.pallas_call(
            kernel,
            out_shape=out_shape,
            in_specs=[vmem] * len(operands),
            out_specs=[vmem] * len(out_shape),
            compiler_params=pltpu.CompilerParams(vmem_limit_bytes=VMEM_LIMIT),
            cost_estimate=pl.CostEstimate(
                flops=operands[0].size, bytes_accessed=0, transcendentals=0
            ),
            name=name,
        )(*operands)
        last[:] = outs[:1]
        return outs

    def float_shape(*shape):
        return jax.ShapeDtypeStruct((*shape, rows_dev, block_size), jnp.float32)

    def split_sum(shape, left, right, name):
        shapes = [float_shape(*shape[1:])] * shape[0]
        mine, *away = step_call(split_sum_kernel, shapes, left, right, name=name)
        return mine, away

    def plain_sum(left, right, name):
        shape = jax.ShapeDtypeStruct(left.shape, left.dtype)
        return step_call(sum_kernel, [shape], left, right, name=name)[0]

    def over_x(away):
        return [swap(value, "x", step + 1) for step, value in enumerate(away)]

    def over_high(mine):
        bits = 2
        while 2 * bits < z_count:
            mine = plain_sum(mine, swap(mine, "z", bits), "sum_z")
            bits *= 2
        return mine, swap(mine, "z", bits)

    def sum_core(which):
        keep, send = sums[2 * which : 2 * which + 2]
        send = swap(send, "core", 1)
        cuts, shapes, offset = [], [], 0
        for index in CALLS[which]:
            block = x_count if index in LOW_FIRST else 2
            cuts.append((offset, sizes[index], block))
            shapes += [float_shape(block, sizes[index])] * (2 * x_count // block)
            offset += sizes[index]
        outs = list(
            step_call(
                functools.partial(core_sum_kernel, cuts), shapes, keep, send, name="sum_core"
            )
        )
        for index, (_, _, block) in zip(CALLS[which], cuts):
            count = 2 * x_count // block
            (mine, *away), outs = outs[:count], outs[count:]
            if index in LOW_FIRST:
                state[index] = mine, swap(away[0], "z", 1)
                continue
            if which > 0:
                away = lax.optimization_barrier((*away, *state[0][1]))[: len(away)]
            state[index] = mine, over_x(away)

    def sum_x(index, mine, arrived):
        for value in arrived[:-1]:
            mine = plain_sum(mine, value, "sum_x")
        if index in LOW_FIRST:
            return over_high(plain_sum(mine, arrived[-1], "sum_x"))
        mine, away = split_sum((2, sizes[index]), mine, arrived[-1], "sum_x")
        return mine, swap(away[0], "z", 1)

    def sum_low(index, mine, arrived):
        if index in LOW_FIRST:
            mine, away = split_sum((x_count, sizes[index]), mine, arrived, "sum_z")
            return mine, over_x(away)
        return over_high(plain_sum(mine, arrived, "sum_z"))

    def to_owners(value):
        both = [(i, i ^ (y_count + 1)) for i in range(block_count)]
        over_both = lax.ppermute(value, ("z", "y"), both)
        return [value, swap(value, "z", 1), swap(value, "y", 1), over_both]

    table = tile_table[0]
    row_block = table[:, 0]
    col_block = table[:, 1]
    first = jnp.maximum(row_block, 0)
    second = jnp.maximum(col_block, 0)
    pair = first * block_count - (first * (first - 1)) // 2 + second - first
    of_list, slot = pair // quarter, pair % quarter
    off = ((of_list // 2) ^ y) * 2 + ((of_list % 2) ^ low_bit)
    in_batch, row, lane, exponent_row, steps_row = (jnp.zeros_like(slot) for _ in range(5))
    for index, batch in enumerate(BATCHES):
        start, end = int(starts[batch[0]]), int(starts[batch[-1] + 1])
        inside = (slot >= start) & (slot < end)
        header_rows = -(-(end - start) * rows_dev // block_size)
        at = (slot - start) * rows_dev
        top = off * SCALE_ROWS + at // block_size
        in_batch = jnp.where(inside, index, in_batch)
        row = jnp.where(inside, SCALE_ROWS + at, row)
        lane = jnp.where(inside, at % block_size, lane)
        exponent_row = jnp.where(inside, top, exponent_row)
        steps_row = jnp.where(inside, top + header_rows, steps_row)
    in_batch = jnp.where(row_block >= 0, in_batch, -1)
    places = jnp.concatenate([in_batch, off, row, lane, exponent_row, steps_row])

    parts, result = [], []
    state = {}
    for stage, which in ORDER:
        if stage == "core":
            sum_core(which)
        elif stage == "x":
            state[which] = sum_x(which, *state[which])
        elif stage == "low":
            state[which] = sum_low(which, *state[which])
        elif stage == "high":
            state[which] = [plain_sum(*state[which], "sum_high")]
        elif stage == "place":
            four = parts[4 * which : 4 * which + 4]
            operands = lax.optimization_barrier((places, *four, *result, *last))[:-1]
            vmem = pl.BlockSpec(memory_space=pltpu.VMEM)
            result = [
                pl.pallas_call(
                    functools.partial(
                        place_kernel, scale_factor / (CODE_TOP * SCALE_STEPS), which
                    ),
                    out_shape=float_shape(table.shape[0]),
                    in_specs=[pl.BlockSpec(memory_space=pltpu.SMEM)]
                    + [vmem] * (len(operands) - 1),
                    out_specs=vmem,
                    scratch_shapes=[
                        pltpu.VMEM((4 * SCALE_ROWS, block_size), jnp.float32),
                        pltpu.VMEM((4, *four[0].shape), jnp.int16),
                    ],
                    compiler_params=pltpu.CompilerParams(vmem_limit_bytes=VMEM_LIMIT),
                    cost_estimate=pl.CostEstimate(
                        flops=table.shape[0] * rows_dev * block_size,
                        bytes_accessed=0,
                        transcendentals=0,
                    ),
                    name="place_tiles",
                )(*operands)
            ]
        else:
            counts = [sizes[index] for index in which]
            shape = (SCALE_ROWS + sum(counts) * rows_dev, block_size)
            kernel = functools.partial(code_kernel, counts, [len(state[i]) for i in which])
            operands = [value for index in which for value in state[index]]
            (code,) = step_call(
                kernel, [jax.ShapeDtypeStruct(shape, jnp.int16)], *operands, name="finish"
            )
            parts += to_owners(code)

    return result[0][None]


def solution(mesh):
    tm, space = mesh.shape["tm"], mesh.shape["space"]
    sizes = (tm // 2, 2, space // 2, 2)
    grid = Mesh(mesh.devices.reshape(sizes), ("z", "y", "x", "core"))
    in_specs = (P(None, ("z", "y"), ("x", "core")), P(("z", "y"), None, None))
    out_specs = P(("z", "y"), None, ("x", "core"), None)
    return jax.shard_map(
        functools.partial(per_device, *sizes),
        mesh=grid,
        in_specs=in_specs,
        out_specs=out_specs,
        check_vma=False,
    )
```
